32 devices in a mesh: dp: 4 (over x, core), seq: 8 (over z, y).
Axes of the slice: x: 2, y: 2, z: 4, core: 2. Of those that a mesh axis runs over, the one named last changes fastest.
Arguments:
- inputs: bfloat16 [4, 1024, 768], P('dp', 'seq'), may hold values from -6 to 6
- segments: int32 [4, 1024], P('dp'), may hold values from 0 to 5, as said below
- rand_blocks: int32 [4, 16, 3], P('dp'), may hold values from 0 to 15, as said below
- glob_blocks: int32 [4, 6, 2], P('dp'), may hold values from 0 to 15, as said below
- w_qkv: bfloat16 [768, 2304], P(('dp', 'seq')), may hold values from -0.21875 to 0.21875
- w_out: bfloat16 [768, 768], P(('dp', 'seq')), may hold values from -2.5 to 2.5
- w_in: bfloat16 [768, 3072], P(('dp', 'seq')), may hold values from -0.21875 to 0.21875
- w_down: bfloat16 [3072, 768], P(('dp', 'seq')), may hold values from -0.109375 to 0.109375
- vec_bias: bfloat16 [4, 768], P(None, ('dp', 'seq')), may hold values from -3 to 3
- ffn_bias: bfloat16 [3072], P(('dp', 'seq')), may hold values from -3 to 3
- norm_gain: bfloat16 [2, 768], P(None, ('dp', 'seq')), may hold values from 0.5 to 1.5
- norm_shift: bfloat16 [2, 768], P(None, ('dp', 'seq')), may hold values from -3 to 3
- cotangent: bfloat16 [4, 1024, 768], P('dp', 'seq'), may hold values from -6 to 6
Outputs:
- output: bfloat16 [4, 1024, 768], P('dp', 'seq')
- input_grad: float32 [4, 1024, 768], P('dp', 'seq')
- grad_qkv: float32 [768, 2304], P(('dp', 'seq'))
- grad_out: float32 [768, 768], P(('dp', 'seq'))
- grad_in: float32 [768, 3072], P(('dp', 'seq'))
- grad_down: float32 [3072, 768], P(('dp', 'seq'))
- grad_vec_bias: float32 [4, 768], P(None, ('dp', 'seq'))
- grad_ffn_bias: float32 [3072], P(('dp', 'seq'))
- grad_norm_gain: float32 [2, 768], P(None, ('dp', 'seq'))
- grad_norm_shift: float32 [2, 768], P(None, ('dp', 'seq'))
The draws below stay inside these ranges and needn't reach their ends.
Inputs may be any that keep to these rules, and one draw needn't show every extreme that they name: segments never fall along a sequence; every document but the last of a sequence has 200 to 2000 tokens. rand_blocks[s, b, :] are blocks that hold tokens of the document of block b's first token. glob_blocks[s, d, :] are blocks that hold tokens of document d, where document d occurs in sequence s.
All inputs are finite; a program needn't handle non-finite values.
Results may differ from the reference program's by a relative error of at most 0.014.
Values may be sent and summed in bfloat16 or wider, within the bound.
No kernel may reach another device: no remote copies, remote signals or barrier semaphores. Data moves between devices by JAX's collectives and lax.ppermute only.
A program may use at most 192 MiB of HBM per device.

```python
import jax
import jax.numpy as jnp
from jax import lax

D = 768
HD = 64
FF = 3072
BLK = 64
NRAND = 3
NGLOB = 2
DMIN = 200
DMAX = 2000
LENGTH = 1024
NBLK = 16
NDOC = 6
SEQ_ALL = 4


def document_bounds(key):
    doc_lengths = jax.random.randint(key, (SEQ_ALL, NDOC), DMIN, DMAX + 1)
    short_seq = jax.random.randint(jax.random.fold_in(key, 3), (), 0, SEQ_ALL)
    short_rows = (jnp.arange(SEQ_ALL, dtype=jnp.int32) == short_seq)[:, None]
    doc_lengths = jnp.where(short_rows, DMIN, doc_lengths)
    doc_ends = jnp.cumsum(doc_lengths, axis=1)
    doc_starts = doc_ends - doc_lengths
    first_block = jnp.minimum(doc_starts // BLK, NBLK - 1)
    last_block = jnp.clip((jnp.minimum(doc_ends, LENGTH) - 1) // BLK, first_block, NBLK - 1)
    return (doc_ends, first_block, last_block)


def token_segments(doc_ends):
    position = jnp.arange(LENGTH, dtype=jnp.int32)
    return jnp.sum((doc_ends[:, None, :] <= position[None, :, None]).astype(jnp.int32), axis=2)


def draw_segments(key, part):
    doc_ends, first_block, last_block = document_bounds(key)
    return token_segments(doc_ends)


def draw_glob_blocks(key, part):
    doc_ends, first_block, last_block = document_bounds(key)
    key = jax.random.fold_in(key, 7)
    return jax.random.randint(key, (SEQ_ALL, NDOC, NGLOB), first_block[:, :, None], last_block[:, :, None] + 1)


def draw_rand_blocks(key, part):
    doc_ends, first_block, last_block = document_bounds(key)
    head_seg = token_segments(doc_ends)[:, ::BLK]
    lowest = jnp.take_along_axis(first_block, head_seg, axis=1)
    highest = jnp.take_along_axis(last_block, head_seg, axis=1)
    key = jax.random.fold_in(key, 9)
    return jax.random.randint(key, (SEQ_ALL, NBLK, NRAND), lowest[:, :, None], highest[:, :, None] + 1)


def block_levels(rng, extent, cuts, smallest, top_value):
    loudness, own = 1.0, jax.random.fold_in(rng, 6)
    for dim, blocks in cuts:
        draws = jnp.exp(jax.random.uniform(jax.random.fold_in(own, dim), (blocks,), jnp.float32, smallest / len(cuts), top_value / len(cuts)))
        loudness = loudness * jnp.repeat(draws, extent[dim] // blocks).reshape([-1 if axis == dim else 1 for axis in range(len(extent))])
    return loudness


def scatter_about(rng, dims, scale, limit, shards=(), held_as=jnp.bfloat16):
    loudness = block_levels(rng, dims, shards, -0.22, 0.18) if shards else 1.0
    array = jax.random.normal(rng, dims, jnp.float32) * scale * loudness
    return jnp.minimum(jnp.maximum(array, -limit), limit).astype(held_as)


def setup_inputs(seed: int = 0) -> dict:
    keys = jax.random.split(jax.random.key(seed), 14)
    return {
        "inputs": scatter_about(keys[0], (SEQ_ALL, LENGTH, D), 1.0, 6.0, ((0, 4), (1, 8))),
        "segments": draw_segments(jax.random.fold_in(keys[13], 71), 0),
        "rand_blocks": draw_rand_blocks(jax.random.fold_in(keys[13], 71), 0),
        "glob_blocks": draw_glob_blocks(jax.random.fold_in(keys[13], 71), 0),
        "w_qkv": scatter_about(keys[4], (D, 3 * D), D ** -0.5, 0.21875, ((0, 32),)),
        "w_out": scatter_about(keys[5], (D, D), (D // 128) ** -0.5, 2.5, ((0, 32),)),
        "w_in": scatter_about(keys[6], (D, FF), D ** -0.5, 0.21875, ((0, 32),)),
        "w_down": scatter_about(keys[7], (FF, D), FF ** -0.5, 0.109375, ((0, 32),)),
        "vec_bias": scatter_about(keys[8], (4, D), 0.5, 3.0, ((1, 32),)),
        "ffn_bias": scatter_about(keys[9], (FF,), 0.5, 3.0, ((0, 32),)),
        "norm_gain": jnp.clip(1.0 + 0.1 * jax.random.normal(keys[10], (2, D), jnp.float32), 0.5, 1.5).astype(jnp.bfloat16),
        "norm_shift": scatter_about(keys[11], (2, D), 0.5, 3.0, ((1, 32),)),
        "cotangent": scatter_about(keys[12], (SEQ_ALL, LENGTH, D), 1.0, 6.0, ((0, 4), (1, 8))),
    }


top_precision = lax.Precision.HIGHEST
norm_eps = 1e-05
masked_score = -1e+30

@jax.custom_vjp
def low(v):
    return lax.optimization_barrier(v.astype(jnp.bfloat16)).astype(jnp.float32)

@jax.custom_vjp
def low_back(v):
    return v

def low_keep(v):
    return (low(v), None)

def low_pass(kept, grad):
    return (grad,)

def back_keep(v):
    return (v, None)

def back_low(kept, grad):
    return (low(grad),)
low.defvjp(low_keep, low_pass)
low_back.defvjp(back_keep, back_low)

def rounded_both(field_in):
    return low_back(low(field_in))

def key_lists(query_block, rand_rows, glob_first, glob_last, block_count):
    window = query_block[..., None] + jnp.arange(-1, 2, dtype=jnp.int32)
    listed = jnp.concatenate([window, rand_rows, glob_first, glob_last], axis=-1)
    inside = (listed >= 0) & (listed < block_count)
    entry_order = jnp.arange(listed.shape[-1])
    earlier = entry_order[None, :] < entry_order[:, None]
    same_block = listed[..., :, None] == listed[..., None, :]
    repeated = jnp.any(same_block & earlier & inside[..., None, :], axis=-1)
    return (jnp.clip(listed, 0, block_count - 1), inside & jnp.logical_not(repeated))

def allowed_mask(seg_query, seg_key, glob_query, listed, valid):
    same_seg = seg_query[:, :, None, None] == seg_key[:, None, :, :]
    member = jnp.any(glob_query[:, :, None, :] == listed[:, None, :, None], axis=-1)
    fixed_part = jnp.arange(listed.shape[1]) < 3 + NRAND
    reach_mask = valid[:, None, :] & (fixed_part[None, None, :] | member)
    return same_seg & reach_mask[..., None]

def layer_norm(field_in, gain_row, shift_row):
    mean_row = lax.optimization_barrier(jnp.mean(field_in, axis=-1, keepdims=True))
    centred = field_in - mean_row
    inverse = lax.rsqrt(lax.optimization_barrier(jnp.mean(centred * centred, axis=-1, keepdims=True)) + norm_eps)
    return centred * inverse * gain_row + shift_row

def attend_sequence(query_low, key_low, value_low, seg_row, rand_rows, glob_table):
    block_count = LENGTH // BLK
    head_count = D // HD
    block_where = jnp.arange(block_count, dtype=jnp.int32)
    glob_first = glob_table[seg_row[::BLK]]
    glob_last = glob_table[seg_row[BLK - 1::BLK]]
    listed, valid = key_lists(block_where, rand_rows, glob_first, glob_last, block_count)
    entry_count = listed.shape[-1]
    key_blocks = key_low.reshape(block_count, BLK, head_count, HD)
    value_blocks = value_low.reshape(block_count, BLK, head_count, HD)
    seg_blocks = seg_row.reshape(block_count, BLK)
    glob_tokens = glob_table[seg_row].reshape(block_count, BLK, NGLOB)
    group_count = block_count // 8

    def one_group(packed):
        query_part, listed_part, valid_part, seg_part, glob_part = packed
        key_part = key_blocks[listed_part]
        value_part = value_blocks[listed_part]
        allowed = allowed_mask(seg_part, seg_blocks[listed_part], glob_part, listed_part, valid_part)
        scores = low_back(jnp.einsum('gihd,gejhd->ghiej', query_part, key_part, precision=top_precision) * HD ** (-0.5))
        scores = jnp.where(allowed[:, None], scores, masked_score).reshape(8, head_count, BLK, entry_count * BLK)
        row_top = lax.optimization_barrier(jnp.max(scores, axis=-1, keepdims=True))
        exp_terms = jnp.exp(scores - row_top)
        attn_probs = low(exp_terms / lax.optimization_barrier(jnp.sum(exp_terms, axis=-1, keepdims=True))).reshape(8, head_count, BLK, entry_count, BLK)
        return jnp.einsum('ghiej,gejhd->gihd', attn_probs, value_part, precision=top_precision)
    packed = (query_low.reshape(group_count, 8, BLK, head_count, HD), listed.reshape(group_count, 8, entry_count), valid.reshape(group_count, 8, entry_count), seg_blocks.reshape(group_count, 8, BLK), glob_tokens.reshape(group_count, 8, BLK, NGLOB))
    result = lax.map(jax.checkpoint(one_group), packed)
    return result.reshape(LENGTH, D)

def forward(inputs, w_qkv, w_out, w_in, w_down, vec_bias, ffn_bias, norm_gain, norm_shift, seg_row, rand_rows, glob_table):
    qkv_mixed = jnp.dot(inputs, w_qkv, precision=top_precision, preferred_element_type=jnp.float32)
    query_low = rounded_both(qkv_mixed[:, :D] + vec_bias[0])
    key_low = rounded_both(qkv_mixed[:, D:2 * D])
    value_low = rounded_both(qkv_mixed[:, 2 * D:] + vec_bias[1])
    attended = rounded_both(attend_sequence(query_low, key_low, value_low, seg_row, rand_rows, glob_table))
    branch = low_back(jnp.dot(attended, w_out, precision=top_precision, preferred_element_type=jnp.float32) + vec_bias[2])
    first = layer_norm(inputs + branch, norm_gain[0], norm_shift[0])
    hidden = low_back(jnp.dot(low(first), w_in, precision=top_precision, preferred_element_type=jnp.float32) + ffn_bias)
    active = low(jax.nn.gelu(hidden, approximate=False))
    second = low_back(jnp.dot(active, w_down, precision=top_precision, preferred_element_type=jnp.float32) + vec_bias[3])
    return layer_norm(first + second, norm_gain[1], norm_shift[1])

def reference(inputs, segments, rand_blocks, glob_blocks, w_qkv, w_out, w_in, w_down, vec_bias, ffn_bias, norm_gain, norm_shift, cotangent):
    weights = tuple((item.astype(jnp.float32) for item in (w_qkv, w_out, w_in, w_down, vec_bias, ffn_bias, norm_gain, norm_shift)))

    def per_sequence(totals, packed):
        seq_in, seq_cot, seg_row, rand_rows, glob_table = packed

        def run(field_in, *params):
            return forward(field_in, *params, seg_row, rand_rows, glob_table)
        result, pullback = jax.vjp(run, seq_in.astype(jnp.float32), *weights)
        grads = pullback(seq_cot.astype(jnp.float32))
        totals = tuple((left + right for left, right in zip(totals, grads[1:])))
        return (totals, (result.astype(jnp.bfloat16), grads[0]))
    zeros = tuple((jnp.zeros_like(item) for item in weights))
    totals, (outputs, input_grads) = lax.scan(per_sequence, zeros, (inputs, cotangent, segments, rand_blocks, glob_blocks))
    return (outputs, input_grads, totals[0], totals[1], totals[2], totals[3], totals[4], totals[5], totals[6], totals[7])
```

```python
import functools

import jax
import jax.numpy as jnp
import numpy as np
from jax import lax
from jax.experimental import pallas as pl
from jax.experimental.pallas import tpu as pltpu
from jax.sharding import PartitionSpec as P

HD = 64
BLK = 64
HEAD_GROUPS = 4
TILE = 128

norm_eps = 1e-05
masked_score = -1e30
BOTH = ("dp", "seq")
bf16 = jnp.bfloat16
f32 = jnp.float32


def normalize(field_in):
    mean_row = jnp.mean(field_in, axis=-1, keepdims=True)
    centred = field_in - mean_row
    inverse = lax.rsqrt(jnp.mean(centred * centred, axis=-1, keepdims=True) + norm_eps)
    return (centred * inverse, inverse)


def norm_back(grad_in, normed, inverse, gain_row):
    weighted = grad_in * gain_row
    inner = jnp.mean(weighted * normed, axis=-1, keepdims=True)
    return inverse * (weighted - jnp.mean(weighted, axis=-1, keepdims=True) - normed * inner)


def gelu_slope(field_in):
    return (
        0.5 * (1.0 + lax.erf(field_in * 0.7071067811865476))
        + field_in * jnp.exp(-0.5 * field_in * field_in) * 0.3989422804014327
    )


def dot(left, right, left_dim=1, right_dim=0):
    return lax.dot_general(
        left, right, (((left_dim,), (right_dim,)), ((), ())), preferred_element_type=f32
    )


def head_mask(shape, head):
    lane = lax.broadcasted_iota(jnp.int32, shape, 1)
    return (lane >= head * HD) & (lane < (head + 1) * HD)


def forward_kernel(q_ref, k_ref, v_ref, b_ref, o_ref, l_ref):
    query, keys, values, bias = q_ref[...], k_ref[...], v_ref[...], b_ref[...]
    width = query.shape[1]
    out = jnp.zeros(query.shape, f32)
    logs = jnp.zeros(l_ref.shape, f32)
    for head in range(width // HD):
        mine = head_mask(query.shape, head)
        scores = dot(jnp.where(mine, query, jnp.zeros_like(query)), keys, 1, 1) + bias
        top = jnp.max(scores, axis=1, keepdims=True)
        terms = jnp.exp(scores - top)
        total = jnp.sum(terms, axis=1, keepdims=True)
        probs = (terms * (1.0 / total)).astype(bf16)
        out = out + jnp.where(mine, dot(probs, values), 0.0)
        lane = lax.broadcasted_iota(jnp.int32, l_ref.shape, 1)
        logs = jnp.where(lane == head, top + jnp.log(total), logs)
    o_ref[...] = out.astype(bf16)
    l_ref[...] = logs


def backward_kernel(q_ref, k_ref, v_ref, b_ref, d_ref, l_ref, dq_ref, dk_ref, dv_ref):
    @pl.when(pl.program_id(0) == 0)
    def _():
        dk_ref[...] = jnp.zeros(dk_ref.shape, f32)
        dv_ref[...] = jnp.zeros(dv_ref.shape, f32)

    query, keys, values, bias = q_ref[...], k_ref[...], v_ref[...], b_ref[...]
    d_att, logs = d_ref[...], l_ref[...]
    width = query.shape[1]
    d_query = jnp.zeros(query.shape, f32)
    for head in range(width // HD):
        mine = head_mask(query.shape, head)
        q_head = jnp.where(mine, query, jnp.zeros_like(query))
        d_head = jnp.where(mine, d_att, jnp.zeros_like(d_att))
        scores = dot(q_head, keys, 1, 1) + bias
        weights = jnp.exp(scores - logs[:, head : head + 1])
        d_probs = dot(d_head, values, 1, 1)
        delta = jnp.sum(weights * d_probs, axis=1, keepdims=True)
        d_scores = (weights * (d_probs - delta)).astype(bf16)
        d_query = d_query + jnp.where(mine, dot(d_scores, keys), 0.0)
        dk_ref[...] += dot(d_scores, q_head, 0, 0)
        dv_ref[...] += dot(weights.astype(bf16), d_head, 0, 0)
    dq_ref[...] = (d_query * HD ** (-0.5)).astype(bf16)


def attention_forward(query, keys, values, bias):
    rows, width = query.shape
    key_rows = keys.shape[0]
    tile = pl.BlockSpec((TILE, width), lambda i: (i, 0))
    whole = pl.BlockSpec((key_rows, width), lambda i: (0, 0))
    return pl.pallas_call(
        forward_kernel,
        grid=(rows // TILE,),
        in_specs=[tile, whole, whole, pl.BlockSpec((TILE, key_rows), lambda i: (i, 0))],
        out_specs=[tile, pl.BlockSpec((TILE, 128), lambda i: (i, 0))],
        out_shape=[
            jax.ShapeDtypeStruct((rows, width), bf16),
            jax.ShapeDtypeStruct((rows, 128), f32),
        ],
        compiler_params=pltpu.CompilerParams(vmem_limit_bytes=48 * 1024 * 1024),
        name="attention_forward",
    )(query, keys, values, bias)


def attention_backward(query, keys, values, bias, d_att, logs):
    rows, width = query.shape
    key_rows = keys.shape[0]
    tile = pl.BlockSpec((TILE, width), lambda i: (i, 0))
    whole = pl.BlockSpec((key_rows, width), lambda i: (0, 0))
    return pl.pallas_call(
        backward_kernel,
        grid=(rows // TILE,),
        in_specs=[
            tile,
            whole,
            whole,
            pl.BlockSpec((TILE, key_rows), lambda i: (i, 0)),
            tile,
            pl.BlockSpec((TILE, 128), lambda i: (i, 0)),
        ],
        out_specs=[tile, whole, whole],
        out_shape=[
            jax.ShapeDtypeStruct((rows, width), bf16),
            jax.ShapeDtypeStruct((key_rows, width), f32),
            jax.ShapeDtypeStruct((key_rows, width), f32),
        ],
        compiler_params=pltpu.CompilerParams(vmem_limit_bytes=48 * 1024 * 1024),
        name="attention_backward",
    )(query, keys, values, bias, d_att, logs)


class Grid:
    def __init__(self, mesh):
        self.dp, self.seq = mesh.shape["dp"], mesh.shape["seq"]
        self.count = self.dp * self.seq
        self.xs, self.parts = self.dp // 2, self.seq // HEAD_GROUPS
        bits = lambda axis, size: [(axis, b) for b in range(size.bit_length() - 1)]
        group_bits = [("g", 1), ("g", 0)]
        x_bits, part_bits = bits("x", self.xs), bits("q", self.parts)
        self.group_bits, self.x_bits, self.part_bits = group_bits, x_bits, part_bits
        alternate = len(x_bits) == len(part_bits)
        first = group_bits + x_bits + part_bits
        second = group_bits + part_bits + x_bits
        self.orders = (first, second if alternate else first)

    def place(self, device):
        dp, seq = divmod(device, self.seq)
        return {"x": dp // 2, "c": dp % 2, "g": seq // self.parts, "q": seq % self.parts}

    def device(self, at):
        return (at["x"] * 2 + at["c"]) * self.seq + at["g"] * self.parts + at["q"]

    def flip(self, bits_of_core):
        pairs = []
        for device in range(self.count):
            at = self.place(device)
            axis, bit = bits_of_core[at["c"]]
            at[axis] ^= 1 << bit
            pairs.append((device, self.device(at)))
        return pairs

    def lines(self, axes):
        found = {}
        for device in range(self.count):
            at = self.place(device)
            key = tuple(v for k, v in at.items() if k not in axes)
            found.setdefault(key, []).append(device)
        return list(found.values())

    def piece_place(self, core, piece):
        at = {"x": 0, "c": core, "g": 0, "q": 0}
        for step, (axis, bit) in enumerate(self.orders[core]):
            at[axis] |= ((piece >> step) & 1) << bit
        return at


def bit_of(coords, bits_of_core):
    picked = [(coords[axis] >> bit) & 1 for axis, bit in bits_of_core]
    if bits_of_core[0] == bits_of_core[1]:
        return picked[0]
    return jnp.where(coords["c"] == 0, picked[0], picked[1])


def gather_steps(grid, coords, held, orders):
    for pair in zip(*orders):
        got = lax.ppermute(held, BOTH, grid.flip(pair))
        upper = bit_of(coords, pair) == 1
        held = jnp.where(
            upper, jnp.concatenate([got, held], axis=0), jnp.concatenate([held, got], axis=0)
        )
    return held


def reduce_steps(grid, coords, total, orders):
    for pair in reversed(list(zip(*orders))):
        half = total.shape[0] // 2
        bit = bit_of(coords, pair)
        keep = lax.dynamic_slice_in_dim(total, bit * half, half, 0)
        send = lax.dynamic_slice_in_dim(total, (1 - bit) * half, half, 0)
        got = lax.ppermute(send.astype(bf16), BOTH, grid.flip(pair))
        total = keep.astype(f32) + got.astype(f32)
    return total


def on_device(
    grid,
    inputs,
    segments,
    rand_blocks,
    glob_blocks,
    w_qkv,
    w_out,
    w_in,
    w_down,
    vec_bias,
    ffn_bias,
    norm_gain,
    norm_shift,
    cotangent,
):
    local_len, width = inputs.shape[1:]
    full_len = segments.shape[1]
    rows_each, ff_each = w_in.shape[0], w_down.shape[0]
    ff = w_in.shape[1]
    ff_half = ff // 2
    groups, parts, xs = HEAD_GROUPS, grid.parts, grid.xs
    chips = grid.count // 2
    head_width = width // groups
    dp_place, seq_place = lax.axis_index("dp"), lax.axis_index("seq")
    coords = {"x": dp_place // 2, "c": dp_place % 2, "g": seq_place // parts, "q": seq_place % parts}
    core = coords["c"]
    same = lambda order: (order, order)
    core_bit = [("c", 0)]
    group_lines = grid.lines("g")
    half_cut = [0, width]

    def own_part(pair):
        return lax.dynamic_index_in_dim(pair, core, 0, keepdims=False)

    small = jnp.concatenate(
        [
            vec_bias.T,
            norm_gain.T,
            norm_shift.T,
            ffn_bias.reshape(rows_each, ff_each // rows_each),
        ],
        axis=1,
    )
    small_count = small.shape[1]
    slices = w_qkv.reshape(rows_each, 3, groups, head_width).transpose(2, 0, 1, 3)
    slices = slices.reshape(groups, rows_each, 3 * head_width)
    spread = lambda a: jnp.broadcast_to(a[None], (groups,) + a.shape)
    packed = jnp.concatenate([slices, spread(w_out), spread(small)], axis=2)
    packed = lax.all_to_all(packed, BOTH, 0, 0, axis_index_groups=group_lines, tiled=True)
    order = ([*grid.x_bits, *grid.part_bits], [*grid.part_bits, *grid.x_bits])
    if len(grid.x_bits) != len(grid.part_bits):
        order = same(order[0])
    held = gather_steps(grid, coords, packed[None], order)
    held = gather_steps(grid, coords, held[None], same(core_bit))
    if len(grid.x_bits) == len(grid.part_bits):
        held = held.reshape(2, parts, xs, groups, rows_each, -1)
        first = held[0].reshape(parts, xs, groups, rows_each, -1).transpose(1, 2, 0, 3, 4)
        second = held[1].reshape(xs, parts, groups, rows_each, -1).transpose(0, 2, 1, 3, 4)
    else:
        held = held.reshape(2, parts, xs, groups, rows_each, -1)
        first, second = held[0].transpose(1, 2, 0, 3, 4), held[1].transpose(1, 2, 0, 3, 4)
    table = jnp.stack([first, second], axis=1).reshape(width, -1)
    qkv_slice = table[:, : 3 * head_width]
    out_full = table[:, 3 * head_width : 3 * head_width + width]
    params = table[:, 3 * head_width + width :].astype(f32)
    bias_rows = params[:, :4].T
    gain_rows, shift_rows = params[:, 4:6].T, params[:, 6:8].T
    ffn_full = params[:, 8:].reshape(grid.count, ff_each)

    tokens = inputs.reshape(local_len, width)
    x_line = gather_steps(grid, coords, tokens[None], same(grid.group_bits))
    x_line = x_line.reshape(2, 2, local_len, width).transpose(1, 0, 2, 3)
    x_line = x_line.reshape(groups * local_len, width)

    piece_places = [[grid.piece_place(c, p) for p in range(chips)] for c in range(2)]
    piece_ids = [[grid.device(at) for at in places] for places in piece_places]
    w_in_units = w_in.reshape(rows_each, grid.count, ff_each)
    columns = [w_in_units[:, np.array(ids)].reshape(rows_each, ff_half) for ids in piece_ids]
    columns = [jnp.stack([c[:, :width], c[:, width:]]) for c in columns]
    own_columns = jnp.where(core == 0, columns[0], columns[1])
    other_columns = jnp.where(core == 0, columns[1], columns[0])
    got_columns = lax.ppermute(other_columns, BOTH, grid.flip(same(core_bit[0])))
    pair_columns = jnp.where(
        core == 0,
        jnp.stack([own_columns, got_columns], 1),
        jnp.stack([got_columns, own_columns], 1),
    )
    in_rows = 2 * rows_each
    piece = jnp.concatenate([pair_columns.reshape(2 * in_rows, width), w_down], axis=0)
    pieces = gather_steps(grid, coords, piece[None], grid.orders)
    in_half = jnp.concatenate(
        [pieces[:, :in_rows].reshape(width, width), pieces[:, in_rows : 2 * in_rows].reshape(width, width)],
        axis=1,
    )
    down_half = pieces[:, 2 * in_rows :].reshape(ff_half, width)
    natural = np.zeros((2, width), np.int32)
    for c in range(2):
        for p, at in enumerate(piece_places[c]):
            for other in range(2):
                start = p * in_rows + other * rows_each
                source = grid.device({**at, "c": other}) * rows_each
                natural[c, start : start + rows_each] = source + np.arange(rows_each)
    natural_row = jnp.where(core == 0, jnp.asarray(natural[0]), jnp.asarray(natural[1]))
    shuffle = (jnp.arange(width, dtype=jnp.int32)[:, None] == natural_row[None, :]).astype(bf16)
    ffn_by_core = [ffn_full[np.array(ids)].reshape(ff_half) for ids in piece_ids]
    ffn_half = jnp.where(core == 0, ffn_by_core[0], ffn_by_core[1])

    own_blocks = local_len // BLK
    token_order = lambda a: a.reshape((groups, parts) + a.shape[1:])
    block_ids = (jnp.arange(full_len, dtype=jnp.int32) // BLK).reshape(groups, parts, local_len)
    seg_chunks = segments.reshape(groups, parts, local_len)
    key_block = block_ids.transpose(1, 0, 2).reshape(1, full_len)
    key_seg = seg_chunks.transpose(1, 0, 2).reshape(1, full_len)
    line = lambda a: lax.dynamic_index_in_dim(a, coords["q"], 1, keepdims=False).reshape(-1, 1)
    query_block, query_seg = line(block_ids), line(seg_chunks)
    near = (key_block >= query_block - 1) & (key_block <= query_block + 1)
    rand_rows = rand_blocks[0].reshape(groups, parts, own_blocks, -1)
    rand_rows = lax.dynamic_index_in_dim(rand_rows, coords["q"], 1, keepdims=False)
    rand_rows = jnp.repeat(rand_rows.reshape(groups * own_blocks, -1), BLK, axis=0)
    for entry in range(rand_rows.shape[1]):
        near = near | (key_block == rand_rows[:, entry : entry + 1])
    glob_table = glob_blocks[0]
    doc = jnp.arange(glob_table.shape[0], dtype=jnp.int32)[None, :]
    for entry in range(glob_table.shape[1]):
        picked = jnp.sum(
            jnp.where(query_seg == doc, glob_table[None, :, entry], 0), axis=1, keepdims=True
        )
        near = near | (key_block == picked)
    allowed = near & (query_seg == key_seg)
    mask_bias = jnp.where(allowed, 0.0, masked_score).astype(f32)

    pair_in = jnp.stack([tokens, cotangent.reshape(local_len, width)])
    got_in = lax.ppermute(pair_in, BOTH, grid.flip(same(core_bit[0])))
    chip_in = jnp.where(core == 0, jnp.concatenate([pair_in, got_in], 1), jnp.concatenate([got_in, pair_in], 1))
    x_float, out_grad = chip_in[0].astype(f32), chip_in[1].astype(f32)

    group_columns = lambda row: lax.dynamic_slice_in_dim(row, coords["g"] * head_width, head_width, 0)
    qkv = dot(x_line, qkv_slice)
    query = ((qkv[:, :head_width] + group_columns(bias_rows[0])) * HD ** (-0.5)).astype(bf16)
    key_low = qkv[:, head_width : 2 * head_width].astype(bf16)
    value_low = (qkv[:, 2 * head_width :] + group_columns(bias_rows[1])).astype(bf16)
    key_values = jnp.concatenate([key_low, value_low], axis=1)
    key_values = gather_steps(grid, coords, key_values[None], same(grid.part_bits))
    key_values = key_values.reshape(full_len, 2 * head_width)
    all_keys, all_values = key_values[:, :head_width], key_values[:, head_width:]
    attended_line, logs = attention_forward(query, all_keys, all_values, mask_bias)
    attended = lax.all_to_all(
        attended_line.reshape(groups, local_len, head_width),
        BOTH,
        0,
        0,
        axis_index_groups=group_lines,
        tiled=True,
    )
    attended = attended.transpose(1, 0, 2).reshape(local_len, width)
    attended = gather_steps(grid, coords, attended[None], same(core_bit)).reshape(2 * local_len, width)

    branch = dot(attended, out_full) + bias_rows[2]
    first_normed, first_inverse = normalize(x_float + branch)
    first = first_normed * gain_rows[0] + shift_rows[0]
    first_low = first.astype(bf16)
    first_mixed = dot(first_low, shuffle).astype(bf16)
    hidden = dot(first_mixed, in_half) + ffn_half
    active = jax.nn.gelu(hidden, approximate=False).astype(bf16)

    def both_cores(part):
        return part + lax.ppermute(part.astype(bf16), BOTH, grid.flip(same(core_bit[0]))).astype(f32)

    second = both_cores(dot(active, down_half)) + bias_rows[3]
    second_normed, second_inverse = normalize(first + second)
    own_rows = lambda a: lax.dynamic_slice_in_dim(a, core * local_len, local_len, 0)
    output = own_rows(second_normed * gain_rows[1] + shift_rows[1]).astype(bf16)

    gain_two = jnp.sum(own_rows(out_grad * second_normed), axis=0)
    shift_two = jnp.sum(own_rows(out_grad), axis=0)
    d_second = norm_back(out_grad, second_normed, second_inverse, gain_rows[1])
    d_two = d_second
    d_second = d_two.astype(bf16)
    bias_two = jnp.sum(own_rows(d_second).astype(f32), axis=0)
    grad_down = dot(active, d_second, 0, 0).astype(bf16)
    d_hidden = (dot(d_second, down_half, 1, 1) * gelu_slope(hidden)).astype(bf16)
    bias_ffn = jnp.sum(d_hidden.astype(f32), axis=0)
    d_mixed = dot(d_hidden, in_half, 1, 1).astype(bf16)
    d_first = d_two + both_cores(dot(d_mixed, shuffle, 1, 1))
    grad_in = [
        dot(first_mixed, d_hidden[:, start : start + width], 0, 0).astype(bf16) for start in half_cut
    ]
    gain_one = jnp.sum(own_rows(d_first * first_normed), axis=0)
    shift_one = jnp.sum(own_rows(d_first), axis=0)
    d_one = norm_back(d_first, first_normed, first_inverse, gain_rows[0])
    d_branch = d_one.astype(bf16)
    bias_out = jnp.sum(own_rows(d_branch).astype(f32), axis=0)
    d_attended = dot(own_rows(d_branch), out_full, 1, 1).astype(bf16)
    d_att_line = lax.all_to_all(
        d_attended.reshape(local_len, groups, head_width).transpose(1, 0, 2),
        BOTH,
        0,
        0,
        axis_index_groups=group_lines,
        tiled=True,
    ).reshape(groups * local_len, head_width)

    grad_out = dot(attended, d_branch, 0, 0).astype(bf16).reshape(grid.count, rows_each, width)
    out_by_core = [grad_out[np.array(ids)] for ids in piece_ids]
    out_pieces = jnp.where(core == 0, out_by_core[0], out_by_core[1])
    grad_pieces = jnp.concatenate(
        [
            grad_in[0].reshape(chips, in_rows, width),
            grad_in[1].reshape(chips, in_rows, width),
            grad_down.reshape(chips, ff_each, width),
            out_pieces,
        ],
        axis=1,
    )
    summed = reduce_steps(grid, coords, grad_pieces, grid.orders)[0]
    sum_down = summed[2 * in_rows : 2 * in_rows + ff_each]
    sum_out = summed[2 * in_rows + ff_each :]
    in_pairs = summed[: 2 * in_rows].reshape(2, 2, rows_each, width)
    own_in = lax.dynamic_index_in_dim(in_pairs, core, 1, keepdims=False)
    other_in = lax.dynamic_index_in_dim(in_pairs, 1 - core, 1, keepdims=False)
    got_in = lax.ppermute(other_in, BOTH, grid.flip(same(core_bit[0])))
    in_by_core = [jnp.where(core == 0, own_in, got_in), jnp.where(core == 0, got_in, own_in)]
    in_units = [
        jnp.concatenate([a[0], a[1]], axis=1).reshape(rows_each, chips, ff_each) for a in in_by_core
    ]
    back = np.zeros(grid.count, np.int32)
    for c in range(2):
        for p, device in enumerate(piece_ids[c]):
            back[device] = c * chips + p
    sum_in = jnp.concatenate(in_units, axis=1)[:, back].reshape(rows_each, ff)

    d_query, key_part, value_part = attention_backward(
        query, all_keys, all_values, mask_bias, d_att_line, logs
    )
    kv_part = jnp.concatenate([key_part, value_part], axis=1)
    kv_part = kv_part.reshape(parts, groups * local_len, 2 * head_width)
    kv_mine = reduce_steps(grid, coords, kv_part, same(grid.part_bits))[0].astype(bf16)
    d_qkv = jnp.concatenate([d_query, kv_mine], axis=1)
    grad_back = dot(d_qkv, qkv_slice, 1, 1).astype(bf16).reshape(groups, local_len, width)
    grad_back = lax.all_to_all(grad_back, BOTH, 0, 0, axis_index_groups=group_lines, tiled=True)
    input_grad = own_rows(d_one) + jnp.sum(grad_back.astype(f32), axis=0)

    grad_qkv = dot(x_line, d_qkv, 0, 0).reshape(xs, 2, groups, parts, rows_each, 3 * head_width)
    if len(grid.x_bits) == len(grid.part_bits):
        first = grad_qkv.transpose(1, 3, 0, 2, 4, 5)
        second = grad_qkv.transpose(1, 0, 3, 2, 4, 5)
        by_core = jnp.stack([first[0], second[1]])
    else:
        by_core = grad_qkv.transpose(1, 3, 0, 2, 4, 5)
    by_core = by_core.reshape(2, xs * parts, groups, rows_each, 3 * head_width)
    part = reduce_steps(grid, coords, by_core, same(core_bit))[0]
    part = reduce_steps(grid, coords, part, order)[0]
    part = lax.all_to_all(part, BOTH, 0, 0, axis_index_groups=group_lines, tiled=True)
    sum_qkv = part.reshape(groups, rows_each, 3, head_width).transpose(1, 2, 0, 3)
    sum_qkv = sum_qkv.reshape(rows_each, 3 * width)

    bias_q = jnp.sum(d_query.astype(f32), axis=0)
    bias_v = jnp.sum(kv_mine[:, head_width:].astype(f32), axis=0)
    place = lambda row: lax.dynamic_update_slice_in_dim(
        jnp.zeros((width,), f32), row, coords["g"] * head_width, 0
    )
    ffn_pieces = bias_ffn.reshape(chips, ff_each)
    ffn_spots = [jnp.zeros((grid.count, ff_each), f32).at[np.array(ids)].set(ffn_pieces) for ids in piece_ids]
    ffn_spread = jnp.where(core == 0, ffn_spots[0], ffn_spots[1])
    vectors = jnp.stack(
        [place(bias_q), place(bias_v), bias_out, bias_two, gain_one, gain_two, shift_one, shift_two]
    )
    vectors = vectors.reshape(8, grid.count, rows_each).transpose(1, 0, 2)
    vectors = jnp.concatenate([vectors.reshape(grid.count, 8 * rows_each), ffn_spread], axis=1)
    vectors = lax.all_to_all(vectors, BOTH, 0, 0, tiled=True)
    vectors = jnp.sum(vectors, axis=0)
    rows = vectors[: 8 * rows_each].reshape(8, rows_each)
    return (
        output[None],
        input_grad[None],
        sum_qkv,
        sum_out,
        sum_in,
        sum_down,
        rows[:4],
        vectors[8 * rows_each :],
        rows[4:6],
        rows[6:8],
    )


def solution(mesh):
    return jax.shard_map(
        functools.partial(on_device, Grid(mesh)),
        mesh=mesh,
        in_specs=(
            P("dp", "seq", None),
            P("dp", None),
            P("dp", None, None),
            P("dp", None, None),
            P(("dp", "seq"), None),
            P(("dp", "seq"), None),
            P(("dp", "seq"), None),
            P(("dp", "seq"), None),
            P(None, ("dp", "seq")),
            P(("dp", "seq")),
            P(None, ("dp", "seq")),
            P(None, ("dp", "seq")),
            P("dp", "seq", None),
        ),
        out_specs=(
            P("dp", "seq", None),
            P("dp", "seq", None),
            P(("dp", "seq"), None),
            P(("dp", "seq"), None),
            P(("dp", "seq"), None),
            P(("dp", "seq"), None),
            P(None, ("dp", "seq")),
            P(("dp", "seq")),
            P(None, ("dp", "seq")),
            P(None, ("dp", "seq")),
        ),
        check_vma=False,
    )
```

```python
import functools

import jax
import jax.numpy as jnp
import numpy as np
from jax import lax
from jax.experimental import pallas as pl
from jax.experimental.pallas import tpu as pltpu
from jax.sharding import PartitionSpec as P

HD = 64
BLK = 64
HEAD_GROUPS = 4
SCORE_CELLS = 512 * 1024

norm_eps = 1e-05
masked_score = -1e30
BOTH = ("dp", "seq")
bf16 = jnp.bfloat16
f32 = jnp.float32


def normalize(field_in):
    mean_row = jnp.mean(field_in, axis=-1, keepdims=True)
    centred = field_in - mean_row
    inverse = lax.rsqrt(jnp.mean(centred * centred, axis=-1, keepdims=True) + norm_eps)
    return (centred * inverse, inverse)


def norm_back(grad_in, normed, inverse, gain_row):
    weighted = grad_in * gain_row
    inner = jnp.mean(weighted * normed, axis=-1, keepdims=True)
    return inverse * (weighted - jnp.mean(weighted, axis=-1, keepdims=True) - normed * inner)


def gelu_slope(field_in):
    return (
        0.5 * (1.0 + lax.erf(field_in * 0.7071067811865476))
        + field_in * jnp.exp(-0.5 * field_in * field_in) * 0.3989422804014327
    )


def dot(left, right, left_dim=1, right_dim=0):
    return lax.dot_general(
        left, right, (((left_dim,), (right_dim,)), ((), ())), preferred_element_type=f32
    )


def call(body, outs, *args, name, scratch=(), flops=1e8, in_place=()):
    space = lambda i, a: (
        pl.ANY if i in in_place else pltpu.SMEM if a.dtype == jnp.int32 else pltpu.VMEM
    )
    specs = [pl.BlockSpec(memory_space=space(i, a)) for i, a in enumerate(args)]
    moved = sum(int(np.prod(a.shape)) * a.dtype.itemsize for a in args)
    return pl.pallas_call(
        body,
        in_specs=specs,
        out_specs=[pl.BlockSpec(memory_space=pltpu.VMEM)] * len(outs),
        out_shape=[jax.ShapeDtypeStruct(shape, dtype) for shape, dtype in outs],
        scratch_shapes=list(scratch),
        compiler_params=pltpu.CompilerParams(vmem_limit_bytes=56 * 1024 * 1024),
        cost_estimate=pl.CostEstimate(flops=int(flops), bytes_accessed=moved, transcendentals=0),
        name=name,
    )(*args)


def copies(pairs, sems):
    started = []
    for i, (source, target) in enumerate(pairs):
        copy = pltpu.make_async_copy(source, target, sems.at[i])
        copy.start()
        started.append(copy)
    return started


def exact(left, right, left_dim=1, right_dim=0):
    return lax.dot_general(
        left,
        right,
        (((left_dim,), (right_dim,)), ((), ())),
        preferred_element_type=f32,
        precision=lax.Precision.HIGHEST,
    )


def iota(shape, dim):
    return lax.broadcasted_iota(jnp.int32, shape, dim)


def spread_rows(row, rows, each):
    lanes = row.shape[1]
    picked = jnp.where(iota((rows, lanes), 1) // each == iota((rows, lanes), 0), row, 0.0)
    select = (iota((lanes, each), 0) % each == iota((lanes, each), 1)).astype(f32)
    return exact(picked, select)


def pick(options, index):
    chosen = options[0]
    for i, option in enumerate(options[1:]):
        chosen = jnp.where(index == i + 1, option, chosen)
    return chosen


def pack_kernel(unit_ids, place_ref, qkv_ref, out_ref, in_ref, vec_ref, ffn_ref, gain_ref, shift_ref, *outs):
    core, group = place_ref[0], place_ref[1]
    rows, width = out_ref.shape
    columns = width // HEAD_GROUPS
    rolled = lambda g: [
        qkv_ref[:, kind * width + g * columns : kind * width + (g + 1) * columns] for kind in (1, 2, 0)
    ]
    by_group = [jnp.concatenate(rolled(g), axis=1) for g in range(HEAD_GROUPS)]
    same_row = (iota((rows, rows), 0) == iota((rows, rows), 1)).astype(bf16)
    turned = [dot(same_row, ref[...], 1, 1) for ref in (vec_ref, gain_ref, shift_ref)]
    turned.append(spread_rows(ffn_ref[...].astype(f32), rows, ffn_ref.shape[1] // rows))
    small = jnp.concatenate(turned, axis=1).astype(bf16)
    for k in range(HEAD_GROUPS):
        chosen = pick(by_group, (group + k) % HEAD_GROUPS)
        rest = outs[k].shape[1] - 3 * columns - width - small.shape[1]
        outs[k][...] = jnp.concatenate(
            [chosen, out_ref[...], small, jnp.zeros((rows, rest), bf16)], axis=1
        )
    each = ffn_ref.shape[1]
    units = [
        jnp.concatenate([in_ref[:, i * each : (i + 1) * each] for i in ids], axis=1) for ids in unit_ids
    ]
    outs[HEAD_GROUPS][...] = jnp.where(core == 0, units[0], units[1])
    outs[HEAD_GROUPS + 1][...] = jnp.where(core == 0, units[1], units[0])


def qkv_kernel(x_ref, table_ref, sel_ref, q_ref, pair_ref):
    columns = sel_ref.shape[1]
    width = x_ref.shape[1]
    mixed = dot(x_ref[...], table_ref[:, : 3 * columns])
    small = table_ref[:, 3 * columns + width : 3 * columns + width + 4]
    biases = dot(small, sel_ref[...], 0, 0)
    keys = mixed[:, :columns]
    values = mixed[:, columns : 2 * columns] + biases[1:2]
    pair_ref[...] = jnp.concatenate([keys, values], axis=1).astype(bf16)
    q_ref[...] = ((mixed[:, 2 * columns :] + biases[0:1]) * HD ** (-0.5)).astype(bf16)


def unfold_kernel(small_each, table_ref, near_ref, line_ref, unit_ref, qkv_ref, out_ref, par_ref, ffn_ref):
    columns = qkv_ref.shape[1]
    width = out_ref.shape[1]
    qkv_ref[...] = dot(near_ref[...], table_ref[:, :columns]).astype(bf16)
    out_ref[...] = dot(line_ref[...], table_ref[:, columns : columns + width]).astype(bf16)
    small = table_ref[:, columns + width : columns + width + 8 + small_each]
    par_ref[...] = dot(small[:, :8], near_ref[...], 0, 1)
    by_slot = dot(small[:, 8:], unit_ref[...], 0, 0)
    slot = iota(by_slot.shape, 1) % small_each == iota(by_slot.shape, 0)
    ffn_ref[...] = jnp.sum(jnp.where(slot, by_slot, 0.0), axis=0, keepdims=True)


def head_mask(shape, head):
    lane = iota(shape, 1)
    return (lane >= head * HD) & (lane < (head + 1) * HD)


def split_pairs(pair_ref, k_ref, v_ref):
    width = k_ref.shape[1]
    k_ref[...] = pair_ref[:, :width]
    v_ref[...] = pair_ref[:, width:]


def forward_kernel(q_ref, kv_ref, b_ref, *refs):
    *o_refs, l_ref, k_ref, v_ref = refs
    step = pl.program_id(0)

    @pl.when(step == 0)
    def _():
        split_pairs(kv_ref, k_ref, v_ref)

    query, keys, values, bias = q_ref[...], k_ref[...], v_ref[...], b_ref[...]
    rows, width = query.shape
    out = jnp.zeros(query.shape, f32)
    logs = jnp.zeros(l_ref.shape, f32)
    for head in range(width // HD):
        mine = head_mask(query.shape, head)
        scores = dot(jnp.where(mine, query, jnp.zeros_like(query)), keys, 1, 1) + bias
        top = jnp.max(scores, axis=1, keepdims=True)
        terms = jnp.exp(scores - top)
        total = jnp.sum(terms, axis=1, keepdims=True)
        probs = (terms * (1.0 / total)).astype(bf16)
        out = out + jnp.where(mine, dot(probs, values), 0.0)
        logs = jnp.where(iota(l_ref.shape, 1) == head, top + jnp.log(total), logs)
    l_ref[...] = logs
    low = out.astype(bf16)
    piece = o_refs[0].shape[0]
    each = rows // piece
    for k, o_ref in enumerate(o_refs):
        start = (k % each) * piece

        @pl.when(step == k // each)
        def _(o_ref=o_ref, start=start):
            o_ref[...] = low[start : start + piece]


def backward_kernel(q_ref, kv_ref, b_ref, *refs):
    pieces, refs = refs[:HEAD_GROUPS], refs[HEAD_GROUPS:]
    l_ref, dq_ref, own_ref, send_ref, k_ref, v_ref, d_ref, dk_ref, dv_ref = refs
    step = pl.program_id(0)
    rows, width = q_ref.shape

    @pl.when(step == 0)
    def _():
        split_pairs(kv_ref, k_ref, v_ref)
        dk_ref[...] = jnp.zeros(dk_ref.shape, f32)
        dv_ref[...] = jnp.zeros(dv_ref.shape, f32)
        piece = pieces[0].shape[0]
        for k, ref in enumerate(pieces):
            d_ref[k * piece : (k + 1) * piece] = ref[...]

    query, keys, values, bias = q_ref[...], k_ref[...], v_ref[...], b_ref[...]
    d_att = d_ref[pl.ds(pl.multiple_of(step * rows, rows), rows)]
    logs = l_ref[...]
    d_query = jnp.zeros(query.shape, f32)
    for head in range(width // HD):
        mine = head_mask(query.shape, head)
        q_head = jnp.where(mine, query, jnp.zeros_like(query))
        d_head = jnp.where(mine, d_att, jnp.zeros_like(d_att))
        scores = dot(q_head, keys, 1, 1) + bias
        weights = jnp.exp(scores - logs[:, head : head + 1])
        d_probs = dot(d_head, values, 1, 1)
        delta = jnp.sum(weights * d_probs, axis=1, keepdims=True)
        d_scores = (weights * (d_probs - delta)).astype(bf16)
        d_query = d_query + jnp.where(mine, dot(d_scores, keys), 0.0)
        dk_ref[...] += dot(d_scores, q_head, 0, 0)
        dv_ref[...] += dot(weights.astype(bf16), d_head, 0, 0)
    dq_ref[...] = (d_query * HD ** (-0.5)).astype(bf16)

    @pl.when(step == pl.num_programs(0) - 1)
    def _():
        kept = own_ref.shape[0]
        own_ref[:, :width] = dk_ref[:kept]
        own_ref[:, width:] = dv_ref[:kept]
        send_ref[:, :width] = dk_ref[kept:].astype(bf16)
        send_ref[:, width:] = dv_ref[kept:].astype(bf16)


def attention_forward(query, pairs, bias):
    rows, width = query.shape
    key_rows = pairs.shape[0]
    tile = min(rows, SCORE_CELLS // key_rows)
    piece = rows // HEAD_GROUPS
    results = pl.pallas_call(
        forward_kernel,
        grid=(rows // tile,),
        in_specs=[
            pl.BlockSpec((tile, width), lambda i: (i, 0)),
            pl.BlockSpec((key_rows, 2 * width), lambda i: (0, 0)),
            pl.BlockSpec((tile, key_rows), lambda i: (i, 0)),
        ],
        out_specs=[pl.BlockSpec((piece, width), lambda i: (0, 0))] * HEAD_GROUPS
        + [pl.BlockSpec((tile, 128), lambda i: (i, 0))],
        out_shape=[jax.ShapeDtypeStruct((piece, width), bf16)] * HEAD_GROUPS
        + [jax.ShapeDtypeStruct((rows, 128), f32)],
        scratch_shapes=[pltpu.VMEM((key_rows, width), bf16)] * 2,
        compiler_params=pltpu.CompilerParams(vmem_limit_bytes=56 * 1024 * 1024),
        cost_estimate=pl.CostEstimate(
            flops=16 * rows * key_rows * width, bytes_accessed=4 * rows * key_rows, transcendentals=0
        ),
        name="attention_forward",
    )(query, pairs, bias)
    return results[:-1], results[-1]


def attention_backward(query, pairs, bias, d_pieces, logs):
    rows, width = query.shape
    key_rows = pairs.shape[0]
    tile = min(rows, SCORE_CELLS // key_rows)
    fixed = lambda n: pl.BlockSpec((n, 2 * width), lambda i: (0, 0))
    return pl.pallas_call(
        backward_kernel,
        grid=(rows // tile,),
        in_specs=[
            pl.BlockSpec((tile, width), lambda i: (i, 0)),
            fixed(key_rows),
            pl.BlockSpec((tile, key_rows), lambda i: (i, 0)),
        ]
        + [pl.BlockSpec(d_pieces[0].shape, lambda i: (0, 0))] * HEAD_GROUPS
        + [pl.BlockSpec((tile, 128), lambda i: (i, 0))],
        out_specs=[
            pl.BlockSpec((tile, width), lambda i: (i, 0)),
            fixed(rows),
            fixed(key_rows - rows),
        ],
        out_shape=[
            jax.ShapeDtypeStruct((rows, width), bf16),
            jax.ShapeDtypeStruct((rows, 2 * width), f32),
            jax.ShapeDtypeStruct((key_rows - rows, 2 * width), bf16),
        ],
        scratch_shapes=[pltpu.VMEM((key_rows, width), bf16)] * 2
        + [pltpu.VMEM((rows, width), bf16)]
        + [pltpu.VMEM((key_rows, width), f32)] * 2,
        compiler_params=pltpu.CompilerParams(vmem_limit_bytes=56 * 1024 * 1024),
        cost_estimate=pl.CostEstimate(
            flops=30 * rows * key_rows * width, bytes_accessed=4 * rows * key_rows, transcendentals=0
        ),
        name="attention_backward",
    )(query, pairs, bias, *d_pieces, logs)


def swap_blocks(a, flags, block):
    for step, flag in enumerate(flags):
        size = block << step
        blocks = [a[:, i : i + size] for i in range(0, a.shape[1], size)]
        flipped = [blocks[i ^ 1] for i in range(len(blocks))]
        a = jnp.where(flag == 1, jnp.concatenate(flipped, axis=1), a)
    return a


def ffn_forward_kernel(
    flag_count,
    block,
    flag_ref,
    att_ref,
    att_far_ref,
    x_ref,
    x_far_ref,
    par_ref,
    ffn_ref,
    out_hbm,
    mix_hbm,
    in_near_hbm,
    in_far_hbm,
    down_near_hbm,
    down_far_hbm,
    first_ref,
    normed_ref,
    inverse_ref,
    mixed_ref,
    hidden_ref,
    active_ref,
    part_ref,
    send_ref,
    out_ref,
    mix_ref,
    in_near_ref,
    in_far_ref,
    down_near_ref,
    down_far_ref,
    sems,
):
    waits = copies(
        [
            (out_hbm, out_ref),
            (mix_hbm, mix_ref),
            (in_near_hbm, in_near_ref),
            (in_far_hbm, in_far_ref),
            (down_near_hbm, down_near_ref),
            (down_far_hbm, down_far_ref),
        ],
        sems,
    )
    flags = [flag_ref[i] for i in range(flag_count)]
    attended = jnp.concatenate([att_ref[...], att_far_ref[...]], axis=0)
    tokens = jnp.concatenate([x_ref[...], x_far_ref[...]], axis=0).astype(f32)
    waits[0].wait()
    branch = dot(attended, out_ref[...]) + par_ref[2:3]
    normed, inverse = normalize(tokens + branch)
    first = normed * par_ref[4:5] + par_ref[6:7]
    first_ref[...] = first
    normed_ref[...] = normed
    inverse_ref[...] = jnp.broadcast_to(inverse, inverse_ref.shape)
    waits[1].wait()
    mixed = dot(first.astype(bf16), mix_ref[...]).astype(bf16)
    mixed_ref[...] = mixed
    half = mixed.shape[1] // 2
    waits[2].wait()
    hidden = dot(mixed[:, :half], in_near_ref[...])
    waits[3].wait()
    hidden = hidden + dot(mixed[:, half:], in_far_ref[...]) + ffn_ref[...]
    hidden = swap_blocks(hidden, flags, block)
    hidden_ref[...] = hidden
    active = (0.5 * hidden * (1.0 + lax.erf(hidden * 0.7071067811865476))).astype(bf16)
    active_ref[...] = active
    units = active.shape[1] // 2
    waits[4].wait()
    part = dot(active[:, :units], down_near_ref[...])
    waits[5].wait()
    part = part + dot(active[:, units:], down_far_ref[...])
    part_ref[...] = part
    send_ref[...] = part.astype(bf16)


def column_sum(a):
    return jnp.sum(a, axis=0, keepdims=True)


def ffn_backward_kernel(
    flag_count,
    block,
    flag_ref,
    part_ref,
    got_ref,
    first_ref,
    cot_ref,
    cot_far_ref,
    hidden_ref,
    par_ref,
    mix_hbm,
    in_near_hbm,
    in_far_hbm,
    down_near_hbm,
    down_far_hbm,
    output_ref,
    keep_ref,
    send_ref,
    second_ref,
    d_hidden_ref,
    sums_ref,
    ffn_sum_ref,
    mix_ref,
    in_near_ref,
    in_far_ref,
    down_near_ref,
    down_far_ref,
    sems,
):
    waits = copies(
        [
            (down_near_hbm, down_near_ref),
            (down_far_hbm, down_far_ref),
            (in_near_hbm, in_near_ref),
            (in_far_hbm, in_far_ref),
            (mix_hbm, mix_ref),
        ],
        sems,
    )
    flags = [flag_ref[i] for i in range(flag_count)]
    rows = got_ref.shape[0] // 2
    other = jnp.concatenate([got_ref[rows:], got_ref[:rows]], axis=0).astype(f32)
    normed, inverse = normalize(first_ref[...] + part_ref[...] + other + par_ref[3:4])
    gain = par_ref[5:6]
    output_ref[...] = (normed[:rows] * gain + par_ref[7:8]).astype(bf16)
    out_grad = jnp.concatenate([cot_ref[...], cot_far_ref[...]], axis=0).astype(f32)
    d_two = norm_back(out_grad, normed, inverse, gain)
    d_second = d_two.astype(bf16)
    second_ref[...] = d_second
    sums_ref[...] = jnp.concatenate(
        [
            column_sum(out_grad[:rows] * normed[:rows]),
            column_sum(out_grad[:rows]),
            column_sum(d_second[:rows].astype(f32)),
            jnp.zeros((5, normed.shape[1]), f32),
        ],
        axis=0,
    )
    waits[0].wait()
    near = dot(d_second, down_near_ref[...], 1, 1)
    waits[1].wait()
    far = dot(d_second, down_far_ref[...], 1, 1)
    slope = gelu_slope(hidden_ref[...])
    d_hidden = jnp.concatenate([near, far], axis=1) * slope
    d_hidden = swap_blocks(d_hidden, flags, block).astype(bf16)
    d_hidden_ref[...] = d_hidden
    ffn_sum_ref[...] = column_sum(d_hidden.astype(f32))
    waits[2].wait()
    near = dot(d_hidden, in_near_ref[...], 1, 1).astype(bf16)
    waits[3].wait()
    far = dot(d_hidden, in_far_ref[...], 1, 1).astype(bf16)
    waits[4].wait()
    part = dot(jnp.concatenate([near, far], axis=1), mix_ref[...], 1, 1)
    keep_ref[...] = d_two[:rows] + part[:rows]
    send_ref[...] = part[rows:].astype(bf16)


def branch_backward_kernel(
    keep_ref, got_ref, normed_ref, inverse_ref, par_ref, out_ref, d_one_ref, branch_ref, sums_ref, *pieces
):
    d_first = keep_ref[...] + got_ref[...].astype(f32)
    normed, inverse = normed_ref[...], inverse_ref[:, :1]
    d_one = norm_back(d_first, normed, inverse, par_ref[4:5])
    d_one_ref[...] = d_one
    d_branch = d_one.astype(bf16)
    branch_ref[...] = d_branch
    sums_ref[...] = jnp.concatenate(
        [
            column_sum(d_first * normed),
            column_sum(d_first),
            column_sum(d_branch.astype(f32)),
            jnp.zeros((5, normed.shape[1]), f32),
        ],
        axis=0,
    )
    d_attended = dot(d_branch, out_ref[...], 1, 1).astype(bf16)
    columns = pieces[0].shape[1]
    for k, piece in enumerate(pieces):
        piece[...] = d_attended[:, k * columns : (k + 1) * columns]


def early_grads_kernel(
    small_each,
    x_ref,
    dq_ref,
    att_ref,
    branch_ref,
    sums_ref,
    sums_two_ref,
    ffn_ref,
    sel_ref,
    near_ref,
    line_ref,
    unit_ref,
    qkv_ref,
    keep_ref,
    send_ref,
    back_ref,
):
    columns = dq_ref.shape[1]
    d_query = dq_ref[...]
    back_ref[...] = dot(d_query, qkv_ref[:, 2 * columns :], 1, 1)
    queries = dot(x_ref[...], d_query, 0, 0)
    attended = dot(att_ref[...], line_ref[...]).astype(bf16)
    outs = dot(attended, branch_ref[...], 0, 0)
    sums = jnp.concatenate([column_sum(d_query.astype(f32)), jnp.zeros((7, columns), f32)], axis=0)
    biases = dot(sel_ref[...], sums.astype(bf16), 1, 1)[:, :2]
    first, second = sums_ref[...], sums_two_ref[...]
    vectors = jnp.concatenate(
        [first[2:3], second[2:3], first[0:1], second[0:1], first[1:2], second[1:2], first[3:5]], axis=0
    )
    vectors = dot(near_ref[...], vectors.astype(bf16), 0, 1)[:, :6]
    units = ffn_ref.shape[1]
    slot = iota((8, units), 1) % small_each == iota((8, units), 0)
    by_slot = jnp.where(slot, ffn_ref[...], 0.0).astype(bf16)
    ffn = dot(unit_ref[...], by_slot, 1, 1)[:, :small_each]
    total = [queries, outs, biases, vectors, ffn]
    rest = keep_ref.shape[1] - sum(a.shape[1] for a in total)
    total = jnp.concatenate([*total, jnp.zeros((queries.shape[0], rest), f32)], axis=1)
    half = total.shape[0] // 2
    keep_ref[...] = total[:half]
    send_ref[...] = total[half:].astype(bf16)


def late_grads_kernel(
    x_ref, own_ref, got_ref, sel_ref, qkv_ref, early_ref, early_send_ref, early_back_ref, *outs
):
    keep_ref, send_ref, back_ref, *back_pieces = outs
    pair_columns = own_ref.shape[1]
    columns = pair_columns // 2
    d_pairs = (own_ref[...] + got_ref[...].astype(f32)).astype(bf16)
    grad_back = early_back_ref[...] + dot(d_pairs, qkv_ref[:, :pair_columns], 1, 1)
    rows = back_ref.shape[0]
    back_ref[...] = grad_back[:rows]
    for k, piece in enumerate(back_pieces):
        piece[...] = grad_back[(k + 1) * rows : (k + 2) * rows].astype(bf16)
    pairs = dot(x_ref[...], d_pairs, 0, 0)
    sums = [jnp.zeros((1, columns), f32), column_sum(d_pairs[:, columns:].astype(f32))]
    sums = jnp.concatenate([*sums, jnp.zeros((6, columns), f32)], axis=0)
    bias = dot(sel_ref[...], sums.astype(bf16), 1, 1)[:, 1:2]
    half = pairs.shape[0] // 2
    width = x_ref.shape[1]
    at = columns + width + 1
    lane = iota(early_ref.shape, 1)
    keep_ref[:, :pair_columns] = pairs[:half]
    keep_ref[:, pair_columns:] = early_ref[...] + jnp.where(lane == at, bias[:half], 0.0)
    send_ref[:, :pair_columns] = pairs[half:].astype(bf16)
    late = early_send_ref[...].astype(f32) + jnp.where(lane == at, bias[half:], 0.0)
    send_ref[:, pair_columns:] = late.astype(bf16)


def finish_kernel(small_each, place_ref, own_ref, *refs):
    pieces, outs = refs[: HEAD_GROUPS - 1], refs[HEAD_GROUPS - 1 :]
    qkv_ref, out_ref, vec_ref, ffn_ref, gain_ref, shift_ref = outs
    group = place_ref[1]
    rows, width = out_ref.shape
    columns = width // HEAD_GROUPS
    line = [own_ref[...]] + [piece[...].astype(f32) for piece in pieces]
    for g in range(HEAD_GROUPS):
        mine = pick([a[:, : 3 * columns] for a in line], (g - group) % HEAD_GROUPS)
        for kind, at in enumerate((2, 0, 1)):
            start = kind * width + g * columns
            qkv_ref[:, start : start + columns] = mine[:, at * columns : (at + 1) * columns]
    rest = sum(a[:, 3 * columns :] for a in line[1:]) + line[0][:, 3 * columns :]
    out_ref[...] = rest[:, :width]
    small = rest[:, width : width + 8 + small_each]
    same_row = (iota((rows, rows), 0) == iota((rows, rows), 1)).astype(f32)
    turned = exact(small[:, :8], same_row, 0, 0)
    vec_ref[...] = turned[:4]
    gain_ref[...] = turned[4:6]
    shift_ref[...] = turned[6:8]
    each = small.shape[1] - 8
    lanes = rows * each
    select = (iota((each, lanes), 1) % each == iota((each, lanes), 0)).astype(f32)
    wide = exact(small[:, 8:], select)
    mine = iota((rows, lanes), 1) // each == iota((rows, lanes), 0)
    ffn_ref[...] = column_sum(jnp.where(mine, wide, 0.0))


def units_kernel(unit_ids, place_ref, keep_ref, got_ref, out_ref):
    core = place_ref[0]
    keep, got = keep_ref[...], got_ref[...].astype(f32)
    sources = [jnp.where(core == 0, keep, got), jnp.where(core == 0, got, keep)]
    count = 2 * len(unit_ids[0])
    each = out_ref.shape[1] // count
    blocks = {}
    for c, ids in enumerate(unit_ids):
        for slot, device in enumerate(ids):
            blocks[int(device)] = sources[c][:, slot * each : (slot + 1) * each]
    out_ref[...] = jnp.concatenate([blocks[i] for i in range(count)], axis=1)


class Grid:
    def __init__(self, mesh):
        self.dp, self.seq = mesh.shape["dp"], mesh.shape["seq"]
        self.count = self.dp * self.seq
        self.xs, self.parts = self.dp // 2, self.seq // HEAD_GROUPS
        bits = lambda axis, size: [(axis, b) for b in range(size.bit_length() - 1)]
        x_bits, self.part_bits = bits("x", self.xs), bits("q", self.parts)
        self.group_bits = [("g", 1), ("g", 0)]
        alternate = len(x_bits) == len(self.part_bits)
        self.plane = (
            x_bits + self.part_bits,
            self.part_bits + x_bits if alternate else x_bits + self.part_bits,
        )
        self.core_bit = [(("c", 0), ("c", 0))]
        self.plane_bits = list(zip(*self.plane))

    def place(self, device):
        dp, seq = divmod(device, self.seq)
        return {"x": dp // 2, "c": dp % 2, "g": seq // self.parts, "q": seq % self.parts}

    def device(self, at):
        return (at["x"] * 2 + at["c"]) * self.seq + at["g"] * self.parts + at["q"]

    def flip(self, bits_of_core):
        pairs = []
        for device in range(self.count):
            at = self.place(device)
            axis, bit = bits_of_core[at["c"]]
            at[axis] ^= 1 << bit
            pairs.append((device, self.device(at)))
        return pairs

    def shift(self, by):
        pairs = []
        for device in range(self.count):
            at = self.place(device)
            at["g"] = (at["g"] + by) % HEAD_GROUPS
            pairs.append((device, self.device(at)))
        return pairs

    def plane_masks(self, core):
        masks = {"x": [], "q": []}
        for index in range(self.xs * self.parts):
            for axis in masks:
                flips = [
                    1 << bit
                    for step, (a, bit) in enumerate(self.plane[core])
                    if a == axis and (index >> step) & 1
                ]
                masks[axis].append(sum(flips))
        return {axis: np.array(m, np.int32) for axis, m in masks.items()}


def same(bits):
    return [(bit, bit) for bit in bits]


def swap(grid, held, bits):
    return lax.ppermute(held, BOTH, grid.flip(bits))


def gather_near(grid, held, bit_pairs):
    for pair in bit_pairs:
        held = jnp.concatenate([held, swap(grid, held, pair)], axis=0)
    return held


def reduce_near(grid, total, bit_pairs):
    for pair in reversed(bit_pairs):
        half = total.shape[0] // 2
        got = swap(grid, total[half:].astype(bf16), pair)
        total = total[:half].astype(f32) + got.astype(f32)
    return total


def line_send(grid, pieces, sign):
    return [
        lax.ppermute(piece, BOTH, grid.shift(sign * (k + 1))) for k, piece in enumerate(pieces)
    ]


def tie(*values):
    return lax.optimization_barrier(values)


def on_device(
    grid,
    inputs,
    segments,
    rand_blocks,
    glob_blocks,
    w_qkv,
    w_out,
    w_in,
    w_down,
    vec_bias,
    ffn_bias,
    norm_gain,
    norm_shift,
    cotangent,
):
    local_len, width = inputs.shape[1:]
    rows_each, ff_each = w_in.shape[0], w_down.shape[0]
    ff = w_in.shape[1]
    ff_half = ff // 2
    groups, parts, xs = HEAD_GROUPS, grid.parts, grid.xs
    planes = xs * parts
    columns = width // groups
    line_len = groups * local_len
    small_each = ff_each // rows_each
    table_width = -(-(3 * columns + width + 8 + small_each) // 128) * 128
    dp_place, seq_place = lax.axis_index("dp"), lax.axis_index("seq")
    core, group, part = dp_place % 2, seq_place // parts, seq_place % parts
    coords = {"x": dp_place // 2, "c": core, "g": group, "q": part}
    place = jnp.stack([core, group]).astype(jnp.int32)
    chip_swap = lambda a: swap(grid, a, grid.core_bit[0])
    group_order = np.array([0, 2, 1, 3])
    group_slot = lambda g: (g % 2) * 2 + g // 2
    tokens = inputs.reshape(local_len, width)
    cot = cotangent.reshape(local_len, width)
    part_bits = same(grid.part_bits)

    masks = [grid.plane_masks(c) for c in range(2)]
    unit_ids = []
    for c in range(2):
        ids = [
            grid.device({"x": masks[c]["x"][index], "c": c, "g": g, "q": masks[c]["q"][index]})
            for index in range(planes)
            for g in group_order
        ]
        unit_ids.append(np.array(ids))

    *packets, own_units, far_units = call(
        functools.partial(pack_kernel, unit_ids),
        [((rows_each, table_width), bf16)] * groups
        + [((rows_each, ff_half), bf16)] * 2,
        place,
        w_qkv,
        w_out,
        w_in,
        vec_bias,
        ffn_bias.reshape(1, ff_each),
        norm_gain,
        norm_shift,
        name="pack_weights",
        scratch=(),
    )
    got_packets = line_send(grid, packets[1:], 1)

    plane_x = [coords["x"] ^ jnp.asarray(masks[c]["x"]) for c in range(2)]
    plane_q = [part ^ jnp.asarray(masks[c]["q"]) for c in range(2)]
    line_groups = (group - jnp.arange(groups, dtype=jnp.int32)) % groups
    row = jnp.arange(rows_each, dtype=jnp.int32)
    row_ids = jnp.arange(width, dtype=jnp.int32)
    by_core = lambda c, pair: jnp.where(c == 0, pair[0], pair[1])

    def device_of(x, c, g, q):
        return (x * 2 + c) * grid.seq + g * parts + q

    near_ids = jnp.stack(
        [
            device_of(by_core(c, plane_x)[:, None], c, line_groups[None, :], by_core(c, plane_q)[:, None])
            for c in (core, 1 - core)
        ]
    )
    near_rows = (near_ids[..., None] * rows_each + row).reshape(width)
    to_near = (row_ids[:, None] == near_rows[None, :]).astype(bf16)
    line_rows = (row_ids + group * columns) % width
    line_near = (line_rows[:, None] == near_rows[None, :]).astype(bf16)
    group_rows = group * columns + jnp.arange(columns, dtype=jnp.int32)
    near_group = (near_rows[:, None] == group_rows[None, :]).astype(bf16)
    own_x, own_q = by_core(core, plane_x), by_core(core, plane_q)
    slot_groups = jnp.asarray(group_order, jnp.int32)
    piece_ids = jnp.stack(
        [
            device_of(own_x[:, None], c, slot_groups[None, :], own_q[:, None])
            for c in (core, 1 - core)
        ],
        axis=2,
    )
    piece_rows = (piece_ids[..., None] * rows_each + row).reshape(width)
    to_piece = (row_ids[:, None] == piece_rows[None, :]).astype(bf16)
    own_ids = by_core(core, [jnp.asarray(ids, jnp.int32) for ids in unit_ids])
    unit = jnp.arange(ff_half, dtype=jnp.int32)
    unit_rows = jnp.repeat(own_ids, ff_each) * rows_each + (unit % ff_each) // small_each
    near_unit = (near_rows[:, None] == unit_rows[None, :]).astype(bf16)

    flags = [
        by_core(core, [(coords[axis] >> bit) & 1 for axis, bit in pair]) for pair in grid.plane_bits
    ]
    unit_block = ff_half // planes
    aligned = unit_block % 128 == 0
    kernel_flags = len(flags) if aligned else 0
    flag_row = jnp.stack(flags).astype(jnp.int32)
    outer_swap = (lambda a: a) if aligned else (lambda a: swap_blocks(a, flags, unit_block))

    own_blocks = local_len // BLK
    part_near = part ^ jnp.arange(parts, dtype=jnp.int32)
    chunk_ids = (line_groups[None, :] * parts + part_near[:, None]).reshape(-1)
    chunk_hot = chunk_ids[:, None] == jnp.arange(grid.seq, dtype=jnp.int32)[None, :]

    def take_chunks(chunks, hot):
        return jnp.sum(jnp.where(hot[:, :, None], chunks[None], 0), axis=1)

    offsets = jnp.arange(local_len, dtype=jnp.int32) // BLK
    block_near = (chunk_ids[:, None] * own_blocks + offsets[None, :]).reshape(-1)
    seg_near = take_chunks(segments.reshape(grid.seq, local_len), chunk_hot).reshape(-1)
    rand_line = take_chunks(rand_blocks.reshape(grid.seq, -1), chunk_hot[:groups])
    rand_line = rand_line.reshape(groups, own_blocks, 1, -1)
    rand_rows = jnp.broadcast_to(rand_line, (groups, own_blocks, BLK, rand_line.shape[-1]))
    rand_rows = rand_rows.reshape(line_len, -1)
    key_block, key_seg = block_near[None, :], seg_near[None, :]
    query_block, query_seg = block_near[:line_len, None], seg_near[:line_len, None]
    near = (key_block >= query_block - 1) & (key_block <= query_block + 1)
    for entry in range(rand_rows.shape[1]):
        near = near | (key_block == rand_rows[:, entry : entry + 1])
    glob_table = glob_blocks[0]
    doc = jnp.arange(glob_table.shape[0], dtype=jnp.int32)[None, :]
    for entry in range(glob_table.shape[1]):
        picked = jnp.sum(
            jnp.where(query_seg == doc, glob_table[None, :, entry], 0), axis=1, keepdims=True
        )
        near = near | (key_block == picked)
    mask_bias = jnp.where(near & (query_seg == key_seg), 0.0, masked_score).astype(f32)

    def group_step(held, entry):
        axis, bit = grid.group_bits[entry]
        got = swap(grid, held, ((axis, bit), (axis, bit)))
        upper = (group >> bit) & 1 == 1
        return jnp.where(upper, jnp.concatenate([got, held]), jnp.concatenate([held, got]))

    def plane_gather(held):
        for pair in grid.plane_bits[:-1]:
            held = jnp.concatenate([held, swap(grid, held, pair)], axis=0)
        return held

    got_units = chip_swap(far_units)
    down = group_step(w_down[None], 0)
    packet, sent_tokens = tie(packets[0], tokens)
    got_tokens = line_send(grid, [sent_tokens] * (groups - 1), 1)
    table = jnp.concatenate([packet, *got_packets], axis=0)
    units = jnp.concatenate([own_units, got_units], axis=0)[None]
    table, units, down = tie(table, units, down)
    down, units = group_step(down, 1), group_step(units, 0)
    table = gather_near(grid, table, grid.plane_bits)
    table, units, down = tie(table, units, down)
    units = group_step(units, 1)
    down_near = plane_gather(down.reshape(-1, width))
    table = gather_near(grid, table, grid.core_bit)
    table, *got_tokens = tie(table, *got_tokens)
    x_line = jnp.concatenate([tokens, *got_tokens], axis=0)
    x_near = dot(x_line, to_near).astype(bf16)

    query, own_pairs = call(
        qkv_kernel,
        [((line_len, columns), bf16), ((line_len, 2 * columns), bf16)],
        x_near,
        table,
        near_group,
        name="project",
    )
    own_pairs, units, down_near = tie(own_pairs, units, down_near)
    down_far = swap(grid, down_near, grid.plane_bits[-1])
    x_far, cot_far = chip_swap(tokens), chip_swap(cot)
    qkv_slice, out_line, params, ffn_row = call(
        functools.partial(unfold_kernel, small_each),
        [
            ((width, 3 * columns), bf16),
            ((width, width), bf16),
            ((8, width), f32),
            ((1, ff_half), f32),
        ],
        table,
        to_near,
        line_near,
        near_unit,
        name="unfold_weights",
    )
    ffn_row = outer_swap(ffn_row)
    kept_pairs, out_line, params, to_piece = tie(own_pairs, out_line, params, to_piece)
    pairs = jnp.concatenate([kept_pairs, swap(grid, own_pairs, part_bits[0])], axis=0)
    pairs = gather_near(grid, pairs, part_bits[1:])

    in_near = plane_gather(units.reshape(-1, ff_half))
    pairs, in_near = tie(pairs, in_near)
    in_far = swap(grid, in_near, grid.plane_bits[-1])
    in_near, in_far = outer_swap(in_near), outer_swap(in_far)

    att_pieces, logs = attention_forward(query, pairs, mask_bias)
    got_att = line_send(grid, att_pieces[1:], -1)
    attended = jnp.concatenate([att_pieces[0], *got_att], axis=1)
    attended_far = chip_swap(attended)

    half = width // 2
    chip_len = 2 * local_len
    weight_scratch = lambda *arrays: [pltpu.VMEM(a.shape, bf16) for a in arrays]
    first, normed, inverse, mixed, hidden, active, part_own, part_send = call(
        functools.partial(ffn_forward_kernel, kernel_flags, unit_block),
        [
            ((chip_len, width), f32),
            ((chip_len, width), f32),
            ((chip_len, 128), f32),
            ((chip_len, width), bf16),
            ((chip_len, ff_half), f32),
            ((chip_len, ff_half), bf16),
            ((chip_len, width), f32),
            ((chip_len, width), bf16),
        ],
        flag_row,
        attended,
        attended_far,
        tokens,
        x_far,
        params,
        ffn_row,
        out_line,
        to_piece,
        in_near,
        in_far,
        down_near,
        down_far,
        name="ffn_forward",
        in_place=(7, 8, 9, 10, 11, 12),
        scratch=weight_scratch(out_line, to_piece, in_near, in_far, down_near, down_far)
        + [pltpu.SemaphoreType.DMA((6,))],
    )
    part_got = chip_swap(part_send)

    output, first_keep, first_send, d_second, d_hidden, sums_two, ffn_sums = call(
        functools.partial(ffn_backward_kernel, kernel_flags, unit_block),
        [
            ((local_len, width), bf16),
            ((local_len, width), f32),
            ((local_len, width), bf16),
            ((chip_len, width), bf16),
            ((chip_len, ff_half), bf16),
            ((8, width), f32),
            ((1, ff_half), f32),
        ],
        flag_row,
        part_own,
        part_got,
        first,
        cot,
        cot_far,
        hidden,
        params,
        to_piece,
        in_near,
        in_far,
        down_near,
        down_far,
        name="ffn_backward",
        in_place=(8, 9, 10, 11, 12),
        scratch=weight_scratch(to_piece, in_near, in_far, down_near, down_far)
        + [pltpu.SemaphoreType.DMA((5,))],
    )
    first_got = chip_swap(first_send)
    down_send = dot(active[:, width:], d_second, 0, 0).astype(bf16)
    down_keep = dot(active[:, :width], d_second, 0, 0).astype(bf16)
    d_hidden, ffn_sums = outer_swap(d_hidden), outer_swap(ffn_sums)
    in_send = dot(mixed[:, half:], d_hidden, 0, 0).astype(bf16)
    in_keep = dot(mixed[:, :half], d_hidden, 0, 0).astype(bf16)
    d_one, d_branch, sums_one, *d_pieces = call(
        branch_backward_kernel,
        [((local_len, width), f32), ((local_len, width), bf16), ((8, width), f32)]
        + [((local_len, columns), bf16)] * groups,
        first_keep,
        first_got,
        normed[:local_len],
        inverse[:local_len],
        params,
        out_line,
        name="branch_backward",
    )
    got_d_att = line_send(grid, d_pieces[1:], 1)

    def far_sum(keep, send):
        return keep.astype(f32) + swap(grid, send, grid.plane_bits[-1]).astype(f32)

    down_total = far_sum(down_keep, down_send)
    in_total = far_sum(in_keep, in_send)

    def line_sum(total):
        total = total.reshape(groups, -1, total.shape[1])
        piece = lambda k: lax.dynamic_index_in_dim(
            total, group_slot((group + k) % groups), 0, keepdims=False
        )
        got = line_send(grid, [piece(k).astype(bf16) for k in range(1, groups)], 1)
        return sum((g.astype(f32) for g in got), piece(0))

    d_query, pairs_own, pairs_send = attention_backward(
        query, pairs, mask_bias, [d_pieces[0], *got_d_att], logs
    )
    pairs_own, pairs_send, down_total, in_total = tie(pairs_own, pairs_send, down_total, in_total)
    down_total = reduce_near(grid, down_total, grid.plane_bits[:-1])
    in_total = reduce_near(grid, in_total, grid.plane_bits[:-1])
    if parts == 2:
        pairs_got = swap(grid, pairs_send, part_bits[0])
    else:
        pairs_all = jnp.concatenate([pairs_own, pairs_send.astype(f32)])
        pairs_own = reduce_near(grid, pairs_all, part_bits)
        pairs_got = jnp.zeros(pairs_own.shape, bf16)
    early_width = table_width - 2 * columns
    early, early_send, early_back = call(
        functools.partial(early_grads_kernel, small_each),
        [
            ((width // 2, early_width), f32),
            ((width // 2, early_width), bf16),
            ((line_len, width), f32),
        ],
        x_near,
        d_query,
        attended,
        d_branch,
        sums_one,
        sums_two,
        ffn_sums,
        near_group,
        to_near,
        line_near,
        near_unit,
        qkv_slice,
        name="early_gradients",
    )
    pairs_own, down_total, early = tie(pairs_own, down_total, early)
    grad_keep, grad_send, back_own, *back_pieces = call(
        late_grads_kernel,
        [
            ((width // 2, table_width), f32),
            ((width // 2, table_width), bf16),
            ((local_len, width), f32),
        ]
        + [((local_len, width), bf16)] * (groups - 1),
        x_near,
        pairs_own,
        pairs_got,
        near_group,
        qkv_slice,
        early,
        early_send,
        early_back,
        name="late_gradients",
    )
    grad_send, in_total = tie(grad_send, in_total)
    sum_down = line_sum(down_total)
    in_pairs = line_sum(in_total)
    got_back = line_send(grid, back_pieces, -1)
    total = grad_keep + chip_swap(grad_send).astype(f32)
    total = reduce_near(grid, total, grid.plane_bits)
    total, in_pairs, d_one = tie(total, in_pairs, d_one)
    in_got = chip_swap(in_pairs[rows_each:])
    (sum_in,) = call(
        functools.partial(units_kernel, unit_ids),
        [((rows_each, ff), f32)],
        place,
        in_pairs[:rows_each],
        in_got,
        name="order_units",
    )

    got_total = line_send(
        grid, [total[k * rows_each : (k + 1) * rows_each].astype(bf16) for k in range(1, groups)], -1
    )
    input_grad = d_one + sum((g.astype(f32) for g in got_back), back_own)
    sum_qkv, sum_out, sum_vec, sum_ffn, sum_gain, sum_shift = call(
        functools.partial(finish_kernel, small_each),
        [
            ((rows_each, 3 * width), f32),
            ((rows_each, width), f32),
            ((4, rows_each), f32),
            ((1, ff_each), f32),
            ((2, rows_each), f32),
            ((2, rows_each), f32),
        ],
        place,
        total[:rows_each],
        *got_total,
        name="finish",
    )
    return (
        output[None],
        input_grad[None],
        sum_qkv,
        sum_out,
        sum_in,
        sum_down,
        sum_vec,
        sum_ffn.reshape(ff_each),
        sum_gain,
        sum_shift,
    )


def solution(mesh):
    return jax.shard_map(
        functools.partial(on_device, Grid(mesh)),
        mesh=mesh,
        in_specs=(
            P("dp", "seq", None),
            P("dp", None),
            P("dp", None, None),
            P("dp", None, None),
            P(("dp", "seq"), None),
            P(("dp", "seq"), None),
            P(("dp", "seq"), None),
            P(("dp", "seq"), None),
            P(None, ("dp", "seq")),
            P(("dp", "seq")),
            P(None, ("dp", "seq")),
            P(None, ("dp", "seq")),
            P("dp", "seq", None),
        ),
        out_specs=(
            P("dp", "seq", None),
            P("dp", "seq", None),
            P(("dp", "seq"), None),
            P(("dp", "seq"), None),
            P(("dp", "seq"), None),
            P(("dp", "seq"), None),
            P(None, ("dp", "seq")),
            P(("dp", "seq")),
            P(None, ("dp", "seq")),
            P(None, ("dp", "seq")),
        ),
        check_vma=False,
    )
```

```python
import functools

import jax
import jax.numpy as jnp
import numpy as np
from jax import lax
from jax.experimental import pallas as pl
from jax.experimental.pallas import tpu as pltpu
from jax.sharding import PartitionSpec as P

HD = 64
BLK = 64
HEAD_GROUPS = 4
SCORE_CELLS = 512 * 1024

norm_eps = 1e-05
masked_score = -1e30
BOTH = ("dp", "seq")
bf16 = jnp.bfloat16
f32 = jnp.float32


def normalize(field_in):
    mean_row = jnp.mean(field_in, axis=-1, keepdims=True)
    centred = field_in - mean_row
    inverse = lax.rsqrt(jnp.mean(centred * centred, axis=-1, keepdims=True) + norm_eps)
    return (centred * inverse, inverse)


def norm_back(grad_in, normed, inverse, gain_row):
    weighted = grad_in * gain_row
    inner = jnp.mean(weighted * normed, axis=-1, keepdims=True)
    return inverse * (weighted - jnp.mean(weighted, axis=-1, keepdims=True) - normed * inner)


def gelu_slope(field_in):
    return (
        0.5 * (1.0 + lax.erf(field_in * 0.7071067811865476))
        + field_in * jnp.exp(-0.5 * field_in * field_in) * 0.3989422804014327
    )


def dot(left, right, left_dim=1, right_dim=0):
    return lax.dot_general(
        left, right, (((left_dim,), (right_dim,)), ((), ())), preferred_element_type=f32
    )


def call(body, outs, *args, name, scratch=(), flops=1e8, in_place=()):
    space = lambda i, a: (
        pl.ANY if i in in_place else pltpu.SMEM if a.dtype == jnp.int32 else pltpu.VMEM
    )
    specs = [pl.BlockSpec(memory_space=space(i, a)) for i, a in enumerate(args)]
    moved = sum(int(np.prod(a.shape)) * a.dtype.itemsize for a in args)
    return pl.pallas_call(
        body,
        in_specs=specs,
        out_specs=[pl.BlockSpec(memory_space=pltpu.VMEM)] * len(outs),
        out_shape=[jax.ShapeDtypeStruct(shape, dtype) for shape, dtype in outs],
        scratch_shapes=list(scratch),
        compiler_params=pltpu.CompilerParams(vmem_limit_bytes=56 * 1024 * 1024),
        cost_estimate=pl.CostEstimate(flops=int(flops), bytes_accessed=moved, transcendentals=0),
        name=name,
    )(*args)


def copies(pairs, sems):
    started = []
    for i, (source, target) in enumerate(pairs):
        copy = pltpu.make_async_copy(source, target, sems.at[i])
        copy.start()
        started.append(copy)
    return started


def exact(left, right, left_dim=1, right_dim=0):
    return lax.dot_general(
        left,
        right,
        (((left_dim,), (right_dim,)), ((), ())),
        preferred_element_type=f32,
        precision=lax.Precision.HIGHEST,
    )


def iota(shape, dim):
    return lax.broadcasted_iota(jnp.int32, shape, dim)


def spread_rows(row, rows, each):
    lanes = row.shape[1]
    picked = jnp.where(iota((rows, lanes), 1) // each == iota((rows, lanes), 0), row, 0.0)
    select = (iota((lanes, each), 0) % each == iota((lanes, each), 1)).astype(f32)
    return exact(picked, select)


def pick(options, index):
    chosen = options[0]
    for i, option in enumerate(options[1:]):
        chosen = jnp.where(index == i + 1, option, chosen)
    return chosen


def crossed(number):
    return (number % 2) * 2 + number // 2


def pack_kernel(
    unit_ids,
    place_ref,
    qkv_ref,
    out_ref,
    in_ref,
    x_ref,
    cot_ref,
    vec_ref,
    ffn_ref,
    gain_ref,
    shift_ref,
    *outs,
):
    core, group = place_ref[0], place_ref[1]
    rows, width = out_ref.shape
    columns = width // HEAD_GROUPS
    rolled = lambda g: [
        qkv_ref[:, kind * width + g * columns : kind * width + (g + 1) * columns] for kind in (1, 2, 0)
    ]
    by_group = [jnp.concatenate(rolled(g), axis=1) for g in range(HEAD_GROUPS)]
    same_row = (iota((rows, rows), 0) == iota((rows, rows), 1)).astype(bf16)
    turned = [dot(same_row, ref[...], 1, 1) for ref in (vec_ref, gain_ref, shift_ref)]
    turned.append(spread_rows(ffn_ref[...].astype(f32), rows, ffn_ref.shape[1] // rows))
    small = jnp.concatenate(turned, axis=1).astype(bf16)
    for k in range(HEAD_GROUPS):
        chosen = pick(by_group, group ^ crossed(k))
        rest = outs[k].shape[1] - 3 * columns - width - small.shape[1]
        outs[k][:, : 2 * columns] = chosen[:, : 2 * columns]
        outs[k][:, 2 * columns : 2 * columns + width] = out_ref[...]
        outs[k][:, 2 * columns + width :] = jnp.concatenate(
            [chosen[:, 2 * columns :], small, jnp.zeros((rows, rest), bf16)], axis=1
        )
    each = ffn_ref.shape[1]
    units = [
        jnp.concatenate([in_ref[:, i * each : (i + 1) * each] for i in ids], axis=1) for ids in unit_ids
    ]
    outs[HEAD_GROUPS][...] = jnp.where(core == 0, units[0], units[1])
    far = jnp.where(core == 0, units[1], units[0])
    far_ref = outs[HEAD_GROUPS + 1]
    tokens = x_ref.shape[0]
    top = far_ref.shape[0] - 2 * tokens
    blank = jnp.zeros((top - 2 * rows, width), bf16)
    far_ref[:top] = jnp.concatenate([far[:, :width], far[:, width:], blank][: 3 if top > 2 * rows else 2])
    far_ref[top : top + tokens] = x_ref[...]
    far_ref[top + tokens :] = cot_ref[...]


def unfold_kernel(
    small_each, table_ref, far_ref, near_ref, line_ref, unit_ref, qkv_ref, out_ref, par_ref, ffn_ref
):
    columns = qkv_ref.shape[1] // 3
    width = out_ref.shape[1]
    start, at = 2 * columns, 2 * columns + width
    near = near_ref[...]
    both = lambda i, j: jnp.concatenate([table_ref[:, i:j], far_ref[:, i:j]], axis=0)
    rest = both(at, table_ref.shape[1])
    qkv_ref[:, :start] = dot(near, both(0, start)).astype(bf16)
    qkv_ref[:, start:] = dot(near, rest[:, :columns]).astype(bf16)
    out_ref[...] = dot(line_ref[...], both(start, at)).astype(bf16)
    small = rest[:, columns : columns + 8 + small_each]
    par_ref[...] = dot(small[:, :8], near, 0, 1)
    by_slot = dot(small[:, 8:], unit_ref[...], 0, 0)
    slot = iota(by_slot.shape, 1) % small_each == iota(by_slot.shape, 0)
    ffn_ref[...] = jnp.sum(jnp.where(slot, by_slot, 0.0), axis=0, keepdims=True)


def qkv_kernel(x_ref, table_ref, far_ref, sel_ref, q_ref, pair_ref):
    columns = q_ref.shape[1]
    width = x_ref.shape[1]
    half = width // 2
    start, at = 2 * columns, 2 * columns + width
    pairs = dot(x_ref[:, :half], table_ref[:, :start]) + dot(x_ref[:, half:], far_ref[:, :start])
    rest = jnp.concatenate([table_ref[:, at:], far_ref[:, at:]], axis=0)
    biases = dot(rest[:, columns : columns + 8], sel_ref[...], 0, 0)
    values = pairs[:, columns:] + biases[1:2]
    pair_ref[...] = jnp.concatenate([pairs[:, :columns], values], axis=1).astype(bf16)
    queries = dot(x_ref[...], rest[:, :columns]) + biases[0:1]
    q_ref[...] = (queries * HD ** (-0.5)).astype(bf16)


def head_mask(shape, head):
    lane = iota(shape, 1)
    return (lane >= head * HD) & (lane < (head + 1) * HD)


def split_pairs(pair_ref, k_ref, v_ref):
    width = k_ref.shape[1]
    k_ref[...] = pair_ref[:, :width]
    v_ref[...] = pair_ref[:, width:]


def forward_kernel(q_ref, kv_ref, b_ref, *refs):
    *o_refs, l_ref, k_ref, v_ref = refs
    step = pl.program_id(0)

    @pl.when(step == 0)
    def _():
        split_pairs(kv_ref, k_ref, v_ref)

    query, keys, values, bias = q_ref[...], k_ref[...], v_ref[...], b_ref[...]
    rows, width = query.shape
    out = jnp.zeros(query.shape, f32)
    logs = jnp.zeros(l_ref.shape, f32)
    for head in range(width // HD):
        mine = head_mask(query.shape, head)
        scores = dot(jnp.where(mine, query, jnp.zeros_like(query)), keys, 1, 1) + bias
        top = jnp.max(scores, axis=1, keepdims=True)
        terms = jnp.exp(scores - top)
        total = jnp.sum(terms, axis=1, keepdims=True)
        probs = (terms * (1.0 / total)).astype(bf16)
        out = out + jnp.where(mine, dot(probs, values), 0.0)
        logs = jnp.where(iota(l_ref.shape, 1) == head, top + jnp.log(total), logs)
    l_ref[...] = logs
    low = out.astype(bf16)
    piece = o_refs[0].shape[0]
    each = rows // piece
    for k, o_ref in enumerate(o_refs):
        start = (k % each) * piece

        @pl.when(step == k // each)
        def _(o_ref=o_ref, start=start):
            o_ref[...] = low[start : start + piece]


def backward_kernel(q_ref, kv_ref, b_ref, *refs):
    pieces, refs = refs[:HEAD_GROUPS], refs[HEAD_GROUPS:]
    l_ref, dq_ref, own_ref, send_ref, k_ref, v_ref, d_ref, dk_ref, dv_ref = refs
    step = pl.program_id(0)
    rows, width = q_ref.shape

    @pl.when(step == 0)
    def _():
        split_pairs(kv_ref, k_ref, v_ref)
        dk_ref[...] = jnp.zeros(dk_ref.shape, f32)
        dv_ref[...] = jnp.zeros(dv_ref.shape, f32)
        piece = pieces[0].shape[0]
        for k, ref in enumerate(pieces):
            d_ref[k * piece : (k + 1) * piece] = ref[...]

    query, keys, values, bias = q_ref[...], k_ref[...], v_ref[...], b_ref[...]
    d_att = d_ref[pl.ds(pl.multiple_of(step * rows, rows), rows)]
    logs = l_ref[...]
    d_query = jnp.zeros(query.shape, f32)
    for head in range(width // HD):
        mine = head_mask(query.shape, head)
        q_head = jnp.where(mine, query, jnp.zeros_like(query))
        d_head = jnp.where(mine, d_att, jnp.zeros_like(d_att))
        scores = dot(q_head, keys, 1, 1) + bias
        weights = jnp.exp(scores - logs[:, head : head + 1])
        d_probs = dot(d_head, values, 1, 1)
        delta = jnp.sum(weights * d_probs, axis=1, keepdims=True)
        d_scores = (weights * (d_probs - delta)).astype(bf16)
        d_query = d_query + jnp.where(mine, dot(d_scores, keys), 0.0)
        dk_ref[...] += dot(d_scores, q_head, 0, 0)
        dv_ref[...] += dot(weights.astype(bf16), d_head, 0, 0)
    dq_ref[...] = (d_query * HD ** (-0.5)).astype(bf16)

    @pl.when(step == pl.num_programs(0) - 1)
    def _():
        kept = own_ref.shape[0]
        own_ref[:, :width] = dk_ref[:kept]
        own_ref[:, width:] = dv_ref[:kept]
        send_ref[:, :width] = dk_ref[kept:].astype(bf16)
        send_ref[:, width:] = dv_ref[kept:].astype(bf16)


def attention_forward(query, pairs, bias):
    rows, width = query.shape
    key_rows = pairs.shape[0]
    tile = min(rows, SCORE_CELLS // key_rows)
    piece = rows // HEAD_GROUPS
    results = pl.pallas_call(
        forward_kernel,
        grid=(rows // tile,),
        in_specs=[
            pl.BlockSpec((tile, width), lambda i: (i, 0)),
            pl.BlockSpec((key_rows, 2 * width), lambda i: (0, 0)),
            pl.BlockSpec((tile, key_rows), lambda i: (i, 0)),
        ],
        out_specs=[pl.BlockSpec((piece, width), lambda i: (0, 0))] * HEAD_GROUPS
        + [pl.BlockSpec((tile, 128), lambda i: (i, 0))],
        out_shape=[jax.ShapeDtypeStruct((piece, width), bf16)] * HEAD_GROUPS
        + [jax.ShapeDtypeStruct((rows, 128), f32)],
        scratch_shapes=[pltpu.VMEM((key_rows, width), bf16)] * 2,
        compiler_params=pltpu.CompilerParams(vmem_limit_bytes=56 * 1024 * 1024),
        cost_estimate=pl.CostEstimate(
            flops=16 * rows * key_rows * width, bytes_accessed=4 * rows * key_rows, transcendentals=0
        ),
        name="attention_forward",
    )(query, pairs, bias)
    return results[:-1], results[-1]


def attention_backward(query, pairs, bias, d_pieces, logs):
    rows, width = query.shape
    key_rows = pairs.shape[0]
    tile = min(rows, SCORE_CELLS // key_rows)
    fixed = lambda n: pl.BlockSpec((n, 2 * width), lambda i: (0, 0))
    return pl.pallas_call(
        backward_kernel,
        grid=(rows // tile,),
        in_specs=[
            pl.BlockSpec((tile, width), lambda i: (i, 0)),
            fixed(key_rows),
            pl.BlockSpec((tile, key_rows), lambda i: (i, 0)),
        ]
        + [pl.BlockSpec(d_pieces[0].shape, lambda i: (0, 0))] * HEAD_GROUPS
        + [pl.BlockSpec((tile, 128), lambda i: (i, 0))],
        out_specs=[
            pl.BlockSpec((tile, width), lambda i: (i, 0)),
            fixed(rows),
            fixed(key_rows - rows),
        ],
        out_shape=[
            jax.ShapeDtypeStruct((rows, width), bf16),
            jax.ShapeDtypeStruct((rows, 2 * width), f32),
            jax.ShapeDtypeStruct((key_rows - rows, 2 * width), bf16),
        ],
        scratch_shapes=[pltpu.VMEM((key_rows, width), bf16)] * 2
        + [pltpu.VMEM((rows, width), bf16)]
        + [pltpu.VMEM((key_rows, width), f32)] * 2,
        compiler_params=pltpu.CompilerParams(vmem_limit_bytes=56 * 1024 * 1024),
        cost_estimate=pl.CostEstimate(
            flops=30 * rows * key_rows * width, bytes_accessed=4 * rows * key_rows, transcendentals=0
        ),
        name="attention_backward",
    )(query, pairs, bias, *d_pieces, logs)


def swap_blocks(a, flags, block):
    for step, flag in enumerate(flags):
        size = block << step
        blocks = [a[:, i : i + size] for i in range(0, a.shape[1], size)]
        flipped = [blocks[i ^ 1] for i in range(len(blocks))]
        a = jnp.where(flag == 1, jnp.concatenate(flipped, axis=1), a)
    return a


def ffn_forward_kernel(
    flag_count,
    block,
    flag_ref,
    att_ref,
    att_far_ref,
    x_ref,
    far_ref,
    par_ref,
    ffn_ref,
    out_hbm,
    mix_hbm,
    in_near_hbm,
    in_far_hbm,
    down_near_hbm,
    down_far_hbm,
    first_ref,
    normed_ref,
    inverse_ref,
    mixed_ref,
    hidden_ref,
    active_ref,
    part_ref,
    send_ref,
    out_ref,
    mix_ref,
    in_near_ref,
    in_far_ref,
    down_near_ref,
    down_far_ref,
    sems,
):
    waits = copies(
        [
            (out_hbm, out_ref),
            (mix_hbm, mix_ref),
            (in_near_hbm, in_near_ref),
            (in_far_hbm, in_far_ref),
            (down_near_hbm, down_near_ref),
            (down_far_hbm, down_far_ref),
        ],
        sems,
    )
    flags = [flag_ref[i] for i in range(flag_count)]
    attended = jnp.concatenate([att_ref[...], att_far_ref[...]], axis=0)
    rows = x_ref.shape[0]
    top = far_ref.shape[0] - 2 * rows
    tokens = jnp.concatenate([x_ref[...], far_ref[top : top + rows]], axis=0).astype(f32)
    waits[0].wait()
    branch = dot(attended, out_ref[...]) + par_ref[2:3]
    normed, inverse = normalize(tokens + branch)
    first = normed * par_ref[4:5] + par_ref[6:7]
    first_ref[...] = first
    normed_ref[...] = normed
    inverse_ref[...] = jnp.broadcast_to(inverse, inverse_ref.shape)
    waits[1].wait()
    mixed = dot(first.astype(bf16), mix_ref[...]).astype(bf16)
    mixed_ref[...] = mixed
    half = mixed.shape[1] // 2
    waits[2].wait()
    hidden = dot(mixed[:, :half], in_near_ref[...])
    waits[3].wait()
    hidden = hidden + dot(mixed[:, half:], in_far_ref[...]) + ffn_ref[...]
    hidden = swap_blocks(hidden, flags, block)
    hidden_ref[...] = hidden
    active = (0.5 * hidden * (1.0 + lax.erf(hidden * 0.7071067811865476))).astype(bf16)
    active_ref[...] = active
    units = active.shape[1] // 2
    waits[4].wait()
    part = dot(active[:, :units], down_near_ref[...])
    waits[5].wait()
    part = part + dot(active[:, units:], down_far_ref[...])
    part_ref[...] = part
    send_ref[...] = part.astype(bf16)


def column_sum(a):
    return jnp.sum(a, axis=0, keepdims=True)


def ffn_backward_kernel(
    flag_count,
    block,
    flag_ref,
    part_ref,
    got_ref,
    first_ref,
    cot_ref,
    far_ref,
    hidden_ref,
    par_ref,
    mix_hbm,
    in_near_hbm,
    in_far_hbm,
    down_near_hbm,
    down_far_hbm,
    output_ref,
    keep_ref,
    send_ref,
    second_ref,
    d_hidden_ref,
    sums_ref,
    ffn_sum_ref,
    mix_ref,
    in_near_ref,
    in_far_ref,
    down_near_ref,
    down_far_ref,
    sems,
):
    waits = copies(
        [
            (down_near_hbm, down_near_ref),
            (down_far_hbm, down_far_ref),
            (in_near_hbm, in_near_ref),
            (in_far_hbm, in_far_ref),
            (mix_hbm, mix_ref),
        ],
        sems,
    )
    flags = [flag_ref[i] for i in range(flag_count)]
    rows = got_ref.shape[0] // 2
    other = jnp.concatenate([got_ref[rows:], got_ref[:rows]], axis=0).astype(f32)
    normed, inverse = normalize(first_ref[...] + part_ref[...] + other + par_ref[3:4])
    gain = par_ref[5:6]
    output_ref[...] = (normed[:rows] * gain + par_ref[7:8]).astype(bf16)
    out_grad = jnp.concatenate([cot_ref[...], far_ref[far_ref.shape[0] - rows :]], axis=0).astype(f32)
    d_two = norm_back(out_grad, normed, inverse, gain)
    d_second = d_two.astype(bf16)
    second_ref[...] = d_second
    sums_ref[...] = jnp.concatenate(
        [
            column_sum(out_grad[:rows] * normed[:rows]),
            column_sum(out_grad[:rows]),
            column_sum(d_second[:rows].astype(f32)),
            jnp.zeros((5, normed.shape[1]), f32),
        ],
        axis=0,
    )
    waits[0].wait()
    near = dot(d_second, down_near_ref[...], 1, 1)
    waits[1].wait()
    far = dot(d_second, down_far_ref[...], 1, 1)
    slope = gelu_slope(hidden_ref[...])
    d_hidden = jnp.concatenate([near, far], axis=1) * slope
    d_hidden = swap_blocks(d_hidden, flags, block).astype(bf16)
    d_hidden_ref[...] = d_hidden
    ffn_sum_ref[...] = column_sum(d_hidden.astype(f32))
    waits[2].wait()
    near = dot(d_hidden, in_near_ref[...], 1, 1).astype(bf16)
    waits[3].wait()
    far = dot(d_hidden, in_far_ref[...], 1, 1).astype(bf16)
    waits[4].wait()
    part = dot(jnp.concatenate([near, far], axis=1), mix_ref[...], 1, 1)
    keep_ref[...] = d_two[:rows] + part[:rows]
    send_ref[...] = part[rows:].astype(bf16)


def branch_backward_kernel(
    keep_ref, got_ref, normed_ref, inverse_ref, par_ref, out_ref, d_one_ref, branch_ref, sums_ref, *pieces
):
    d_first = keep_ref[...] + got_ref[...].astype(f32)
    normed, inverse = normed_ref[...], inverse_ref[:, :1]
    d_one = norm_back(d_first, normed, inverse, par_ref[4:5])
    d_one_ref[...] = d_one
    d_branch = d_one.astype(bf16)
    branch_ref[...] = d_branch
    sums_ref[...] = jnp.concatenate(
        [
            column_sum(d_first * normed),
            column_sum(d_first),
            column_sum(d_branch.astype(f32)),
            jnp.zeros((5, normed.shape[1]), f32),
        ],
        axis=0,
    )
    d_attended = dot(d_branch, out_ref[...], 1, 1).astype(bf16)
    columns = pieces[0].shape[1]
    for k, piece in enumerate(pieces):
        piece[...] = d_attended[:, k * columns : (k + 1) * columns]


def branch_grads_kernel(
    small_each,
    att_ref,
    branch_ref,
    sums_ref,
    sums_two_ref,
    ffn_ref,
    near_ref,
    line_ref,
    unit_ref,
    keep_ref,
    send_ref,
    small_ref,
):
    attended = dot(att_ref[...], line_ref[...]).astype(bf16)
    outs = dot(attended, branch_ref[...], 0, 0)
    half = outs.shape[0] // 2
    keep_ref[...] = outs[:half]
    send_ref[...] = outs[half:].astype(bf16)
    first, second = sums_ref[...], sums_two_ref[...]
    blank = jnp.zeros((2, first.shape[1]), f32)
    vectors = jnp.concatenate(
        [blank, first[2:3], second[2:3], first[0:1], second[0:1], first[1:2], second[1:2]], axis=0
    )
    vectors = dot(near_ref[...], vectors.astype(bf16), 0, 1)
    units = ffn_ref.shape[1]
    slot = iota((8, units), 1) % small_each == iota((8, units), 0)
    by_slot = jnp.where(slot, ffn_ref[...], 0.0).astype(bf16)
    ffn = dot(unit_ref[...], by_slot, 1, 1)
    small_ref[...] = jnp.concatenate([vectors, ffn], axis=1)


def query_grads_kernel(x_ref, dq_ref, sel_ref, qkv_ref, grad_ref, bias_ref, back_ref):
    columns = dq_ref.shape[1]
    d_query = dq_ref[...]
    back_ref[...] = dot(d_query, qkv_ref[:, 2 * columns :], 1, 1)
    grad_ref[...] = dot(x_ref[...], d_query, 0, 0)
    sums = jnp.concatenate([column_sum(d_query.astype(f32)), jnp.zeros((7, columns), f32)], axis=0)
    bias_ref[...] = dot(sel_ref[...], sums.astype(bf16), 1, 1)


def pair_grads_kernel(
    x_ref,
    own_ref,
    got_ref,
    sel_ref,
    qkv_ref,
    out_ref,
    out_send_ref,
    small_ref,
    query_ref,
    bias_ref,
    query_back_ref,
    keep_ref,
    send_ref,
    back_ref,
    back_send_ref,
):
    pair_columns = own_ref.shape[1]
    columns = pair_columns // 2
    width = x_ref.shape[1]
    d_pairs = (own_ref[...] + got_ref[...].astype(f32)).astype(bf16)
    grad_back = query_back_ref[...] + dot(d_pairs, qkv_ref[:, :pair_columns], 1, 1)
    rows = back_ref.shape[0]
    back_ref[...] = grad_back[:rows]
    back_send_ref[...] = grad_back[rows:].astype(bf16)
    pairs = dot(x_ref[...], d_pairs, 0, 0)
    sums = [jnp.zeros((1, columns), f32), column_sum(d_pairs[:, columns:].astype(f32))]
    sums = jnp.concatenate([*sums, jnp.zeros((6, columns), f32)], axis=0)
    bias = dot(sel_ref[...], sums.astype(bf16), 1, 1)
    small = small_ref[...]
    vectors = small[:, :8] + bias + bias_ref[...]
    at = pair_columns + width
    rest = keep_ref.shape[1] - at - columns - 16
    last = [query_ref[...], vectors, small[:, 8:], jnp.zeros((width, rest), f32)]
    last = jnp.concatenate(last, axis=1)
    half = width // 2
    keep_ref[:, :pair_columns] = pairs[:half]
    keep_ref[:, pair_columns:at] = out_ref[...]
    keep_ref[:, at:] = last[:half]
    send_ref[:, :pair_columns] = pairs[half:].astype(bf16)
    send_ref[:, pair_columns:at] = out_send_ref[...]
    send_ref[:, at:] = last[half:].astype(bf16)


def finish_kernel(small_each, place_ref, own_ref, *refs):
    pieces, outs = refs[: HEAD_GROUPS - 1], refs[HEAD_GROUPS - 1 :]
    qkv_ref, out_ref, vec_ref, ffn_ref, gain_ref, shift_ref = outs
    group = place_ref[1]
    rows, width = out_ref.shape
    columns = width // HEAD_GROUPS
    line = [own_ref[...]] + [piece[...].astype(f32) for piece in pieces]
    at = 2 * columns + width
    for g in range(HEAD_GROUPS):
        source = crossed(group ^ g)
        pairs = pick([a[:, : 2 * columns] for a in line], source)
        queries = pick([a[:, at : at + columns] for a in line], source)
        for kind, mine in enumerate((queries, pairs[:, :columns], pairs[:, columns:])):
            start = kind * width + g * columns
            qkv_ref[:, start : start + columns] = mine
    out_ref[...] = sum(a[:, 2 * columns : at] for a in line)
    rest = sum(a[:, at:] for a in line)
    small = rest[:, columns : columns + 8 + small_each]
    same_row = (iota((rows, rows), 0) == iota((rows, rows), 1)).astype(f32)
    turned = exact(small[:, :8], same_row, 0, 0)
    vec_ref[...] = turned[:4]
    gain_ref[...] = turned[4:6]
    shift_ref[...] = turned[6:8]
    each = small.shape[1] - 8
    lanes = rows * each
    select = (iota((each, lanes), 1) % each == iota((each, lanes), 0)).astype(f32)
    wide = exact(small[:, 8:], select)
    mine = iota((rows, lanes), 1) // each == iota((rows, lanes), 0)
    ffn_ref[...] = column_sum(jnp.where(mine, wide, 0.0))


def units_kernel(unit_ids, place_ref, keep_ref, got_ref, out_ref):
    core = place_ref[0]
    keep, got = keep_ref[...], got_ref[...].astype(f32)
    sources = [jnp.where(core == 0, keep, got), jnp.where(core == 0, got, keep)]
    count = 2 * len(unit_ids[0])
    each = out_ref.shape[1] // count
    blocks = {}
    for c, ids in enumerate(unit_ids):
        for slot, device in enumerate(ids):
            blocks[int(device)] = sources[c][:, slot * each : (slot + 1) * each]
    out_ref[...] = jnp.concatenate([blocks[i] for i in range(count)], axis=1)


class Grid:
    def __init__(self, mesh):
        self.dp, self.seq = mesh.shape["dp"], mesh.shape["seq"]
        self.count = self.dp * self.seq
        self.xs, self.parts = self.dp // 2, self.seq // HEAD_GROUPS
        bits = lambda axis, size: [(axis, b) for b in range(size.bit_length() - 1)]
        x_bits, self.part_bits = bits("x", self.xs), bits("q", self.parts)
        self.group_bits = [("g", 1), ("g", 0)]
        alternate = len(x_bits) == len(self.part_bits)
        self.plane = (
            x_bits + self.part_bits,
            self.part_bits + x_bits if alternate else x_bits + self.part_bits,
        )
        self.core_bit = [(("c", 0), ("c", 0))]
        self.plane_bits = list(zip(*self.plane))

    def place(self, device):
        dp, seq = divmod(device, self.seq)
        return {"x": dp // 2, "c": dp % 2, "g": seq // self.parts, "q": seq % self.parts}

    def device(self, at):
        return (at["x"] * 2 + at["c"]) * self.seq + at["g"] * self.parts + at["q"]

    def flip(self, bits_of_core):
        pairs = []
        for device in range(self.count):
            at = self.place(device)
            axis, bit = bits_of_core[at["c"]]
            at[axis] ^= 1 << bit
            pairs.append((device, self.device(at)))
        return pairs

    def cross(self, by):
        pairs = []
        for device in range(self.count):
            at = self.place(device)
            at["g"] ^= by
            pairs.append((device, self.device(at)))
        return pairs

    def plane_masks(self, core):
        masks = {"x": [], "q": []}
        for index in range(self.xs * self.parts):
            for axis in masks:
                flips = [
                    1 << bit
                    for step, (a, bit) in enumerate(self.plane[core])
                    if a == axis and (index >> step) & 1
                ]
                masks[axis].append(sum(flips))
        return {axis: np.array(m, np.int32) for axis, m in masks.items()}


def same(bits):
    return [(bit, bit) for bit in bits]


def swap(grid, held, bits):
    return lax.ppermute(held, BOTH, grid.flip(bits))


def gather_near(grid, held, bit_pairs):
    for pair in bit_pairs:
        held = jnp.concatenate([held, swap(grid, held, pair)], axis=0)
    return held


def reduce_near(grid, total, bit_pairs):
    for pair in reversed(bit_pairs):
        half = total.shape[0] // 2
        got = swap(grid, total[half:].astype(bf16), pair)
        total = total[:half].astype(f32) + got.astype(f32)
    return total


def line_swap(grid, pieces):
    return [
        lax.ppermute(piece, BOTH, grid.cross(crossed(k + 1))) for k, piece in enumerate(pieces)
    ]


def tie(*values):
    return lax.optimization_barrier(values)


def on_device(
    grid,
    inputs,
    segments,
    rand_blocks,
    glob_blocks,
    w_qkv,
    w_out,
    w_in,
    w_down,
    vec_bias,
    ffn_bias,
    norm_gain,
    norm_shift,
    cotangent,
):
    local_len, width = inputs.shape[1:]
    rows_each, ff_each = w_in.shape[0], w_down.shape[0]
    ff = w_in.shape[1]
    ff_half = ff // 2
    groups, parts, xs = HEAD_GROUPS, grid.parts, grid.xs
    planes = xs * parts
    columns = width // groups
    line_len = groups * local_len
    small_each = ff_each // rows_each
    table_width = -(-(3 * columns + width + 8 + small_each) // 128) * 128
    dp_place, seq_place = lax.axis_index("dp"), lax.axis_index("seq")
    core, group, part = dp_place % 2, seq_place // parts, seq_place % parts
    coords = {"x": dp_place // 2, "c": core, "g": group, "q": part}
    place = jnp.stack([core, group]).astype(jnp.int32)
    chip_swap = lambda a: swap(grid, a, grid.core_bit[0])
    group_order = np.array([0, 2, 1, 3])
    group_slot = lambda g: (g % 2) * 2 + g // 2
    tokens = inputs.reshape(local_len, width)
    cot = cotangent.reshape(local_len, width)
    part_bits = same(grid.part_bits)

    masks = [grid.plane_masks(c) for c in range(2)]
    unit_ids = []
    for c in range(2):
        ids = [
            grid.device({"x": masks[c]["x"][index], "c": c, "g": g, "q": masks[c]["q"][index]})
            for index in range(planes)
            for g in group_order
        ]
        unit_ids.append(np.array(ids))

    far_top = -(-2 * rows_each // 16) * 16
    *packets, own_units, far_pack = call(
        functools.partial(pack_kernel, unit_ids),
        [((rows_each, table_width), bf16)] * groups
        + [((rows_each, ff_half), bf16), ((far_top + 2 * local_len, width), bf16)],
        place,
        w_qkv,
        w_out,
        w_in,
        tokens,
        cot,
        vec_bias,
        ffn_bias.reshape(1, ff_each),
        norm_gain,
        norm_shift,
        name="pack_weights",
        scratch=(),
    )
    got_packets = line_swap(grid, packets[1:])

    plane_x = [coords["x"] ^ jnp.asarray(masks[c]["x"]) for c in range(2)]
    plane_q = [part ^ jnp.asarray(masks[c]["q"]) for c in range(2)]
    line_groups = group ^ jnp.asarray(group_order, jnp.int32)
    row = jnp.arange(rows_each, dtype=jnp.int32)
    row_ids = jnp.arange(width, dtype=jnp.int32)
    by_core = lambda c, pair: jnp.where(c == 0, pair[0], pair[1])

    def device_of(x, c, g, q):
        return (x * 2 + c) * grid.seq + g * parts + q

    near_ids = jnp.stack(
        [
            device_of(by_core(c, plane_x)[:, None], c, line_groups[None, :], by_core(c, plane_q)[:, None])
            for c in (core, 1 - core)
        ]
    )
    line_bits = same(grid.group_bits)
    x_half = gather_near(grid, tokens, line_bits[:1])
    got_pack = chip_swap(far_pack)
    got_units = jnp.concatenate([got_pack[:rows_each], got_pack[rows_each : 2 * rows_each]], axis=1)
    table = jnp.concatenate([packets[0], *got_packets], axis=0)
    units = jnp.concatenate([own_units, got_units], axis=0)[None]
    table, x_half, units, near_ids, line_groups, segments = tie(
        table, x_half, units, near_ids, line_groups, segments
    )
    near_rows = (near_ids[..., None] * rows_each + row).reshape(width)
    to_near = (row_ids[:, None] == near_rows[None, :]).astype(bf16)
    line_rows = jnp.repeat(line_groups, columns) * columns + row_ids % columns
    line_near = (line_rows[:, None] == near_rows[None, :]).astype(bf16)
    group_rows = group * columns + jnp.arange(columns, dtype=jnp.int32)
    near_group = (near_rows[:, None] == group_rows[None, :]).astype(bf16)
    own_x, own_q = by_core(core, plane_x), by_core(core, plane_q)
    slot_groups = jnp.asarray(group_order, jnp.int32)
    piece_ids = jnp.stack(
        [
            device_of(own_x[:, None], c, slot_groups[None, :], own_q[:, None])
            for c in (core, 1 - core)
        ],
        axis=2,
    )
    piece_rows = (piece_ids[..., None] * rows_each + row).reshape(width)
    to_piece = (row_ids[:, None] == piece_rows[None, :]).astype(bf16)
    own_ids = by_core(core, [jnp.asarray(ids, jnp.int32) for ids in unit_ids])
    unit = jnp.arange(ff_half, dtype=jnp.int32)
    unit_rows = jnp.repeat(own_ids, ff_each) * rows_each + (unit % ff_each) // small_each
    near_unit = (near_rows[:, None] == unit_rows[None, :]).astype(bf16)

    flags = [
        by_core(core, [(coords[axis] >> bit) & 1 for axis, bit in pair]) for pair in grid.plane_bits
    ]
    unit_block = ff_half // planes
    aligned = unit_block % 128 == 0
    kernel_flags = len(flags) if aligned else 0
    flag_row = jnp.stack(flags).astype(jnp.int32)
    outer_swap = (lambda a: a) if aligned else (lambda a: swap_blocks(a, flags, unit_block))

    own_blocks = local_len // BLK
    part_near = part ^ jnp.arange(parts, dtype=jnp.int32)
    chunk_ids = (line_groups[None, :] * parts + part_near[:, None]).reshape(-1)
    chunk_hot = chunk_ids[:, None] == jnp.arange(grid.seq, dtype=jnp.int32)[None, :]

    def take_chunks(chunks, hot):
        return jnp.sum(jnp.where(hot[:, :, None], chunks[None], 0), axis=1)

    offsets = jnp.arange(local_len, dtype=jnp.int32) // BLK
    block_near = (chunk_ids[:, None] * own_blocks + offsets[None, :]).reshape(-1)
    seg_near = take_chunks(segments.reshape(grid.seq, local_len), chunk_hot).reshape(-1)
    rand_line = take_chunks(rand_blocks.reshape(grid.seq, -1), chunk_hot[:groups])
    rand_line = rand_line.reshape(groups, own_blocks, 1, -1)
    rand_rows = jnp.broadcast_to(rand_line, (groups, own_blocks, BLK, rand_line.shape[-1]))
    rand_rows = rand_rows.reshape(line_len, -1)
    key_block, key_seg = block_near[None, :], seg_near[None, :]
    query_block, query_seg = block_near[:line_len, None], seg_near[:line_len, None]
    near = (key_block >= query_block - 1) & (key_block <= query_block + 1)
    for entry in range(rand_rows.shape[1]):
        near = near | (key_block == rand_rows[:, entry : entry + 1])
    glob_table = glob_blocks[0]
    doc = jnp.arange(glob_table.shape[0], dtype=jnp.int32)[None, :]
    for entry in range(glob_table.shape[1]):
        picked = jnp.sum(
            jnp.where(query_seg == doc, glob_table[None, :, entry], 0), axis=1, keepdims=True
        )
        near = near | (key_block == picked)
    mask_bias = jnp.where(near & (query_seg == key_seg), 0.0, masked_score).astype(f32)

    steps = len(grid.plane_bits)

    def group_step(held, entry):
        axis, bit = grid.group_bits[entry]
        got = swap(grid, held, ((axis, bit), (axis, bit)))
        upper = (group >> bit) & 1 == 1
        return jnp.where(upper, jnp.concatenate([got, held]), jnp.concatenate([held, got]))

    def plane_gather(held):
        for pair in grid.plane_bits[:-1]:
            held = jnp.concatenate([held, swap(grid, held, pair)], axis=0)
        return held

    x_far_half = swap(grid, x_half, line_bits[1])
    table = gather_near(grid, table, grid.plane_bits[: steps // 2])
    down = group_step(w_down[None], 0)
    table, down, x_far_half, to_near, near_group, mask_bias = tie(
        table, down, x_far_half, to_near, near_group, mask_bias
    )
    x_near = dot(jnp.concatenate([x_half, x_far_half]), to_near).astype(bf16)
    table = gather_near(grid, table, grid.plane_bits[steps // 2 :])
    down = group_step(down, 1)
    units = group_step(units, 0)
    table, down, units, x_near, line_near, near_unit, to_piece = tie(
        table, down, units, x_near, line_near, near_unit, to_piece
    )
    table_far = swap(grid, table, grid.core_bit[0])
    down_near = plane_gather(down.reshape(-1, width))
    units = group_step(units, 1)

    query, own_pairs = call(
        qkv_kernel,
        [((line_len, columns), bf16), ((line_len, 2 * columns), bf16)],
        x_near,
        table,
        table_far,
        near_group,
        name="project",
    )
    own_pairs, units, down_near, table_far = tie(own_pairs, units, down_near, table_far)
    in_near = plane_gather(units.reshape(-1, ff_half))
    down_far = swap(grid, down_near, grid.plane_bits[-1])
    qkv_slice, out_line, params, ffn_row = call(
        functools.partial(unfold_kernel, small_each),
        [
            ((width, 3 * columns), bf16),
            ((width, width), bf16),
            ((8, width), f32),
            ((1, ff_half), f32),
        ],
        table,
        table_far,
        to_near,
        line_near,
        near_unit,
        name="unfold_weights",
    )
    ffn_row = outer_swap(ffn_row)
    kept_pairs, out_line, params, qkv_slice = tie(own_pairs, out_line, params, qkv_slice)
    pairs = jnp.concatenate([kept_pairs, swap(grid, own_pairs, part_bits[0])], axis=0)
    pairs = gather_near(grid, pairs, part_bits[1:])
    pairs, in_near = tie(pairs, in_near)
    in_far = swap(grid, in_near, grid.plane_bits[-1])
    in_near, in_far = outer_swap(in_near), outer_swap(in_far)

    att_pieces, logs = attention_forward(query, pairs, mask_bias)
    got_att = line_swap(grid, att_pieces[1:])
    attended = jnp.concatenate([att_pieces[0], *got_att], axis=1)
    attended_far = chip_swap(attended)

    half = width // 2
    chip_len = 2 * local_len
    weight_scratch = lambda *arrays: [pltpu.VMEM(a.shape, bf16) for a in arrays]
    first, normed, inverse, mixed, hidden, active, part_own, part_send = call(
        functools.partial(ffn_forward_kernel, kernel_flags, unit_block),
        [
            ((chip_len, width), f32),
            ((chip_len, width), f32),
            ((chip_len, 128), f32),
            ((chip_len, width), bf16),
            ((chip_len, ff_half), f32),
            ((chip_len, ff_half), bf16),
            ((chip_len, width), f32),
            ((chip_len, width), bf16),
        ],
        flag_row,
        attended,
        attended_far,
        tokens,
        got_pack,
        params,
        ffn_row,
        out_line,
        to_piece,
        in_near,
        in_far,
        down_near,
        down_far,
        name="ffn_forward",
        in_place=(7, 8, 9, 10, 11, 12),
        scratch=weight_scratch(out_line, to_piece, in_near, in_far, down_near, down_far)
        + [pltpu.SemaphoreType.DMA((6,))],
    )
    part_got = chip_swap(part_send)

    output, first_keep, first_send, d_second, d_hidden, sums_two, ffn_sums = call(
        functools.partial(ffn_backward_kernel, kernel_flags, unit_block),
        [
            ((local_len, width), bf16),
            ((local_len, width), f32),
            ((local_len, width), bf16),
            ((chip_len, width), bf16),
            ((chip_len, ff_half), bf16),
            ((8, width), f32),
            ((1, ff_half), f32),
        ],
        flag_row,
        part_own,
        part_got,
        first,
        cot,
        got_pack,
        hidden,
        params,
        to_piece,
        in_near,
        in_far,
        down_near,
        down_far,
        name="ffn_backward",
        in_place=(8, 9, 10, 11, 12),
        scratch=weight_scratch(to_piece, in_near, in_far, down_near, down_far)
        + [pltpu.SemaphoreType.DMA((5,))],
    )
    first_got = chip_swap(first_send)
    first_got, d_hidden, d_second = tie(first_got, d_hidden, d_second)
    down_send = dot(active[:, width:], d_second, 0, 0).astype(bf16)
    down_keep = dot(active[:, :width], d_second, 0, 0).astype(bf16)
    d_hidden, ffn_sums = outer_swap(d_hidden), outer_swap(ffn_sums)
    in_send = dot(mixed[:, half:], d_hidden, 0, 0).astype(bf16)
    in_keep = dot(mixed[:, :half], d_hidden, 0, 0).astype(bf16)
    d_one, d_branch, sums_one, *d_pieces = call(
        branch_backward_kernel,
        [((local_len, width), f32), ((local_len, width), bf16), ((8, width), f32)]
        + [((local_len, columns), bf16)] * groups,
        first_keep,
        first_got,
        normed[:local_len],
        inverse[:local_len],
        params,
        out_line,
        name="branch_backward",
    )
    got_d_att = line_swap(grid, d_pieces[1:])

    def far_sum(keep, send):
        return keep.astype(f32) + swap(grid, send, grid.plane_bits[-1]).astype(f32)

    down_total = far_sum(down_keep, down_send)
    in_total = far_sum(in_keep, in_send)

    def line_sum(total):
        for axis, bit in reversed(grid.group_bits):
            size = total.shape[0] // 2
            upper = (group >> bit) & 1
            keep = lax.dynamic_slice_in_dim(total, upper * size, size, 0)
            send = lax.dynamic_slice_in_dim(total, (1 - upper) * size, size, 0)
            got = swap(grid, send.astype(bf16), ((axis, bit), (axis, bit)))
            total = keep + got.astype(f32)
        return total

    small_sums = call(
        functools.partial(branch_grads_kernel, small_each),
        [((width // 2, width), f32), ((width // 2, width), bf16), ((width, 16), f32)],
        attended,
        d_branch,
        sums_one,
        sums_two,
        ffn_sums,
        to_near,
        line_near,
        near_unit,
        name="branch_gradients",
    )
    d_pieces[0], *small_sums = tie(d_pieces[0], *small_sums)

    d_query, pairs_own, pairs_send = attention_backward(
        query, pairs, mask_bias, [d_pieces[0], *got_d_att], logs
    )
    pairs_own, down_total, in_total = tie(pairs_own, down_total, in_total)
    down_total = reduce_near(grid, down_total, grid.plane_bits[:-1])
    in_total = reduce_near(grid, in_total, grid.plane_bits[:-1])
    if parts == 2:
        pairs_got = swap(grid, pairs_send, part_bits[0])
    else:
        pairs_all = jnp.concatenate([pairs_own, pairs_send.astype(f32)])
        pairs_own = reduce_near(grid, pairs_all, part_bits)
        pairs_got = jnp.zeros(pairs_own.shape, bf16)
    query_grads = call(
        query_grads_kernel,
        [((width, columns), f32), ((width, 8), f32), ((line_len, width), f32)],
        x_near,
        d_query,
        near_group,
        qkv_slice,
        name="query_gradients",
    )
    grad_keep, grad_send, back_keep, back_send = call(
        pair_grads_kernel,
        [
            ((width // 2, table_width), f32),
            ((width // 2, table_width), bf16),
            ((line_len // 2, width), f32),
            ((line_len // 2, width), bf16),
        ],
        x_near,
        pairs_own,
        pairs_got,
        near_group,
        qkv_slice,
        *small_sums,
        *query_grads,
        name="pair_gradients",
    )
    grad_send, down_total, in_total = tie(grad_send, down_total, in_total)
    sum_down = line_sum(down_total)
    in_pairs = line_sum(in_total)
    back = back_keep + swap(grid, back_send, line_bits[1]).astype(f32)
    back = reduce_near(grid, back, line_bits[:1])
    total = grad_keep + chip_swap(grad_send).astype(f32)
    total = reduce_near(grid, total, grid.plane_bits)
    total, in_pairs, d_one = tie(total, in_pairs, d_one)
    in_got = chip_swap(in_pairs[rows_each:])
    (sum_in,) = call(
        functools.partial(units_kernel, unit_ids),
        [((rows_each, ff), f32)],
        place,
        in_pairs[:rows_each],
        in_got,
        name="order_units",
    )

    got_total = line_swap(
        grid, [total[k * rows_each : (k + 1) * rows_each].astype(bf16) for k in range(1, groups)]
    )
    input_grad = d_one + back
    sum_qkv, sum_out, sum_vec, sum_ffn, sum_gain, sum_shift = call(
        functools.partial(finish_kernel, small_each),
        [
            ((rows_each, 3 * width), f32),
            ((rows_each, width), f32),
            ((4, rows_each), f32),
            ((1, ff_each), f32),
            ((2, rows_each), f32),
            ((2, rows_each), f32),
        ],
        place,
        total[:rows_each],
        *got_total,
        name="finish",
    )
    return (
        output[None],
        input_grad[None],
        sum_qkv,
        sum_out,
        sum_in,
        sum_down,
        sum_vec,
        sum_ffn.reshape(ff_each),
        sum_gain,
        sum_shift,
    )


def solution(mesh):
    return jax.shard_map(
        functools.partial(on_device, Grid(mesh)),
        mesh=mesh,
        in_specs=(
            P("dp", "seq", None),
            P("dp", None),
            P("dp", None, None),
            P("dp", None, None),
            P(("dp", "seq"), None),
            P(("dp", "seq"), None),
            P(("dp", "seq"), None),
            P(("dp", "seq"), None),
            P(None, ("dp", "seq")),
            P(("dp", "seq")),
            P(None, ("dp", "seq")),
            P(None, ("dp", "seq")),
            P("dp", "seq", None),
        ),
        out_specs=(
            P("dp", "seq", None),
            P("dp", "seq", None),
            P(("dp", "seq"), None),
            P(("dp", "seq"), None),
            P(("dp", "seq"), None),
            P(("dp", "seq"), None),
            P(None, ("dp", "seq")),
            P(("dp", "seq")),
            P(None, ("dp", "seq")),
            P(None, ("dp", "seq")),
        ),
        check_vma=False,
    )
```

```python
import functools

import jax
import jax.numpy as jnp
import numpy as np
from jax import lax
from jax.experimental import pallas as pl
from jax.experimental.pallas import tpu as pltpu
from jax.sharding import PartitionSpec as P

HD = 64
BLK = 64
HEAD_GROUPS = 4
SCORE_CELLS = 512 * 1024

norm_eps = 1e-05
masked_score = -1e30
BOTH = ("dp", "seq")
bf16 = jnp.bfloat16
f32 = jnp.float32


def normalize(field_in):
    mean_row = jnp.mean(field_in, axis=-1, keepdims=True)
    centred = field_in - mean_row
    inverse = lax.rsqrt(jnp.mean(centred * centred, axis=-1, keepdims=True) + norm_eps)
    return (centred * inverse, inverse)


def norm_back(grad_in, normed, inverse, gain_row):
    weighted = grad_in * gain_row
    inner = jnp.mean(weighted * normed, axis=-1, keepdims=True)
    return inverse * (weighted - jnp.mean(weighted, axis=-1, keepdims=True) - normed * inner)


def gelu_slope(field_in):
    return (
        0.5 * (1.0 + lax.erf(field_in * 0.7071067811865476))
        + field_in * jnp.exp(-0.5 * field_in * field_in) * 0.3989422804014327
    )


def dot(left, right, left_dim=1, right_dim=0):
    return lax.dot_general(
        left, right, (((left_dim,), (right_dim,)), ((), ())), preferred_element_type=f32
    )


def call(body, outs, *args, name, scratch=(), flops=1e8, in_place=()):
    space = lambda i, a: (
        pl.ANY if i in in_place else pltpu.SMEM if a.dtype == jnp.int32 else pltpu.VMEM
    )
    specs = [pl.BlockSpec(memory_space=space(i, a)) for i, a in enumerate(args)]
    moved = sum(int(np.prod(a.shape)) * a.dtype.itemsize for a in args)
    return pl.pallas_call(
        body,
        in_specs=specs,
        out_specs=[pl.BlockSpec(memory_space=pltpu.VMEM)] * len(outs),
        out_shape=[jax.ShapeDtypeStruct(shape, dtype) for shape, dtype in outs],
        scratch_shapes=list(scratch),
        compiler_params=pltpu.CompilerParams(vmem_limit_bytes=56 * 1024 * 1024),
        cost_estimate=pl.CostEstimate(flops=int(flops), bytes_accessed=moved, transcendentals=0),
        name=name,
    )(*args)


def copies(pairs, sems):
    started = []
    for i, (source, target) in enumerate(pairs):
        copy = pltpu.make_async_copy(source, target, sems.at[i])
        copy.start()
        started.append(copy)
    return started


def exact(left, right, left_dim=1, right_dim=0):
    return lax.dot_general(
        left,
        right,
        (((left_dim,), (right_dim,)), ((), ())),
        preferred_element_type=f32,
        precision=lax.Precision.HIGHEST,
    )


def iota(shape, dim):
    return lax.broadcasted_iota(jnp.int32, shape, dim)


def spread_rows(row, rows, each):
    lanes = row.shape[1]
    picked = jnp.where(iota((rows, lanes), 1) // each == iota((rows, lanes), 0), row, 0.0)
    select = (iota((lanes, each), 0) % each == iota((lanes, each), 1)).astype(f32)
    return exact(picked, select)


def pick(options, index):
    chosen = options[0]
    for i, option in enumerate(options[1:]):
        chosen = jnp.where(index == i + 1, option, chosen)
    return chosen


def crossed(number):
    return (number % 2) * 2 + number // 2


def pack_kernel(
    unit_ids,
    place_ref,
    qkv_ref,
    out_ref,
    in_ref,
    x_ref,
    cot_ref,
    vec_ref,
    ffn_ref,
    gain_ref,
    shift_ref,
    *outs,
):
    core, group = place_ref[0], place_ref[1]
    rows, width = out_ref.shape
    columns = width // HEAD_GROUPS
    rolled = lambda g: [
        qkv_ref[:, kind * width + g * columns : kind * width + (g + 1) * columns] for kind in (1, 2, 0)
    ]
    by_group = [jnp.concatenate(rolled(g), axis=1) for g in range(HEAD_GROUPS)]
    same_row = (iota((rows, rows), 0) == iota((rows, rows), 1)).astype(bf16)
    turned = [dot(same_row, ref[...], 1, 1) for ref in (vec_ref, gain_ref, shift_ref)]
    turned.append(spread_rows(ffn_ref[...].astype(f32), rows, ffn_ref.shape[1] // rows))
    small = jnp.concatenate(turned, axis=1).astype(bf16)
    for k in range(HEAD_GROUPS):
        chosen = pick(by_group, group ^ crossed(k))
        rest = outs[k].shape[1] - 3 * columns - width - small.shape[1]
        outs[k][:, : 2 * columns] = chosen[:, : 2 * columns]
        outs[k][:, 2 * columns : 2 * columns + width] = out_ref[...]
        outs[k][:, 2 * columns + width :] = jnp.concatenate(
            [chosen[:, 2 * columns :], small, jnp.zeros((rows, rest), bf16)], axis=1
        )
    each = ffn_ref.shape[1]
    units = [
        jnp.concatenate([in_ref[:, i * each : (i + 1) * each] for i in ids], axis=1) for ids in unit_ids
    ]
    outs[HEAD_GROUPS][...] = jnp.where(core == 0, units[0], units[1])
    far = jnp.where(core == 0, units[1], units[0])
    far_ref = outs[HEAD_GROUPS + 1]
    tokens = x_ref.shape[0]
    top = far_ref.shape[0] - 2 * tokens
    blank = jnp.zeros((top - 2 * rows, width), bf16)
    far_ref[:top] = jnp.concatenate([far[:, :width], far[:, width:], blank][: 3 if top > 2 * rows else 2])
    far_ref[top : top + tokens] = x_ref[...]
    far_ref[top + tokens :] = cot_ref[...]


def unfold_kernel(
    small_each, table_ref, far_ref, near_ref, line_ref, unit_ref, qkv_ref, out_ref, par_ref, ffn_ref
):
    columns = qkv_ref.shape[1] // 3
    width = out_ref.shape[1]
    start, at = 2 * columns, 2 * columns + width
    near = near_ref[...]
    both = lambda i, j: jnp.concatenate([table_ref[:, i:j], far_ref[:, i:j]], axis=0)
    rest = both(at, table_ref.shape[1])
    qkv_ref[:, :start] = dot(near, both(0, start)).astype(bf16)
    qkv_ref[:, start:] = dot(near, rest[:, :columns]).astype(bf16)
    out_ref[...] = dot(line_ref[...], both(start, at)).astype(bf16)
    small = rest[:, columns : columns + 8 + small_each]
    par_ref[...] = dot(small[:, :8], near, 0, 1)
    by_slot = dot(small[:, 8:], unit_ref[...], 0, 0)
    slot = iota(by_slot.shape, 1) % small_each == iota(by_slot.shape, 0)
    ffn_ref[...] = jnp.sum(jnp.where(slot, by_slot, 0.0), axis=0, keepdims=True)


def qkv_kernel(x_ref, table_ref, far_ref, sel_ref, q_ref, pair_ref):
    columns = q_ref.shape[1]
    width = x_ref.shape[1]
    half = width // 2
    start, at = 2 * columns, 2 * columns + width
    pairs = dot(x_ref[:, :half], table_ref[:, :start]) + dot(x_ref[:, half:], far_ref[:, :start])
    rest = jnp.concatenate([table_ref[:, at:], far_ref[:, at:]], axis=0)
    biases = dot(rest[:, columns : columns + 8], sel_ref[...], 0, 0)
    values = pairs[:, columns:] + biases[1:2]
    pair_ref[...] = jnp.concatenate([pairs[:, :columns], values], axis=1).astype(bf16)
    queries = dot(x_ref[...], rest[:, :columns]) + biases[0:1]
    q_ref[...] = (queries * HD ** (-0.5)).astype(bf16)


def head_mask(shape, head):
    lane = iota(shape, 1)
    return (lane >= head * HD) & (lane < (head + 1) * HD)


def split_pairs(pair_ref, k_ref, v_ref):
    width = k_ref.shape[1]
    k_ref[...] = pair_ref[:, :width]
    v_ref[...] = pair_ref[:, width:]


def forward_kernel(q_ref, kv_ref, b_ref, *refs):
    *o_refs, l_ref, k_ref, v_ref = refs
    step = pl.program_id(0)

    @pl.when(step == 0)
    def _():
        split_pairs(kv_ref, k_ref, v_ref)

    query, keys, values, bias = q_ref[...], k_ref[...], v_ref[...], b_ref[...]
    rows, width = query.shape
    out = jnp.zeros(query.shape, f32)
    logs = jnp.zeros(l_ref.shape, f32)
    for head in range(width // HD):
        mine = head_mask(query.shape, head)
        scores = dot(jnp.where(mine, query, jnp.zeros_like(query)), keys, 1, 1) + bias
        top = jnp.max(scores, axis=1, keepdims=True)
        terms = jnp.exp(scores - top)
        total = jnp.sum(terms, axis=1, keepdims=True)
        probs = (terms * (1.0 / total)).astype(bf16)
        out = out + jnp.where(mine, dot(probs, values), 0.0)
        logs = jnp.where(iota(l_ref.shape, 1) == head, top + jnp.log(total), logs)
    l_ref[...] = logs
    low = out.astype(bf16)
    piece = o_refs[0].shape[0]
    each = rows // piece
    for k, o_ref in enumerate(o_refs):
        start = (k % each) * piece

        @pl.when(step == k // each)
        def _(o_ref=o_ref, start=start):
            o_ref[...] = low[start : start + piece]


def backward_kernel(q_ref, kv_ref, b_ref, *refs):
    pieces, refs = refs[:HEAD_GROUPS], refs[HEAD_GROUPS:]
    l_ref, dq_ref, own_ref, send_ref, k_ref, v_ref, d_ref, dk_ref, dv_ref = refs
    step = pl.program_id(0)
    rows, width = q_ref.shape

    @pl.when(step == 0)
    def _():
        split_pairs(kv_ref, k_ref, v_ref)
        dk_ref[...] = jnp.zeros(dk_ref.shape, f32)
        dv_ref[...] = jnp.zeros(dv_ref.shape, f32)
        piece = pieces[0].shape[0]
        for k, ref in enumerate(pieces):
            d_ref[k * piece : (k + 1) * piece] = ref[...]

    query, keys, values, bias = q_ref[...], k_ref[...], v_ref[...], b_ref[...]
    d_att = d_ref[pl.ds(pl.multiple_of(step * rows, rows), rows)]
    logs = l_ref[...]
    d_query = jnp.zeros(query.shape, f32)
    for head in range(width // HD):
        mine = head_mask(query.shape, head)
        q_head = jnp.where(mine, query, jnp.zeros_like(query))
        d_head = jnp.where(mine, d_att, jnp.zeros_like(d_att))
        scores = dot(q_head, keys, 1, 1) + bias
        weights = jnp.exp(scores - logs[:, head : head + 1])
        d_probs = dot(d_head, values, 1, 1)
        delta = jnp.sum(weights * d_probs, axis=1, keepdims=True)
        d_scores = (weights * (d_probs - delta)).astype(bf16)
        d_query = d_query + jnp.where(mine, dot(d_scores, keys), 0.0)
        dk_ref[...] += dot(d_scores, q_head, 0, 0)
        dv_ref[...] += dot(weights.astype(bf16), d_head, 0, 0)
    dq_ref[...] = (d_query * HD ** (-0.5)).astype(bf16)

    @pl.when(step == pl.num_programs(0) - 1)
    def _():
        kept = own_ref.shape[0]
        own_ref[:, :width] = dk_ref[:kept]
        own_ref[:, width:] = dv_ref[:kept]
        send_ref[:, :width] = dk_ref[kept:].astype(bf16)
        send_ref[:, width:] = dv_ref[kept:].astype(bf16)


def attention_forward(query, pairs, bias):
    rows, width = query.shape
    key_rows = pairs.shape[0]
    tile = min(rows, SCORE_CELLS // key_rows)
    piece = rows // HEAD_GROUPS
    results = pl.pallas_call(
        forward_kernel,
        grid=(rows // tile,),
        in_specs=[
            pl.BlockSpec((tile, width), lambda i: (i, 0)),
            pl.BlockSpec((key_rows, 2 * width), lambda i: (0, 0)),
            pl.BlockSpec((tile, key_rows), lambda i: (i, 0)),
        ],
        out_specs=[pl.BlockSpec((piece, width), lambda i: (0, 0))] * HEAD_GROUPS
        + [pl.BlockSpec((tile, 128), lambda i: (i, 0))],
        out_shape=[jax.ShapeDtypeStruct((piece, width), bf16)] * HEAD_GROUPS
        + [jax.ShapeDtypeStruct((rows, 128), f32)],
        scratch_shapes=[pltpu.VMEM((key_rows, width), bf16)] * 2,
        compiler_params=pltpu.CompilerParams(vmem_limit_bytes=56 * 1024 * 1024),
        cost_estimate=pl.CostEstimate(
            flops=16 * rows * key_rows * width, bytes_accessed=4 * rows * key_rows, transcendentals=0
        ),
        name="attention_forward",
    )(query, pairs, bias)
    return results[:-1], results[-1]


def attention_backward(query, pairs, bias, d_pieces, logs):
    rows, width = query.shape
    key_rows = pairs.shape[0]
    tile = min(rows, SCORE_CELLS // key_rows)
    fixed = lambda n: pl.BlockSpec((n, 2 * width), lambda i: (0, 0))
    return pl.pallas_call(
        backward_kernel,
        grid=(rows // tile,),
        in_specs=[
            pl.BlockSpec((tile, width), lambda i: (i, 0)),
            fixed(key_rows),
            pl.BlockSpec((tile, key_rows), lambda i: (i, 0)),
        ]
        + [pl.BlockSpec(d_pieces[0].shape, lambda i: (0, 0))] * HEAD_GROUPS
        + [pl.BlockSpec((tile, 128), lambda i: (i, 0))],
        out_specs=[
            pl.BlockSpec((tile, width), lambda i: (i, 0)),
            fixed(rows),
            fixed(key_rows - rows),
        ],
        out_shape=[
            jax.ShapeDtypeStruct((rows, width), bf16),
            jax.ShapeDtypeStruct((rows, 2 * width), f32),
            jax.ShapeDtypeStruct((key_rows - rows, 2 * width), bf16),
        ],
        scratch_shapes=[pltpu.VMEM((key_rows, width), bf16)] * 2
        + [pltpu.VMEM((rows, width), bf16)]
        + [pltpu.VMEM((key_rows, width), f32)] * 2,
        compiler_params=pltpu.CompilerParams(vmem_limit_bytes=56 * 1024 * 1024),
        cost_estimate=pl.CostEstimate(
            flops=30 * rows * key_rows * width, bytes_accessed=4 * rows * key_rows, transcendentals=0
        ),
        name="attention_backward",
    )(query, pairs, bias, *d_pieces, logs)


def swap_blocks(a, flags, block):
    for step, flag in enumerate(flags):
        size = block << step
        blocks = [a[:, i : i + size] for i in range(0, a.shape[1], size)]
        flipped = [blocks[i ^ 1] for i in range(len(blocks))]
        a = jnp.where(flag == 1, jnp.concatenate(flipped, axis=1), a)
    return a


def ffn_forward_kernel(
    flag_count,
    block,
    flag_ref,
    att_ref,
    att_far_ref,
    x_ref,
    far_ref,
    par_ref,
    ffn_ref,
    out_hbm,
    mix_hbm,
    in_near_hbm,
    in_far_hbm,
    down_near_hbm,
    down_far_hbm,
    first_ref,
    normed_ref,
    inverse_ref,
    mixed_ref,
    hidden_ref,
    active_ref,
    part_ref,
    send_ref,
    out_ref,
    mix_ref,
    in_near_ref,
    in_far_ref,
    down_near_ref,
    down_far_ref,
    sems,
):
    waits = copies(
        [
            (out_hbm, out_ref),
            (mix_hbm, mix_ref),
            (in_near_hbm, in_near_ref),
            (in_far_hbm, in_far_ref),
            (down_near_hbm, down_near_ref),
            (down_far_hbm, down_far_ref),
        ],
        sems,
    )
    flags = [flag_ref[i] for i in range(flag_count)]
    attended = jnp.concatenate([att_ref[...], att_far_ref[...]], axis=0)
    rows = x_ref.shape[0]
    top = far_ref.shape[0] - 2 * rows
    tokens = jnp.concatenate([x_ref[...], far_ref[top : top + rows]], axis=0).astype(f32)
    waits[0].wait()
    branch = dot(attended, out_ref[...]) + par_ref[2:3]
    normed, inverse = normalize(tokens + branch)
    first = normed * par_ref[4:5] + par_ref[6:7]
    first_ref[...] = first
    normed_ref[...] = normed
    inverse_ref[...] = jnp.broadcast_to(inverse, inverse_ref.shape)
    waits[1].wait()
    mixed = dot(first.astype(bf16), mix_ref[...]).astype(bf16)
    mixed_ref[...] = mixed
    half = mixed.shape[1] // 2
    waits[2].wait()
    hidden = dot(mixed[:, :half], in_near_ref[...])
    waits[3].wait()
    hidden = hidden + dot(mixed[:, half:], in_far_ref[...]) + ffn_ref[...]
    hidden = swap_blocks(hidden, flags, block)
    hidden_ref[...] = hidden
    active = (0.5 * hidden * (1.0 + lax.erf(hidden * 0.7071067811865476))).astype(bf16)
    active_ref[...] = active
    units = active.shape[1] // 2
    waits[4].wait()
    part = dot(active[:, :units], down_near_ref[...])
    waits[5].wait()
    part = part + dot(active[:, units:], down_far_ref[...])
    part_ref[...] = part
    send_ref[...] = part.astype(bf16)


def column_sum(a):
    return jnp.sum(a, axis=0, keepdims=True)


def ffn_backward_kernel(
    flag_count,
    block,
    flag_ref,
    part_ref,
    got_ref,
    first_ref,
    cot_ref,
    far_ref,
    hidden_ref,
    par_ref,
    mix_hbm,
    in_near_hbm,
    in_far_hbm,
    down_near_hbm,
    down_far_hbm,
    output_ref,
    keep_ref,
    send_ref,
    second_ref,
    d_hidden_ref,
    sums_ref,
    ffn_sum_ref,
    mix_ref,
    in_near_ref,
    in_far_ref,
    down_near_ref,
    down_far_ref,
    sems,
):
    waits = copies(
        [
            (down_near_hbm, down_near_ref),
            (down_far_hbm, down_far_ref),
            (in_near_hbm, in_near_ref),
            (in_far_hbm, in_far_ref),
            (mix_hbm, mix_ref),
        ],
        sems,
    )
    flags = [flag_ref[i] for i in range(flag_count)]
    rows = got_ref.shape[0] // 2
    other = jnp.concatenate([got_ref[rows:], got_ref[:rows]], axis=0).astype(f32)
    normed, inverse = normalize(first_ref[...] + part_ref[...] + other + par_ref[3:4])
    gain = par_ref[5:6]
    output_ref[...] = (normed[:rows] * gain + par_ref[7:8]).astype(bf16)
    out_grad = jnp.concatenate([cot_ref[...], far_ref[far_ref.shape[0] - rows :]], axis=0).astype(f32)
    d_two = norm_back(out_grad, normed, inverse, gain)
    d_second = d_two.astype(bf16)
    second_ref[...] = d_second
    sums_ref[...] = jnp.concatenate(
        [
            column_sum(out_grad[:rows] * normed[:rows]),
            column_sum(out_grad[:rows]),
            column_sum(d_second[:rows].astype(f32)),
            jnp.zeros((5, normed.shape[1]), f32),
        ],
        axis=0,
    )
    waits[0].wait()
    near = dot(d_second, down_near_ref[...], 1, 1)
    waits[1].wait()
    far = dot(d_second, down_far_ref[...], 1, 1)
    slope = gelu_slope(hidden_ref[...])
    d_hidden = jnp.concatenate([near, far], axis=1) * slope
    d_hidden = swap_blocks(d_hidden, flags, block).astype(bf16)
    d_hidden_ref[...] = d_hidden
    ffn_sum_ref[...] = column_sum(d_hidden.astype(f32))
    waits[2].wait()
    near = dot(d_hidden, in_near_ref[...], 1, 1).astype(bf16)
    waits[3].wait()
    far = dot(d_hidden, in_far_ref[...], 1, 1).astype(bf16)
    waits[4].wait()
    part = dot(jnp.concatenate([near, far], axis=1), mix_ref[...], 1, 1)
    keep_ref[...] = d_two[:rows] + part[:rows]
    send_ref[...] = part[rows:].astype(bf16)


def branch_backward_kernel(
    keep_ref, got_ref, normed_ref, inverse_ref, par_ref, out_ref, d_one_ref, branch_ref, sums_ref, *pieces
):
    d_first = keep_ref[...] + got_ref[...].astype(f32)
    normed, inverse = normed_ref[...], inverse_ref[:, :1]
    d_one = norm_back(d_first, normed, inverse, par_ref[4:5])
    d_one_ref[...] = d_one
    d_branch = d_one.astype(bf16)
    branch_ref[...] = d_branch
    sums_ref[...] = jnp.concatenate(
        [
            column_sum(d_first * normed),
            column_sum(d_first),
            column_sum(d_branch.astype(f32)),
            jnp.zeros((5, normed.shape[1]), f32),
        ],
        axis=0,
    )
    d_attended = dot(d_branch, out_ref[...], 1, 1).astype(bf16)
    columns = pieces[0].shape[1]
    for k, piece in enumerate(pieces):
        piece[...] = d_attended[:, k * columns : (k + 1) * columns]


def branch_grads_kernel(
    small_each,
    att_ref,
    branch_ref,
    sums_ref,
    sums_two_ref,
    ffn_ref,
    near_ref,
    line_ref,
    unit_ref,
    keep_ref,
    send_ref,
    small_ref,
):
    attended = dot(att_ref[...], line_ref[...]).astype(bf16)
    outs = dot(attended, branch_ref[...], 0, 0)
    half = outs.shape[0] // 2
    keep_ref[...] = outs[:half]
    send_ref[...] = outs[half:].astype(bf16)
    first, second = sums_ref[...], sums_two_ref[...]
    blank = jnp.zeros((2, first.shape[1]), f32)
    vectors = jnp.concatenate(
        [blank, first[2:3], second[2:3], first[0:1], second[0:1], first[1:2], second[1:2]], axis=0
    )
    vectors = dot(near_ref[...], vectors.astype(bf16), 0, 1)
    units = ffn_ref.shape[1]
    slot = iota((8, units), 1) % small_each == iota((8, units), 0)
    by_slot = jnp.where(slot, ffn_ref[...], 0.0).astype(bf16)
    ffn = dot(unit_ref[...], by_slot, 1, 1)
    small_ref[...] = jnp.concatenate([vectors, ffn], axis=1)


def query_grads_kernel(x_ref, dq_ref, sel_ref, qkv_ref, grad_ref, bias_ref, back_ref):
    columns = dq_ref.shape[1]
    d_query = dq_ref[...]
    back_ref[...] = dot(d_query, qkv_ref[:, 2 * columns :], 1, 1)
    grad_ref[...] = dot(x_ref[...], d_query, 0, 0)
    sums = jnp.concatenate([column_sum(d_query.astype(f32)), jnp.zeros((7, columns), f32)], axis=0)
    bias_ref[...] = dot(sel_ref[...], sums.astype(bf16), 1, 1)


def pair_grads_kernel(
    x_ref,
    own_ref,
    got_ref,
    sel_ref,
    qkv_ref,
    out_ref,
    out_send_ref,
    small_ref,
    query_ref,
    bias_ref,
    query_back_ref,
    keep_ref,
    send_ref,
    back_ref,
    back_send_ref,
):
    pair_columns = own_ref.shape[1]
    columns = pair_columns // 2
    width = x_ref.shape[1]
    d_pairs = (own_ref[...] + got_ref[...].astype(f32)).astype(bf16)
    grad_back = query_back_ref[...] + dot(d_pairs, qkv_ref[:, :pair_columns], 1, 1)
    rows = back_ref.shape[0]
    back_ref[...] = grad_back[:rows]
    back_send_ref[...] = grad_back[rows:].astype(bf16)
    pairs = dot(x_ref[...], d_pairs, 0, 0)
    sums = [jnp.zeros((1, columns), f32), column_sum(d_pairs[:, columns:].astype(f32))]
    sums = jnp.concatenate([*sums, jnp.zeros((6, columns), f32)], axis=0)
    bias = dot(sel_ref[...], sums.astype(bf16), 1, 1)
    small = small_ref[...]
    vectors = small[:, :8] + bias + bias_ref[...]
    at = pair_columns + width
    rest = keep_ref.shape[1] - at - columns - 16
    last = [query_ref[...], vectors, small[:, 8:], jnp.zeros((width, rest), f32)]
    last = jnp.concatenate(last, axis=1)
    half = width // 2
    keep_ref[:, :pair_columns] = pairs[:half]
    keep_ref[:, pair_columns:at] = out_ref[...]
    keep_ref[:, at:] = last[:half]
    send_ref[:, :pair_columns] = pairs[half:].astype(bf16)
    send_ref[:, pair_columns:at] = out_send_ref[...]
    send_ref[:, at:] = last[half:].astype(bf16)


def finish_kernel(small_each, place_ref, own_ref, *refs):
    pieces, outs = refs[: HEAD_GROUPS - 1], refs[HEAD_GROUPS - 1 :]
    qkv_ref, out_ref, vec_ref, ffn_ref, gain_ref, shift_ref = outs
    group = place_ref[1]
    rows, width = out_ref.shape
    columns = width // HEAD_GROUPS
    line = [own_ref[...]] + [piece[...].astype(f32) for piece in pieces]
    at = 2 * columns + width
    for g in range(HEAD_GROUPS):
        source = crossed(group ^ g)
        pairs = pick([a[:, : 2 * columns] for a in line], source)
        queries = pick([a[:, at : at + columns] for a in line], source)
        for kind, mine in enumerate((queries, pairs[:, :columns], pairs[:, columns:])):
            start = kind * width + g * columns
            qkv_ref[:, start : start + columns] = mine
    out_ref[...] = sum(a[:, 2 * columns : at] for a in line)
    rest = sum(a[:, at:] for a in line)
    small = rest[:, columns : columns + 8 + small_each]
    same_row = (iota((rows, rows), 0) == iota((rows, rows), 1)).astype(f32)
    turned = exact(small[:, :8], same_row, 0, 0)
    vec_ref[...] = turned[:4]
    gain_ref[...] = turned[4:6]
    shift_ref[...] = turned[6:8]
    each = small.shape[1] - 8
    lanes = rows * each
    select = (iota((each, lanes), 1) % each == iota((each, lanes), 0)).astype(f32)
    wide = exact(small[:, 8:], select)
    mine = iota((rows, lanes), 1) // each == iota((rows, lanes), 0)
    ffn_ref[...] = column_sum(jnp.where(mine, wide, 0.0))


def units_kernel(unit_ids, place_ref, keep_ref, got_ref, out_ref):
    core = place_ref[0]
    keep, got = keep_ref[...], got_ref[...].astype(f32)
    sources = [jnp.where(core == 0, keep, got), jnp.where(core == 0, got, keep)]
    count = 2 * len(unit_ids[0])
    each = out_ref.shape[1] // count
    blocks = {}
    for c, ids in enumerate(unit_ids):
        for slot, device in enumerate(ids):
            blocks[int(device)] = sources[c][:, slot * each : (slot + 1) * each]
    out_ref[...] = jnp.concatenate([blocks[i] for i in range(count)], axis=1)


class Grid:
    def __init__(self, mesh):
        self.dp, self.seq = mesh.shape["dp"], mesh.shape["seq"]
        self.count = self.dp * self.seq
        self.xs, self.parts = self.dp // 2, self.seq // HEAD_GROUPS
        bits = lambda axis, size: [(axis, b) for b in range(size.bit_length() - 1)]
        x_bits, self.part_bits = bits("x", self.xs), bits("q", self.parts)
        self.group_bits = [("g", 1), ("g", 0)]
        alternate = len(x_bits) == len(self.part_bits)
        self.plane = (
            x_bits + self.part_bits,
            self.part_bits + x_bits if alternate else x_bits + self.part_bits,
        )
        self.core_bit = [(("c", 0), ("c", 0))]
        self.plane_bits = list(zip(*self.plane))

    def place(self, device):
        dp, seq = divmod(device, self.seq)
        return {"x": dp // 2, "c": dp % 2, "g": seq // self.parts, "q": seq % self.parts}

    def device(self, at):
        return (at["x"] * 2 + at["c"]) * self.seq + at["g"] * self.parts + at["q"]

    def flip(self, bits_of_core):
        pairs = []
        for device in range(self.count):
            at = self.place(device)
            axis, bit = bits_of_core[at["c"]]
            at[axis] ^= 1 << bit
            pairs.append((device, self.device(at)))
        return pairs

    def cross(self, by):
        pairs = []
        for device in range(self.count):
            at = self.place(device)
            at["g"] ^= by
            pairs.append((device, self.device(at)))
        return pairs

    def plane_masks(self, core):
        masks = {"x": [], "q": []}
        for index in range(self.xs * self.parts):
            for axis in masks:
                flips = [
                    1 << bit
                    for step, (a, bit) in enumerate(self.plane[core])
                    if a == axis and (index >> step) & 1
                ]
                masks[axis].append(sum(flips))
        return {axis: np.array(m, np.int32) for axis, m in masks.items()}


def same(bits):
    return [(bit, bit) for bit in bits]


def swap(grid, held, bits):
    return lax.ppermute(held, BOTH, grid.flip(bits))


def gather_near(grid, held, bit_pairs):
    for pair in bit_pairs:
        held = jnp.concatenate([held, swap(grid, held, pair)], axis=0)
    return held


def reduce_near(grid, total, bit_pairs):
    for pair in reversed(bit_pairs):
        half = total.shape[0] // 2
        got = swap(grid, total[half:].astype(bf16), pair)
        total = total[:half].astype(f32) + got.astype(f32)
    return total


def line_swap(grid, pieces):
    return [
        lax.ppermute(piece, BOTH, grid.cross(crossed(k + 1))) for k, piece in enumerate(pieces)
    ]


def tie(*values):
    return lax.optimization_barrier(values)


def on_device(
    grid,
    inputs,
    segments,
    rand_blocks,
    glob_blocks,
    w_qkv,
    w_out,
    w_in,
    w_down,
    vec_bias,
    ffn_bias,
    norm_gain,
    norm_shift,
    cotangent,
):
    local_len, width = inputs.shape[1:]
    rows_each, ff_each = w_in.shape[0], w_down.shape[0]
    ff = w_in.shape[1]
    ff_half = ff // 2
    groups, parts, xs = HEAD_GROUPS, grid.parts, grid.xs
    planes = xs * parts
    columns = width // groups
    line_len = groups * local_len
    small_each = ff_each // rows_each
    table_width = -(-(3 * columns + width + 8 + small_each) // 128) * 128
    dp_place, seq_place = lax.axis_index("dp"), lax.axis_index("seq")
    core, group, part = dp_place % 2, seq_place // parts, seq_place % parts
    coords = {"x": dp_place // 2, "c": core, "g": group, "q": part}
    place = jnp.stack([core, group]).astype(jnp.int32)
    chip_swap = lambda a: swap(grid, a, grid.core_bit[0])
    group_order = np.array([0, 2, 1, 3])
    group_slot = lambda g: (g % 2) * 2 + g // 2
    tokens = inputs.reshape(local_len, width)
    cot = cotangent.reshape(local_len, width)
    part_bits = same(grid.part_bits)

    masks = [grid.plane_masks(c) for c in range(2)]
    unit_ids = []
    for c in range(2):
        ids = [
            grid.device({"x": masks[c]["x"][index], "c": c, "g": g, "q": masks[c]["q"][index]})
            for index in range(planes)
            for g in group_order
        ]
        unit_ids.append(np.array(ids))

    far_top = -(-2 * rows_each // 16) * 16
    *packets, own_units, far_pack = call(
        functools.partial(pack_kernel, unit_ids),
        [((rows_each, table_width), bf16)] * groups
        + [((rows_each, ff_half), bf16), ((far_top + 2 * local_len, width), bf16)],
        place,
        w_qkv,
        w_out,
        w_in,
        tokens,
        cot,
        vec_bias,
        ffn_bias.reshape(1, ff_each),
        norm_gain,
        norm_shift,
        name="pack_weights",
        scratch=(),
    )
    got_packets = line_swap(grid, packets[1:])

    plane_x = [coords["x"] ^ jnp.asarray(masks[c]["x"]) for c in range(2)]
    plane_q = [part ^ jnp.asarray(masks[c]["q"]) for c in range(2)]
    line_groups = group ^ jnp.asarray(group_order, jnp.int32)
    row = jnp.arange(rows_each, dtype=jnp.int32)
    row_ids = jnp.arange(width, dtype=jnp.int32)
    by_core = lambda c, pair: jnp.where(c == 0, pair[0], pair[1])

    def device_of(x, c, g, q):
        return (x * 2 + c) * grid.seq + g * parts + q

    near_ids = jnp.stack(
        [
            device_of(by_core(c, plane_x)[:, None], c, line_groups[None, :], by_core(c, plane_q)[:, None])
            for c in (core, 1 - core)
        ]
    )
    def group_step(held, entry):
        axis, bit = grid.group_bits[entry]
        got = swap(grid, held, ((axis, bit), (axis, bit)))
        upper = (group >> bit) & 1 == 1
        return jnp.where(upper, jnp.concatenate([got, held]), jnp.concatenate([held, got]))

    def plane_gather(held):
        for pair in grid.plane_bits[:-1]:
            held = jnp.concatenate([held, swap(grid, held, pair)], axis=0)
        return held

    line_bits = same(grid.group_bits)
    got_pack = chip_swap(far_pack)
    got_units = jnp.concatenate([got_pack[:rows_each], got_pack[rows_each : 2 * rows_each]], axis=1)
    table = jnp.concatenate([packets[0], *got_packets], axis=0)
    units = jnp.concatenate([own_units, got_units], axis=0)[None]
    down = group_step(w_down[None], 0)
    table, units, down, sent_tokens, near_ids, line_groups, segments = tie(
        table, units, down, tokens, near_ids, line_groups, segments
    )
    near_rows = (near_ids[..., None] * rows_each + row).reshape(width)
    to_near = (row_ids[:, None] == near_rows[None, :]).astype(bf16)
    line_rows = jnp.repeat(line_groups, columns) * columns + row_ids % columns
    line_near = (line_rows[:, None] == near_rows[None, :]).astype(bf16)
    group_rows = group * columns + jnp.arange(columns, dtype=jnp.int32)
    near_group = (near_rows[:, None] == group_rows[None, :]).astype(bf16)
    own_x, own_q = by_core(core, plane_x), by_core(core, plane_q)
    slot_groups = jnp.asarray(group_order, jnp.int32)
    piece_ids = jnp.stack(
        [
            device_of(own_x[:, None], c, slot_groups[None, :], own_q[:, None])
            for c in (core, 1 - core)
        ],
        axis=2,
    )
    piece_rows = (piece_ids[..., None] * rows_each + row).reshape(width)
    to_piece = (row_ids[:, None] == piece_rows[None, :]).astype(bf16)
    own_ids = by_core(core, [jnp.asarray(ids, jnp.int32) for ids in unit_ids])
    unit = jnp.arange(ff_half, dtype=jnp.int32)
    unit_rows = jnp.repeat(own_ids, ff_each) * rows_each + (unit % ff_each) // small_each
    near_unit = (near_rows[:, None] == unit_rows[None, :]).astype(bf16)

    flags = [
        by_core(core, [(coords[axis] >> bit) & 1 for axis, bit in pair]) for pair in grid.plane_bits
    ]
    unit_block = ff_half // planes
    aligned = unit_block % 128 == 0
    kernel_flags = len(flags) if aligned else 0
    flag_row = jnp.stack(flags).astype(jnp.int32)
    outer_swap = (lambda a: a) if aligned else (lambda a: swap_blocks(a, flags, unit_block))

    own_blocks = local_len // BLK
    part_near = part ^ jnp.arange(parts, dtype=jnp.int32)
    chunk_ids = (line_groups[None, :] * parts + part_near[:, None]).reshape(-1)
    chunk_hot = chunk_ids[:, None] == jnp.arange(grid.seq, dtype=jnp.int32)[None, :]

    def take_chunks(chunks, hot):
        return jnp.sum(jnp.where(hot[:, :, None], chunks[None], 0), axis=1)

    offsets = jnp.arange(local_len, dtype=jnp.int32) // BLK
    block_near = (chunk_ids[:, None] * own_blocks + offsets[None, :]).reshape(-1)
    seg_near = take_chunks(segments.reshape(grid.seq, local_len), chunk_hot).reshape(-1)
    rand_line = take_chunks(rand_blocks.reshape(grid.seq, -1), chunk_hot[:groups])
    rand_line = rand_line.reshape(groups, own_blocks, 1, -1)
    rand_rows = jnp.broadcast_to(rand_line, (groups, own_blocks, BLK, rand_line.shape[-1]))
    rand_rows = rand_rows.reshape(line_len, -1)
    key_block, key_seg = block_near[None, :], seg_near[None, :]
    query_block, query_seg = block_near[:line_len, None], seg_near[:line_len, None]
    near = (key_block >= query_block - 1) & (key_block <= query_block + 1)
    for entry in range(rand_rows.shape[1]):
        near = near | (key_block == rand_rows[:, entry : entry + 1])
    glob_table = glob_blocks[0]
    doc = jnp.arange(glob_table.shape[0], dtype=jnp.int32)[None, :]
    for entry in range(glob_table.shape[1]):
        picked = jnp.sum(
            jnp.where(query_seg == doc, glob_table[None, :, entry], 0), axis=1, keepdims=True
        )
        near = near | (key_block == picked)
    mask_bias = jnp.where(near & (query_seg == key_seg), 0.0, masked_score).astype(f32)

    steps = len(grid.plane_bits)

    x_half = gather_near(grid, sent_tokens, line_bits[:1])
    table = gather_near(grid, table, grid.plane_bits[: steps // 2])
    down = group_step(down, 1)
    table, x_half, down, units = tie(table, x_half, down, units)
    x_far_half = swap(grid, x_half, line_bits[1])
    table = gather_near(grid, table, grid.plane_bits[steps // 2 :])
    units = group_step(units, 0)
    x_near = dot(jnp.concatenate([x_half, x_far_half]), to_near).astype(bf16)
    table, units, down, x_near, mask_bias, to_near, near_group, line_near, near_unit, to_piece = tie(
        table, units, down, x_near, mask_bias, to_near, near_group, line_near, near_unit, to_piece
    )
    table_far = swap(grid, table, grid.core_bit[0])
    down_near = plane_gather(down.reshape(-1, width))
    units = group_step(units, 1)

    query, own_pairs = call(
        qkv_kernel,
        [((line_len, columns), bf16), ((line_len, 2 * columns), bf16)],
        x_near,
        table,
        table_far,
        near_group,
        name="project",
    )
    own_pairs, table_far = tie(own_pairs, table_far)
    in_near = plane_gather(units.reshape(-1, ff_half))
    down_far = swap(grid, down_near, grid.plane_bits[-1])
    qkv_slice, out_line, params, ffn_row = call(
        functools.partial(unfold_kernel, small_each),
        [
            ((width, 3 * columns), bf16),
            ((width, width), bf16),
            ((8, width), f32),
            ((1, ff_half), f32),
        ],
        table,
        table_far,
        to_near,
        line_near,
        near_unit,
        name="unfold_weights",
    )
    ffn_row = outer_swap(ffn_row)
    kept_pairs, out_line, params, qkv_slice = tie(own_pairs, out_line, params, qkv_slice)
    pairs = jnp.concatenate([kept_pairs, swap(grid, own_pairs, part_bits[0])], axis=0)
    pairs = gather_near(grid, pairs, part_bits[1:])
    pairs, in_near = tie(pairs, in_near)
    in_far = swap(grid, in_near, grid.plane_bits[-1])
    in_near, in_far = outer_swap(in_near), outer_swap(in_far)

    att_pieces, logs = attention_forward(query, pairs, mask_bias)
    got_att = line_swap(grid, att_pieces[1:])
    attended = jnp.concatenate([att_pieces[0], *got_att], axis=1)
    attended_far = chip_swap(attended)

    half = width // 2
    chip_len = 2 * local_len
    weight_scratch = lambda *arrays: [pltpu.VMEM(a.shape, bf16) for a in arrays]
    first, normed, inverse, mixed, hidden, active, part_own, part_send = call(
        functools.partial(ffn_forward_kernel, kernel_flags, unit_block),
        [
            ((chip_len, width), f32),
            ((chip_len, width), f32),
            ((chip_len, 128), f32),
            ((chip_len, width), bf16),
            ((chip_len, ff_half), f32),
            ((chip_len, ff_half), bf16),
            ((chip_len, width), f32),
            ((chip_len, width), bf16),
        ],
        flag_row,
        attended,
        attended_far,
        tokens,
        got_pack,
        params,
        ffn_row,
        out_line,
        to_piece,
        in_near,
        in_far,
        down_near,
        down_far,
        name="ffn_forward",
        in_place=(7, 8, 9, 10, 11, 12),
        scratch=weight_scratch(out_line, to_piece, in_near, in_far, down_near, down_far)
        + [pltpu.SemaphoreType.DMA((6,))],
    )
    part_got = chip_swap(part_send)

    output, first_keep, first_send, d_second, d_hidden, sums_two, ffn_sums = call(
        functools.partial(ffn_backward_kernel, kernel_flags, unit_block),
        [
            ((local_len, width), bf16),
            ((local_len, width), f32),
            ((local_len, width), bf16),
            ((chip_len, width), bf16),
            ((chip_len, ff_half), bf16),
            ((8, width), f32),
            ((1, ff_half), f32),
        ],
        flag_row,
        part_own,
        part_got,
        first,
        cot,
        got_pack,
        hidden,
        params,
        to_piece,
        in_near,
        in_far,
        down_near,
        down_far,
        name="ffn_backward",
        in_place=(8, 9, 10, 11, 12),
        scratch=weight_scratch(to_piece, in_near, in_far, down_near, down_far)
        + [pltpu.SemaphoreType.DMA((5,))],
    )
    first_got = chip_swap(first_send)
    first_got, d_hidden, d_second = tie(first_got, d_hidden, d_second)
    down_send = dot(active[:, width:], d_second, 0, 0).astype(bf16)
    down_keep = dot(active[:, :width], d_second, 0, 0).astype(bf16)
    d_hidden, ffn_sums = outer_swap(d_hidden), outer_swap(ffn_sums)
    in_send = dot(mixed[:, half:], d_hidden, 0, 0).astype(bf16)
    in_keep = dot(mixed[:, :half], d_hidden, 0, 0).astype(bf16)
    d_one, d_branch, sums_one, *d_pieces = call(
        branch_backward_kernel,
        [((local_len, width), f32), ((local_len, width), bf16), ((8, width), f32)]
        + [((local_len, columns), bf16)] * groups,
        first_keep,
        first_got,
        normed[:local_len],
        inverse[:local_len],
        params,
        out_line,
        name="branch_backward",
    )
    got_d_att = line_swap(grid, d_pieces[1:])

    def far_sum(keep, send):
        return keep.astype(f32) + swap(grid, send, grid.plane_bits[-1]).astype(f32)

    down_total = far_sum(down_keep, down_send)
    in_total = far_sum(in_keep, in_send)

    def line_sum(total):
        for axis, bit in reversed(grid.group_bits):
            size = total.shape[0] // 2
            upper = (group >> bit) & 1
            keep = lax.dynamic_slice_in_dim(total, upper * size, size, 0)
            send = lax.dynamic_slice_in_dim(total, (1 - upper) * size, size, 0)
            got = swap(grid, send.astype(bf16), ((axis, bit), (axis, bit)))
            total = keep + got.astype(f32)
        return total

    small_sums = call(
        functools.partial(branch_grads_kernel, small_each),
        [((width // 2, width), f32), ((width // 2, width), bf16), ((width, 16), f32)],
        attended,
        d_branch,
        sums_one,
        sums_two,
        ffn_sums,
        to_near,
        line_near,
        near_unit,
        name="branch_gradients",
    )
    d_pieces[0], *small_sums = tie(d_pieces[0], *small_sums)

    d_query, pairs_own, pairs_send = attention_backward(
        query, pairs, mask_bias, [d_pieces[0], *got_d_att], logs
    )
    pairs_own, down_total, in_total = tie(pairs_own, down_total, in_total)
    down_total = reduce_near(grid, down_total, grid.plane_bits[:-1])
    in_total = reduce_near(grid, in_total, grid.plane_bits[:-1])
    if parts == 2:
        pairs_got = swap(grid, pairs_send, part_bits[0])
    else:
        pairs_all = jnp.concatenate([pairs_own, pairs_send.astype(f32)])
        pairs_own = reduce_near(grid, pairs_all, part_bits)
        pairs_got = jnp.zeros(pairs_own.shape, bf16)
    query_grads = call(
        query_grads_kernel,
        [((width, columns), f32), ((width, 8), f32), ((line_len, width), f32)],
        x_near,
        d_query,
        near_group,
        qkv_slice,
        name="query_gradients",
    )
    grad_keep, grad_send, back_keep, back_send = call(
        pair_grads_kernel,
        [
            ((width // 2, table_width), f32),
            ((width // 2, table_width), bf16),
            ((line_len // 2, width), f32),
            ((line_len // 2, width), bf16),
        ],
        x_near,
        pairs_own,
        pairs_got,
        near_group,
        qkv_slice,
        *small_sums,
        *query_grads,
        name="pair_gradients",
    )
    grad_send, down_total, in_total = tie(grad_send, down_total, in_total)
    sum_down = line_sum(down_total)
    in_pairs = line_sum(in_total)
    back = back_keep + swap(grid, back_send, line_bits[1]).astype(f32)
    back = reduce_near(grid, back, line_bits[:1])
    total = grad_keep + chip_swap(grad_send).astype(f32)
    total = reduce_near(grid, total, grid.plane_bits)
    total, in_pairs, d_one = tie(total, in_pairs, d_one)
    in_got = chip_swap(in_pairs[rows_each:])
    (sum_in,) = call(
        functools.partial(units_kernel, unit_ids),
        [((rows_each, ff), f32)],
        place,
        in_pairs[:rows_each],
        in_got,
        name="order_units",
    )

    got_total = line_swap(
        grid, [total[k * rows_each : (k + 1) * rows_each].astype(bf16) for k in range(1, groups)]
    )
    input_grad = d_one + back
    sum_qkv, sum_out, sum_vec, sum_ffn, sum_gain, sum_shift = call(
        functools.partial(finish_kernel, small_each),
        [
            ((rows_each, 3 * width), f32),
            ((rows_each, width), f32),
            ((4, rows_each), f32),
            ((1, ff_each), f32),
            ((2, rows_each), f32),
            ((2, rows_each), f32),
        ],
        place,
        total[:rows_each],
        *got_total,
        name="finish",
    )
    return (
        output[None],
        input_grad[None],
        sum_qkv,
        sum_out,
        sum_in,
        sum_down,
        sum_vec,
        sum_ffn.reshape(ff_each),
        sum_gain,
        sum_shift,
    )


def solution(mesh):
    return jax.shard_map(
        functools.partial(on_device, Grid(mesh)),
        mesh=mesh,
        in_specs=(
            P("dp", "seq", None),
            P("dp", None),
            P("dp", None, None),
            P("dp", None, None),
            P(("dp", "seq"), None),
            P(("dp", "seq"), None),
            P(("dp", "seq"), None),
            P(("dp", "seq"), None),
            P(None, ("dp", "seq")),
            P(("dp", "seq")),
            P(None, ("dp", "seq")),
            P(None, ("dp", "seq")),
            P("dp", "seq", None),
        ),
        out_specs=(
            P("dp", "seq", None),
            P("dp", "seq", None),
            P(("dp", "seq"), None),
            P(("dp", "seq"), None),
            P(("dp", "seq"), None),
            P(("dp", "seq"), None),
            P(None, ("dp", "seq")),
            P(("dp", "seq")),
            P(None, ("dp", "seq")),
            P(None, ("dp", "seq")),
        ),
        check_vma=False,
    )
```

```python
import functools

import jax
import jax.numpy as jnp
import numpy as np
from jax import lax
from jax.experimental import pallas as pl
from jax.experimental.pallas import tpu as pltpu
from jax.sharding import PartitionSpec as P

HD = 64
BLK = 64
HEAD_GROUPS = 4
SCORE_CELLS = 512 * 1024

norm_eps = 1e-05
masked_score = -1e30
BOTH = ("dp", "seq")
bf16 = jnp.bfloat16
f32 = jnp.float32


def normalize(field_in):
    mean_row = jnp.mean(field_in, axis=-1, keepdims=True)
    centred = field_in - mean_row
    inverse = lax.rsqrt(jnp.mean(centred * centred, axis=-1, keepdims=True) + norm_eps)
    return (centred * inverse, inverse)


def norm_back(grad_in, normed, inverse, gain_row):
    weighted = grad_in * gain_row
    inner = jnp.mean(weighted * normed, axis=-1, keepdims=True)
    return inverse * (weighted - jnp.mean(weighted, axis=-1, keepdims=True) - normed * inner)


def gelu_slope(field_in):
    return (
        0.5 * (1.0 + lax.erf(field_in * 0.7071067811865476))
        + field_in * jnp.exp(-0.5 * field_in * field_in) * 0.3989422804014327
    )


def dot(left, right, left_dim=1, right_dim=0):
    return lax.dot_general(
        left, right, (((left_dim,), (right_dim,)), ((), ())), preferred_element_type=f32
    )


def call(body, outs, *args, name, scratch=(), flops=1e8, in_place=()):
    space = lambda i, a: (
        pl.ANY if i in in_place else pltpu.SMEM if a.dtype == jnp.int32 else pltpu.VMEM
    )
    specs = [pl.BlockSpec(memory_space=space(i, a)) for i, a in enumerate(args)]
    moved = sum(int(np.prod(a.shape)) * a.dtype.itemsize for a in args)
    return pl.pallas_call(
        body,
        in_specs=specs,
        out_specs=[pl.BlockSpec(memory_space=pltpu.VMEM)] * len(outs),
        out_shape=[jax.ShapeDtypeStruct(shape, dtype) for shape, dtype in outs],
        scratch_shapes=list(scratch),
        compiler_params=pltpu.CompilerParams(vmem_limit_bytes=56 * 1024 * 1024),
        cost_estimate=pl.CostEstimate(flops=int(flops), bytes_accessed=moved, transcendentals=0),
        name=name,
    )(*args)


def copies(pairs, sems):
    started = []
    for i, (source, target) in enumerate(pairs):
        copy = pltpu.make_async_copy(source, target, sems.at[i])
        copy.start()
        started.append(copy)
    return started


def exact(left, right, left_dim=1, right_dim=0):
    return lax.dot_general(
        left,
        right,
        (((left_dim,), (right_dim,)), ((), ())),
        preferred_element_type=f32,
        precision=lax.Precision.HIGHEST,
    )


def iota(shape, dim):
    return lax.broadcasted_iota(jnp.int32, shape, dim)


def spread_rows(row, rows, each):
    lanes = row.shape[1]
    picked = jnp.where(iota((rows, lanes), 1) // each == iota((rows, lanes), 0), row, 0.0)
    select = (iota((lanes, each), 0) % each == iota((lanes, each), 1)).astype(f32)
    return exact(picked, select)


def pick(options, index):
    chosen = options[0]
    for i, option in enumerate(options[1:]):
        chosen = jnp.where(index == i + 1, option, chosen)
    return chosen


def crossed(number):
    return (number % 2) * 2 + number // 2


def pack_kernel(
    unit_ids,
    place_ref,
    qkv_ref,
    out_ref,
    in_ref,
    x_ref,
    cot_ref,
    vec_ref,
    ffn_ref,
    gain_ref,
    shift_ref,
    *outs,
):
    core, group = place_ref[0], place_ref[1]
    rows, width = out_ref.shape
    columns = width // HEAD_GROUPS
    rolled = lambda g: [
        qkv_ref[:, kind * width + g * columns : kind * width + (g + 1) * columns] for kind in (1, 2, 0)
    ]
    by_group = [jnp.concatenate(rolled(g), axis=1) for g in range(HEAD_GROUPS)]
    same_row = (iota((rows, rows), 0) == iota((rows, rows), 1)).astype(bf16)
    turned = [dot(same_row, ref[...], 1, 1) for ref in (vec_ref, gain_ref, shift_ref)]
    turned.append(spread_rows(ffn_ref[...].astype(f32), rows, ffn_ref.shape[1] // rows))
    small = jnp.concatenate(turned, axis=1).astype(bf16)
    for k in range(HEAD_GROUPS):
        chosen = pick(by_group, group ^ crossed(k))
        rest = outs[k].shape[1] - 3 * columns - width - small.shape[1]
        outs[k][:, : 2 * columns] = chosen[:, : 2 * columns]
        outs[k][:, 2 * columns : 2 * columns + width] = out_ref[...]
        outs[k][:, 2 * columns + width :] = jnp.concatenate(
            [chosen[:, 2 * columns :], small, jnp.zeros((rows, rest), bf16)], axis=1
        )
    each = ffn_ref.shape[1]
    units = [
        jnp.concatenate([in_ref[:, i * each : (i + 1) * each] for i in ids], axis=1) for ids in unit_ids
    ]
    outs[HEAD_GROUPS][...] = jnp.where(core == 0, units[0], units[1])
    far = jnp.where(core == 0, units[1], units[0])
    far_ref = outs[HEAD_GROUPS + 1]
    tokens = x_ref.shape[0]
    top = far_ref.shape[0] - 2 * tokens
    blank = jnp.zeros((top - 2 * rows, width), bf16)
    far_ref[:top] = jnp.concatenate([far[:, :width], far[:, width:], blank][: 3 if top > 2 * rows else 2])
    far_ref[top : top + tokens] = x_ref[...]
    far_ref[top + tokens :] = cot_ref[...]


def unfold_kernel(
    small_each, table_ref, far_ref, near_ref, line_ref, unit_ref, qkv_ref, out_ref, par_ref, ffn_ref
):
    columns = qkv_ref.shape[1] // 3
    width = out_ref.shape[1]
    start, at = 2 * columns, 2 * columns + width
    near = near_ref[...]
    both = lambda i, j: jnp.concatenate([table_ref[:, i:j], far_ref[:, i:j]], axis=0)
    rest = both(at, table_ref.shape[1])
    qkv_ref[:, :start] = dot(near, both(0, start)).astype(bf16)
    qkv_ref[:, start:] = dot(near, rest[:, :columns]).astype(bf16)
    out_ref[...] = dot(line_ref[...], both(start, at)).astype(bf16)
    small = rest[:, columns : columns + 8 + small_each]
    par_ref[...] = dot(small[:, :8], near, 0, 1)
    by_slot = dot(small[:, 8:], unit_ref[...], 0, 0)
    slot = iota(by_slot.shape, 1) % small_each == iota(by_slot.shape, 0)
    ffn_ref[...] = jnp.sum(jnp.where(slot, by_slot, 0.0), axis=0, keepdims=True)


def qkv_kernel(x_ref, table_ref, far_ref, sel_ref, q_ref, pair_ref):
    columns = q_ref.shape[1]
    width = x_ref.shape[1]
    half = width // 2
    start, at = 2 * columns, 2 * columns + width
    pairs = dot(x_ref[:, :half], table_ref[:, :start]) + dot(x_ref[:, half:], far_ref[:, :start])
    rest = jnp.concatenate([table_ref[:, at:], far_ref[:, at:]], axis=0)
    biases = dot(rest[:, columns : columns + 8], sel_ref[...], 0, 0)
    values = pairs[:, columns:] + biases[1:2]
    pair_ref[...] = jnp.concatenate([pairs[:, :columns], values], axis=1).astype(bf16)
    queries = dot(x_ref[...], rest[:, :columns]) + biases[0:1]
    q_ref[...] = (queries * HD ** (-0.5)).astype(bf16)


def head_mask(shape, head):
    lane = iota(shape, 1)
    return (lane >= head * HD) & (lane < (head + 1) * HD)


def split_pairs(pair_refs, k_ref, v_ref):
    width = k_ref.shape[1]
    start = 0
    for ref in pair_refs:
        end = start + ref.shape[0]
        k_ref[start:end] = ref[:, :width]
        v_ref[start:end] = ref[:, width:]
        start = end


def forward_kernel(q_ref, kv_ref, far_ref, b_ref, *refs):
    *o_refs, l_ref, k_ref, v_ref = refs
    step = pl.program_id(0)

    @pl.when(step == 0)
    def _():
        split_pairs((kv_ref, far_ref), k_ref, v_ref)

    query, keys, values, bias = q_ref[...], k_ref[...], v_ref[...], b_ref[...]
    rows, width = query.shape
    out = jnp.zeros(query.shape, f32)
    logs = jnp.zeros(l_ref.shape, f32)
    for head in range(width // HD):
        mine = head_mask(query.shape, head)
        scores = dot(jnp.where(mine, query, jnp.zeros_like(query)), keys, 1, 1) + bias
        top = jnp.max(scores, axis=1, keepdims=True)
        terms = jnp.exp(scores - top)
        total = jnp.sum(terms, axis=1, keepdims=True)
        probs = (terms * (1.0 / total)).astype(bf16)
        out = out + jnp.where(mine, dot(probs, values), 0.0)
        logs = jnp.where(iota(l_ref.shape, 1) == head, top + jnp.log(total), logs)
    l_ref[...] = logs
    low = out.astype(bf16)
    piece = o_refs[0].shape[0]
    each = rows // piece
    for k, o_ref in enumerate(o_refs):
        start = (k % each) * piece

        @pl.when(step == k // each)
        def _(o_ref=o_ref, start=start):
            o_ref[...] = low[start : start + piece]


def backward_kernel(q_ref, kv_ref, far_ref, b_ref, *refs):
    pieces, att_refs, refs = refs[:HEAD_GROUPS], refs[HEAD_GROUPS : 2 * HEAD_GROUPS], refs[2 * HEAD_GROUPS :]
    l_ref, dq_ref, own_ref, send_ref, k_ref, v_ref, d_ref, o_ref, dk_ref, dv_ref = refs
    step = pl.program_id(0)
    rows, width = q_ref.shape

    @pl.when(step == 0)
    def _():
        split_pairs((kv_ref, far_ref), k_ref, v_ref)
        dk_ref[...] = jnp.zeros(dk_ref.shape, f32)
        dv_ref[...] = jnp.zeros(dv_ref.shape, f32)
        piece = pieces[0].shape[0]
        for k, ref in enumerate(pieces):
            d_ref[k * piece : (k + 1) * piece] = ref[...]
            o_ref[k * piece : (k + 1) * piece] = att_refs[k][...]

    query, keys, values, bias = q_ref[...], k_ref[...], v_ref[...], b_ref[...]
    here = pl.ds(pl.multiple_of(step * rows, rows), rows)
    d_att = d_ref[here]
    products = d_att.astype(f32) * o_ref[here].astype(f32)
    logs = l_ref[...]
    d_query = jnp.zeros(query.shape, f32)
    for head in range(width // HD):
        mine = head_mask(query.shape, head)
        q_head = jnp.where(mine, query, jnp.zeros_like(query))
        d_head = jnp.where(mine, d_att, jnp.zeros_like(d_att))
        scores = dot(q_head, keys, 1, 1) + bias
        weights = jnp.exp(scores - logs[:, head : head + 1])
        d_probs = dot(d_head, values, 1, 1)
        delta = jnp.sum(jnp.where(mine, products, 0.0), axis=1, keepdims=True)
        d_scores = (weights * (d_probs - delta)).astype(bf16)
        d_query = d_query + jnp.where(mine, dot(d_scores, keys), 0.0)
        dk_ref[...] += dot(d_scores, q_head, 0, 0)
        dv_ref[...] += dot(weights.astype(bf16), d_head, 0, 0)
    dq_ref[...] = (d_query * HD ** (-0.5)).astype(bf16)

    @pl.when(step == pl.num_programs(0) - 1)
    def _():
        kept = own_ref.shape[0]
        own_ref[:, :width] = dk_ref[:kept]
        own_ref[:, width:] = dv_ref[:kept]
        send_ref[:, :width] = dk_ref[kept:].astype(bf16)
        send_ref[:, width:] = dv_ref[kept:].astype(bf16)


def attention_forward(query, pairs, bias):
    rows, width = query.shape
    key_rows = sum(a.shape[0] for a in pairs)
    tile = min(rows, SCORE_CELLS // key_rows)
    piece = rows // HEAD_GROUPS
    results = pl.pallas_call(
        forward_kernel,
        grid=(rows // tile,),
        in_specs=[
            pl.BlockSpec((tile, width), lambda i: (i, 0)),
            *[pl.BlockSpec(a.shape, lambda i: (0, 0)) for a in pairs],
            pl.BlockSpec((tile, key_rows), lambda i: (i, 0)),
        ],
        out_specs=[pl.BlockSpec((piece, width), lambda i: (0, 0))] * HEAD_GROUPS
        + [pl.BlockSpec((tile, 128), lambda i: (i, 0))],
        out_shape=[jax.ShapeDtypeStruct((piece, width), bf16)] * HEAD_GROUPS
        + [jax.ShapeDtypeStruct((rows, 128), f32)],
        scratch_shapes=[pltpu.VMEM((key_rows, width), bf16)] * 2,
        compiler_params=pltpu.CompilerParams(vmem_limit_bytes=56 * 1024 * 1024),
        cost_estimate=pl.CostEstimate(
            flops=16 * rows * key_rows * width, bytes_accessed=4 * rows * key_rows, transcendentals=0
        ),
        name="attention_forward",
    )(query, *pairs, bias)
    return results[:-1], results[-1]


def attention_backward(query, pairs, bias, d_pieces, att_pieces, logs):
    rows, width = query.shape
    key_rows = sum(a.shape[0] for a in pairs)
    tile = min(rows, SCORE_CELLS // key_rows)
    fixed = lambda n: pl.BlockSpec((n, 2 * width), lambda i: (0, 0))
    return pl.pallas_call(
        backward_kernel,
        grid=(rows // tile,),
        in_specs=[
            pl.BlockSpec((tile, width), lambda i: (i, 0)),
            *[pl.BlockSpec(a.shape, lambda i: (0, 0)) for a in pairs],
            pl.BlockSpec((tile, key_rows), lambda i: (i, 0)),
        ]
        + [pl.BlockSpec(d_pieces[0].shape, lambda i: (0, 0))] * (2 * HEAD_GROUPS)
        + [pl.BlockSpec((tile, 128), lambda i: (i, 0))],
        out_specs=[
            pl.BlockSpec((tile, width), lambda i: (i, 0)),
            fixed(rows),
            fixed(key_rows - rows),
        ],
        out_shape=[
            jax.ShapeDtypeStruct((rows, width), bf16),
            jax.ShapeDtypeStruct((rows, 2 * width), f32),
            jax.ShapeDtypeStruct((key_rows - rows, 2 * width), bf16),
        ],
        scratch_shapes=[pltpu.VMEM((key_rows, width), bf16)] * 2
        + [pltpu.VMEM((rows, width), bf16)] * 2
        + [pltpu.VMEM((key_rows, width), f32)] * 2,
        compiler_params=pltpu.CompilerParams(vmem_limit_bytes=56 * 1024 * 1024),
        cost_estimate=pl.CostEstimate(
            flops=30 * rows * key_rows * width, bytes_accessed=4 * rows * key_rows, transcendentals=0
        ),
        name="attention_backward",
    )(query, *pairs, bias, *d_pieces, *att_pieces, logs)


def swap_blocks(a, flags, block):
    for step, flag in enumerate(flags):
        size = block << step
        blocks = [a[:, i : i + size] for i in range(0, a.shape[1], size)]
        flipped = [blocks[i ^ 1] for i in range(len(blocks))]
        a = jnp.where(flag == 1, jnp.concatenate(flipped, axis=1), a)
    return a


def ffn_forward_kernel(
    flag_count,
    block,
    flag_ref,
    att_ref,
    att_far_ref,
    x_ref,
    far_ref,
    par_ref,
    ffn_ref,
    out_hbm,
    mix_hbm,
    in_near_hbm,
    in_far_hbm,
    down_near_hbm,
    down_far_hbm,
    first_ref,
    normed_ref,
    inverse_ref,
    mixed_ref,
    hidden_ref,
    active_ref,
    part_ref,
    send_ref,
    out_ref,
    mix_ref,
    in_near_ref,
    in_far_ref,
    down_near_ref,
    down_far_ref,
    sems,
):
    waits = copies(
        [
            (out_hbm, out_ref),
            (mix_hbm, mix_ref),
            (in_near_hbm, in_near_ref),
            (in_far_hbm, in_far_ref),
            (down_near_hbm, down_near_ref),
            (down_far_hbm, down_far_ref),
        ],
        sems,
    )
    flags = [flag_ref[i] for i in range(flag_count)]
    attended = jnp.concatenate([att_ref[...], att_far_ref[...]], axis=0)
    rows = x_ref.shape[0]
    top = far_ref.shape[0] - 2 * rows
    tokens = jnp.concatenate([x_ref[...], far_ref[top : top + rows]], axis=0).astype(f32)
    waits[0].wait()
    branch = dot(attended, out_ref[...]) + par_ref[2:3]
    normed, inverse = normalize(tokens + branch)
    first = normed * par_ref[4:5] + par_ref[6:7]
    first_ref[...] = first
    normed_ref[...] = normed
    inverse_ref[...] = jnp.broadcast_to(inverse, inverse_ref.shape)
    waits[1].wait()
    mixed = dot(first.astype(bf16), mix_ref[...]).astype(bf16)
    mixed_ref[...] = mixed
    half = mixed.shape[1] // 2
    waits[2].wait()
    hidden = dot(mixed[:, :half], in_near_ref[...])
    waits[3].wait()
    hidden = hidden + dot(mixed[:, half:], in_far_ref[...]) + ffn_ref[...]
    hidden = swap_blocks(hidden, flags, block)
    hidden_ref[...] = hidden
    active = (0.5 * hidden * (1.0 + lax.erf(hidden * 0.7071067811865476))).astype(bf16)
    active_ref[...] = active
    units = active.shape[1] // 2
    waits[4].wait()
    part = dot(active[:, :units], down_near_ref[...])
    waits[5].wait()
    part = part + dot(active[:, units:], down_far_ref[...])
    part_ref[...] = part
    send_ref[...] = part.astype(bf16)


def column_sum(a):
    return jnp.sum(a, axis=0, keepdims=True)


def ffn_backward_kernel(
    flag_count,
    block,
    flag_ref,
    part_ref,
    got_ref,
    first_ref,
    cot_ref,
    far_ref,
    hidden_ref,
    par_ref,
    mix_hbm,
    in_near_hbm,
    in_far_hbm,
    down_near_hbm,
    down_far_hbm,
    output_ref,
    keep_ref,
    send_ref,
    second_ref,
    d_hidden_ref,
    sums_ref,
    ffn_sum_ref,
    mix_ref,
    in_near_ref,
    in_far_ref,
    down_near_ref,
    down_far_ref,
    sems,
):
    waits = copies(
        [
            (down_near_hbm, down_near_ref),
            (down_far_hbm, down_far_ref),
            (in_near_hbm, in_near_ref),
            (in_far_hbm, in_far_ref),
            (mix_hbm, mix_ref),
        ],
        sems,
    )
    flags = [flag_ref[i] for i in range(flag_count)]
    rows = got_ref.shape[0] // 2
    other = jnp.concatenate([got_ref[rows:], got_ref[:rows]], axis=0).astype(f32)
    normed, inverse = normalize(first_ref[...] + part_ref[...] + other + par_ref[3:4])
    gain = par_ref[5:6]
    output_ref[...] = (normed[:rows] * gain + par_ref[7:8]).astype(bf16)
    out_grad = jnp.concatenate([cot_ref[...], far_ref[far_ref.shape[0] - rows :]], axis=0).astype(f32)
    d_two = norm_back(out_grad, normed, inverse, gain)
    d_second = d_two.astype(bf16)
    second_ref[...] = d_second
    sums_ref[...] = jnp.concatenate(
        [
            column_sum(out_grad[:rows] * normed[:rows]),
            column_sum(out_grad[:rows]),
            column_sum(d_second[:rows].astype(f32)),
            jnp.zeros((5, normed.shape[1]), f32),
        ],
        axis=0,
    )
    waits[0].wait()
    near = dot(d_second, down_near_ref[...], 1, 1)
    waits[1].wait()
    far = dot(d_second, down_far_ref[...], 1, 1)
    slope = gelu_slope(hidden_ref[...])
    d_hidden = jnp.concatenate([near, far], axis=1) * slope
    d_hidden = swap_blocks(d_hidden, flags, block).astype(bf16)
    d_hidden_ref[...] = d_hidden
    ffn_sum_ref[...] = column_sum(d_hidden.astype(f32))
    waits[2].wait()
    near = dot(d_hidden, in_near_ref[...], 1, 1).astype(bf16)
    waits[3].wait()
    far = dot(d_hidden, in_far_ref[...], 1, 1).astype(bf16)
    waits[4].wait()
    part = dot(jnp.concatenate([near, far], axis=1), mix_ref[...], 1, 1)
    keep_ref[...] = d_two[:rows] + part[:rows]
    send_ref[...] = part[rows:].astype(bf16)


def branch_backward_kernel(
    keep_ref, got_ref, normed_ref, inverse_ref, par_ref, out_ref, d_one_ref, branch_ref, sums_ref, *pieces
):
    d_first = keep_ref[...] + got_ref[...].astype(f32)
    normed, inverse = normed_ref[...], inverse_ref[:, :1]
    d_one = norm_back(d_first, normed, inverse, par_ref[4:5])
    d_one_ref[...] = d_one
    d_branch = d_one.astype(bf16)
    branch_ref[...] = d_branch
    sums_ref[...] = jnp.concatenate(
        [
            column_sum(d_first * normed),
            column_sum(d_first),
            column_sum(d_branch.astype(f32)),
            jnp.zeros((5, normed.shape[1]), f32),
        ],
        axis=0,
    )
    d_attended = dot(d_branch, out_ref[...], 1, 1).astype(bf16)
    columns = pieces[0].shape[1]
    for k, piece in enumerate(pieces):
        piece[...] = d_attended[:, k * columns : (k + 1) * columns]


def branch_grads_kernel(att_ref, branch_ref, line_ref, out_ref):
    attended = dot(att_ref[...], line_ref[...]).astype(bf16)
    out_ref[...] = dot(attended, branch_ref[...], 0, 0).astype(bf16)


def query_grads_kernel(
    small_each,
    x_ref,
    dq_ref,
    sel_ref,
    sums_ref,
    sums_two_ref,
    ffn_ref,
    near_ref,
    unit_ref,
    last_ref,
):
    columns = dq_ref.shape[1]
    d_query = dq_ref[...]
    queries = dot(x_ref[...], d_query, 0, 0)
    sums = jnp.concatenate([column_sum(d_query.astype(f32)), jnp.zeros((7, columns), f32)], axis=0)
    bias = dot(sel_ref[...], sums.astype(bf16), 1, 1)
    first, second = sums_ref[...], sums_two_ref[...]
    blank = jnp.zeros((2, first.shape[1]), f32)
    vectors = jnp.concatenate(
        [blank, first[2:3], second[2:3], first[0:1], second[0:1], first[1:2], second[1:2]], axis=0
    )
    vectors = dot(near_ref[...], vectors.astype(bf16), 0, 1) + bias
    units = ffn_ref.shape[1]
    slot = iota((8, units), 1) % small_each == iota((8, units), 0)
    by_slot = jnp.where(slot, ffn_ref[...], 0.0).astype(bf16)
    ffn = dot(unit_ref[...], by_slot, 1, 1)
    rest = last_ref.shape[1] - columns - 16
    last = [queries, vectors, ffn, jnp.zeros((queries.shape[0], rest), f32)]
    last_ref[...] = jnp.concatenate(last, axis=1)


def pair_grads_kernel(
    x_ref,
    own_ref,
    got_ref,
    dq_ref,
    sel_ref,
    qkv_ref,
    out_ref,
    last_ref,
    keep_ref,
    send_ref,
    back_ref,
    back_send_ref,
):
    pair_columns = own_ref.shape[1]
    columns = pair_columns // 2
    width = x_ref.shape[1]
    half = width // 2
    at = pair_columns + width
    d_pairs = (own_ref[...] + got_ref[...].astype(f32)).astype(bf16)
    pairs = dot(x_ref[...], d_pairs, 0, 0).astype(bf16)
    sums = [jnp.zeros((1, columns), f32), column_sum(d_pairs[:, columns:].astype(f32))]
    sums = jnp.concatenate([*sums, jnp.zeros((6, columns), f32)], axis=0)
    bias = dot(sel_ref[...], sums.astype(bf16), 1, 1)[:, 1:2]
    last = last_ref[...]
    last = (last + jnp.where(iota(last.shape, 1) == columns + 1, bias, 0.0)).astype(bf16)
    for ref, rows in ((send_ref, slice(half, width)), (keep_ref, slice(0, half))):
        ref[:, :pair_columns] = pairs[rows]
        ref[:, pair_columns:at] = out_ref[rows]
        ref[:, at:] = last[rows]
    grad_back = dot(dq_ref[...], qkv_ref[:, pair_columns:], 1, 1)
    grad_back = grad_back + dot(d_pairs, qkv_ref[:, :pair_columns], 1, 1)
    rows = back_ref.shape[0]
    back_ref[...] = grad_back[:rows]
    back_send_ref[...] = grad_back[rows:].astype(bf16)


def finish_kernel(small_each, place_ref, own_ref, *refs):
    pieces, outs = refs[: HEAD_GROUPS - 1], refs[HEAD_GROUPS - 1 :]
    qkv_ref, out_ref, vec_ref, ffn_ref, gain_ref, shift_ref = outs
    group = place_ref[1]
    rows, width = out_ref.shape
    columns = width // HEAD_GROUPS
    line = [own_ref[...]] + [piece[...].astype(f32) for piece in pieces]
    at = 2 * columns + width
    for g in range(HEAD_GROUPS):
        source = crossed(group ^ g)
        pairs = pick([a[:, : 2 * columns] for a in line], source)
        queries = pick([a[:, at : at + columns] for a in line], source)
        for kind, mine in enumerate((queries, pairs[:, :columns], pairs[:, columns:])):
            start = kind * width + g * columns
            qkv_ref[:, start : start + columns] = mine
    out_ref[...] = sum(a[:, 2 * columns : at] for a in line)
    rest = sum(a[:, at:] for a in line)
    small = rest[:, columns : columns + 8 + small_each]
    same_row = (iota((rows, rows), 0) == iota((rows, rows), 1)).astype(f32)
    turned = exact(small[:, :8], same_row, 0, 0)
    vec_ref[...] = turned[:4]
    gain_ref[...] = turned[4:6]
    shift_ref[...] = turned[6:8]
    each = small.shape[1] - 8
    lanes = rows * each
    select = (iota((each, lanes), 1) % each == iota((each, lanes), 0)).astype(f32)
    wide = exact(small[:, 8:], select)
    mine = iota((rows, lanes), 1) // each == iota((rows, lanes), 0)
    ffn_ref[...] = column_sum(jnp.where(mine, wide, 0.0))


def units_kernel(unit_ids, place_ref, keep_ref, got_ref, out_ref):
    core = place_ref[0]
    keep, got = keep_ref[...], got_ref[...].astype(f32)
    sources = [jnp.where(core == 0, keep, got), jnp.where(core == 0, got, keep)]
    count = 2 * len(unit_ids[0])
    each = out_ref.shape[1] // count
    blocks = {}
    for c, ids in enumerate(unit_ids):
        for slot, device in enumerate(ids):
            blocks[int(device)] = sources[c][:, slot * each : (slot + 1) * each]
    out_ref[...] = jnp.concatenate([blocks[i] for i in range(count)], axis=1)


class Grid:
    def __init__(self, mesh):
        self.dp, self.seq = mesh.shape["dp"], mesh.shape["seq"]
        self.count = self.dp * self.seq
        self.xs, self.parts = self.dp // 2, self.seq // HEAD_GROUPS
        bits = lambda axis, size: [(axis, b) for b in range(size.bit_length() - 1)]
        x_bits, self.part_bits = bits("x", self.xs), bits("q", self.parts)
        self.group_bits = [("g", 1), ("g", 0)]
        alternate = len(x_bits) == len(self.part_bits)
        self.plane = (
            x_bits + self.part_bits,
            self.part_bits + x_bits if alternate else x_bits + self.part_bits,
        )
        self.core_bit = [(("c", 0), ("c", 0))]
        self.plane_bits = list(zip(*self.plane))

    def place(self, device):
        dp, seq = divmod(device, self.seq)
        return {"x": dp // 2, "c": dp % 2, "g": seq // self.parts, "q": seq % self.parts}

    def device(self, at):
        return (at["x"] * 2 + at["c"]) * self.seq + at["g"] * self.parts + at["q"]

    def flip(self, bits_of_core):
        pairs = []
        for device in range(self.count):
            at = self.place(device)
            axis, bit = bits_of_core[at["c"]]
            at[axis] ^= 1 << bit
            pairs.append((device, self.device(at)))
        return pairs

    def cross(self, by):
        pairs = []
        for device in range(self.count):
            at = self.place(device)
            at["g"] ^= by
            pairs.append((device, self.device(at)))
        return pairs

    def plane_masks(self, core):
        masks = {"x": [], "q": []}
        for index in range(self.xs * self.parts):
            for axis in masks:
                flips = [
                    1 << bit
                    for step, (a, bit) in enumerate(self.plane[core])
                    if a == axis and (index >> step) & 1
                ]
                masks[axis].append(sum(flips))
        return {axis: np.array(m, np.int32) for axis, m in masks.items()}


def same(bits):
    return [(bit, bit) for bit in bits]


def swap(grid, held, bits):
    return lax.ppermute(held, BOTH, grid.flip(bits))


def gather_near(grid, held, bit_pairs):
    for pair in bit_pairs:
        held = jnp.concatenate([held, swap(grid, held, pair)], axis=0)
    return held


def reduce_near(grid, total, bit_pairs):
    for pair in reversed(bit_pairs):
        half = total.shape[0] // 2
        got = swap(grid, total[half:].astype(bf16), pair)
        total = total[:half].astype(f32) + got.astype(f32)
    return total


def line_swap(grid, pieces):
    return [
        lax.ppermute(piece, BOTH, grid.cross(crossed(k + 1))) for k, piece in enumerate(pieces)
    ]


def tie(*values):
    return lax.optimization_barrier(values)


def on_device(
    grid,
    inputs,
    segments,
    rand_blocks,
    glob_blocks,
    w_qkv,
    w_out,
    w_in,
    w_down,
    vec_bias,
    ffn_bias,
    norm_gain,
    norm_shift,
    cotangent,
):
    local_len, width = inputs.shape[1:]
    rows_each, ff_each = w_in.shape[0], w_down.shape[0]
    ff = w_in.shape[1]
    ff_half = ff // 2
    groups, parts, xs = HEAD_GROUPS, grid.parts, grid.xs
    planes = xs * parts
    columns = width // groups
    line_len = groups * local_len
    small_each = ff_each // rows_each
    table_width = -(-(3 * columns + width + 8 + small_each) // 128) * 128
    dp_place, seq_place = lax.axis_index("dp"), lax.axis_index("seq")
    core, group, part = dp_place % 2, seq_place // parts, seq_place % parts
    coords = {"x": dp_place // 2, "c": core, "g": group, "q": part}
    place = jnp.stack([core, group]).astype(jnp.int32)
    chip_swap = lambda a: swap(grid, a, grid.core_bit[0])
    group_order = np.array([0, 2, 1, 3])
    group_slot = lambda g: (g % 2) * 2 + g // 2
    tokens = inputs.reshape(local_len, width)
    cot = cotangent.reshape(local_len, width)
    part_bits = same(grid.part_bits)

    masks = [grid.plane_masks(c) for c in range(2)]
    unit_ids = []
    for c in range(2):
        ids = [
            grid.device({"x": masks[c]["x"][index], "c": c, "g": g, "q": masks[c]["q"][index]})
            for index in range(planes)
            for g in group_order
        ]
        unit_ids.append(np.array(ids))

    far_top = -(-2 * rows_each // 16) * 16
    *packets, own_units, far_pack = call(
        functools.partial(pack_kernel, unit_ids),
        [((rows_each, table_width), bf16)] * groups
        + [((rows_each, ff_half), bf16), ((far_top + 2 * local_len, width), bf16)],
        place,
        w_qkv,
        w_out,
        w_in,
        tokens,
        cot,
        vec_bias,
        ffn_bias.reshape(1, ff_each),
        norm_gain,
        norm_shift,
        name="pack_weights",
        scratch=(),
    )
    got_packets = line_swap(grid, packets[1:])

    plane_x = [coords["x"] ^ jnp.asarray(masks[c]["x"]) for c in range(2)]
    plane_q = [part ^ jnp.asarray(masks[c]["q"]) for c in range(2)]
    line_groups = group ^ jnp.asarray(group_order, jnp.int32)
    row = jnp.arange(rows_each, dtype=jnp.int32)
    row_ids = jnp.arange(width, dtype=jnp.int32)
    by_core = lambda c, pair: jnp.where(c == 0, pair[0], pair[1])

    def device_of(x, c, g, q):
        return (x * 2 + c) * grid.seq + g * parts + q

    near_ids = jnp.stack(
        [
            device_of(by_core(c, plane_x)[:, None], c, line_groups[None, :], by_core(c, plane_q)[:, None])
            for c in (core, 1 - core)
        ]
    )
    def group_step(held, entry):
        axis, bit = grid.group_bits[entry]
        got = swap(grid, held, ((axis, bit), (axis, bit)))
        upper = (group >> bit) & 1 == 1
        return jnp.where(upper, jnp.concatenate([got, held]), jnp.concatenate([held, got]))

    def plane_gather(held):
        for pair in grid.plane_bits[:-1]:
            held = jnp.concatenate([held, swap(grid, held, pair)], axis=0)
        return held

    line_bits = same(grid.group_bits)
    got_pack = chip_swap(far_pack)
    got_units = jnp.concatenate([got_pack[:rows_each], got_pack[rows_each : 2 * rows_each]], axis=1)
    table = jnp.concatenate([packets[0], *got_packets], axis=0)
    units = jnp.concatenate([own_units, got_units], axis=0)[None]
    down = group_step(w_down[None], 0)
    table, units, down, sent_tokens, near_ids, line_groups, segments = tie(
        table, units, down, tokens, near_ids, line_groups, segments
    )
    near_rows = (near_ids[..., None] * rows_each + row).reshape(width)
    to_near = (row_ids[:, None] == near_rows[None, :]).astype(bf16)
    line_rows = jnp.repeat(line_groups, columns) * columns + row_ids % columns
    line_near = (line_rows[:, None] == near_rows[None, :]).astype(bf16)
    group_rows = group * columns + jnp.arange(columns, dtype=jnp.int32)
    near_group = (near_rows[:, None] == group_rows[None, :]).astype(bf16)
    own_x, own_q = by_core(core, plane_x), by_core(core, plane_q)
    slot_groups = jnp.asarray(group_order, jnp.int32)
    piece_ids = jnp.stack(
        [
            device_of(own_x[:, None], c, slot_groups[None, :], own_q[:, None])
            for c in (core, 1 - core)
        ],
        axis=2,
    )
    piece_rows = (piece_ids[..., None] * rows_each + row).reshape(width)
    to_piece = (row_ids[:, None] == piece_rows[None, :]).astype(bf16)
    own_ids = by_core(core, [jnp.asarray(ids, jnp.int32) for ids in unit_ids])
    unit = jnp.arange(ff_half, dtype=jnp.int32)
    unit_rows = jnp.repeat(own_ids, ff_each) * rows_each + (unit % ff_each) // small_each
    near_unit = (near_rows[:, None] == unit_rows[None, :]).astype(bf16)

    flags = [
        by_core(core, [(coords[axis] >> bit) & 1 for axis, bit in pair]) for pair in grid.plane_bits
    ]
    unit_block = ff_half // planes
    aligned = unit_block % 128 == 0
    kernel_flags = len(flags) if aligned else 0
    flag_row = jnp.stack(flags).astype(jnp.int32)
    outer_swap = (lambda a: a) if aligned else (lambda a: swap_blocks(a, flags, unit_block))

    own_blocks = local_len // BLK
    part_near = part ^ jnp.arange(parts, dtype=jnp.int32)
    chunk_ids = (line_groups[None, :] * parts + part_near[:, None]).reshape(-1)
    chunk_hot = chunk_ids[:, None] == jnp.arange(grid.seq, dtype=jnp.int32)[None, :]

    def take_chunks(chunks, hot):
        return jnp.sum(jnp.where(hot[:, :, None], chunks[None], 0), axis=1)

    offsets = jnp.arange(local_len, dtype=jnp.int32) // BLK
    block_near = (chunk_ids[:, None] * own_blocks + offsets[None, :]).reshape(-1)
    seg_near = take_chunks(segments.reshape(grid.seq, local_len), chunk_hot).reshape(-1)
    rand_line = take_chunks(rand_blocks.reshape(grid.seq, -1), chunk_hot[:groups])
    rand_line = rand_line.reshape(groups, own_blocks, 1, -1)
    rand_rows = jnp.broadcast_to(rand_line, (groups, own_blocks, BLK, rand_line.shape[-1]))
    rand_rows = rand_rows.reshape(line_len, -1)
    key_block, key_seg = block_near[None, :], seg_near[None, :]
    query_block, query_seg = block_near[:line_len, None], seg_near[:line_len, None]
    near = (key_block >= query_block - 1) & (key_block <= query_block + 1)
    for entry in range(rand_rows.shape[1]):
        near = near | (key_block == rand_rows[:, entry : entry + 1])
    glob_table = glob_blocks[0]
    doc = jnp.arange(glob_table.shape[0], dtype=jnp.int32)[None, :]
    for entry in range(glob_table.shape[1]):
        picked = jnp.sum(
            jnp.where(query_seg == doc, glob_table[None, :, entry], 0), axis=1, keepdims=True
        )
        near = near | (key_block == picked)
    mask_bias = jnp.where(near & (query_seg == key_seg), 0.0, masked_score).astype(f32)

    steps = len(grid.plane_bits)

    x_half = gather_near(grid, sent_tokens, line_bits[:1])
    table = gather_near(grid, table, grid.plane_bits[: steps // 2])
    down = group_step(down, 1)
    table, x_half, down, units = tie(table, x_half, down, units)
    x_far_half = swap(grid, x_half, line_bits[1])
    table = gather_near(grid, table, grid.plane_bits[steps // 2 :])
    units = group_step(units, 0)
    x_near = dot(jnp.concatenate([x_half, x_far_half]), to_near).astype(bf16)
    table, units, down, x_near, mask_bias, to_near, near_group, line_near, near_unit, to_piece = tie(
        table, units, down, x_near, mask_bias, to_near, near_group, line_near, near_unit, to_piece
    )
    table_far = swap(grid, table, grid.core_bit[0])
    down_near = plane_gather(down.reshape(-1, width))
    units = group_step(units, 1)

    query, own_pairs = call(
        qkv_kernel,
        [((line_len, columns), bf16), ((line_len, 2 * columns), bf16)],
        x_near,
        table,
        table_far,
        near_group,
        name="project",
    )
    own_pairs, table_far = tie(own_pairs, table_far)
    in_near = plane_gather(units.reshape(-1, ff_half))
    down_far = swap(grid, down_near, grid.plane_bits[-1])
    qkv_slice, out_line, params, ffn_row = call(
        functools.partial(unfold_kernel, small_each),
        [
            ((width, 3 * columns), bf16),
            ((width, width), bf16),
            ((8, width), f32),
            ((1, ff_half), f32),
        ],
        table,
        table_far,
        to_near,
        line_near,
        near_unit,
        name="unfold_weights",
    )
    ffn_row = outer_swap(ffn_row)
    kept_pairs, out_line, params, qkv_slice = tie(own_pairs, out_line, params, qkv_slice)
    far_pairs = swap(grid, own_pairs, part_bits[0])
    if parts > 2:
        far_pairs = gather_near(grid, jnp.concatenate([kept_pairs, far_pairs]), part_bits[1:])[line_len:]
    kept_pairs, far_pairs, in_near = tie(kept_pairs, far_pairs, in_near)
    pairs = (kept_pairs, far_pairs)
    in_far = swap(grid, in_near, grid.plane_bits[-1])
    in_near, in_far = outer_swap(in_near), outer_swap(in_far)

    att_pieces, logs = attention_forward(query, pairs, mask_bias)
    got_att = line_swap(grid, att_pieces[1:])
    attended = jnp.concatenate([att_pieces[0], *got_att], axis=1)
    attended_far = chip_swap(attended)

    half = width // 2
    chip_len = 2 * local_len
    weight_scratch = lambda *arrays: [pltpu.VMEM(a.shape, bf16) for a in arrays]
    first, normed, inverse, mixed, hidden, active, part_own, part_send = call(
        functools.partial(ffn_forward_kernel, kernel_flags, unit_block),
        [
            ((chip_len, width), f32),
            ((chip_len, width), f32),
            ((chip_len, 128), f32),
            ((chip_len, width), bf16),
            ((chip_len, ff_half), f32),
            ((chip_len, ff_half), bf16),
            ((chip_len, width), f32),
            ((chip_len, width), bf16),
        ],
        flag_row,
        attended,
        attended_far,
        tokens,
        got_pack,
        params,
        ffn_row,
        out_line,
        to_piece,
        in_near,
        in_far,
        down_near,
        down_far,
        name="ffn_forward",
        in_place=(7, 8, 9, 10, 11, 12),
        scratch=weight_scratch(out_line, to_piece, in_near, in_far, down_near, down_far)
        + [pltpu.SemaphoreType.DMA((6,))],
    )
    part_got = chip_swap(part_send)

    output, first_keep, first_send, d_second, d_hidden, sums_two, ffn_sums = call(
        functools.partial(ffn_backward_kernel, kernel_flags, unit_block),
        [
            ((local_len, width), bf16),
            ((local_len, width), f32),
            ((local_len, width), bf16),
            ((chip_len, width), bf16),
            ((chip_len, ff_half), bf16),
            ((8, width), f32),
            ((1, ff_half), f32),
        ],
        flag_row,
        part_own,
        part_got,
        first,
        cot,
        got_pack,
        hidden,
        params,
        to_piece,
        in_near,
        in_far,
        down_near,
        down_far,
        name="ffn_backward",
        in_place=(8, 9, 10, 11, 12),
        scratch=weight_scratch(to_piece, in_near, in_far, down_near, down_far)
        + [pltpu.SemaphoreType.DMA((5,))],
    )
    first_got = chip_swap(first_send)
    first_got, d_hidden, d_second = tie(first_got, d_hidden, d_second)
    down_send = dot(active[:, width:], d_second, 0, 0).astype(bf16)
    down_keep = dot(active[:, :width], d_second, 0, 0).astype(bf16)
    d_hidden, ffn_sums = outer_swap(d_hidden), outer_swap(ffn_sums)
    in_send = dot(mixed[:, half:], d_hidden, 0, 0).astype(bf16)
    in_keep = dot(mixed[:, :half], d_hidden, 0, 0).astype(bf16)
    d_one, d_branch, sums_one, *d_pieces = call(
        branch_backward_kernel,
        [((local_len, width), f32), ((local_len, width), bf16), ((8, width), f32)]
        + [((local_len, columns), bf16)] * groups,
        first_keep,
        first_got,
        normed[:local_len],
        inverse[:local_len],
        params,
        out_line,
        name="branch_backward",
    )
    got_d_att = line_swap(grid, d_pieces[1:])

    def far_sum(keep, send):
        return keep.astype(f32) + swap(grid, send, grid.plane_bits[-1]).astype(f32)

    down_total = far_sum(down_keep, down_send)
    in_total = far_sum(in_keep, in_send)

    def line_sum(total):
        for axis, bit in reversed(grid.group_bits):
            size = total.shape[0] // 2
            upper = (group >> bit) & 1
            keep = lax.dynamic_slice_in_dim(total, upper * size, size, 0)
            send = lax.dynamic_slice_in_dim(total, (1 - upper) * size, size, 0)
            got = swap(grid, send.astype(bf16), ((axis, bit), (axis, bit)))
            total = keep + got.astype(f32)
        return total

    (grad_out,) = call(
        branch_grads_kernel,
        [((width, width), bf16)],
        attended,
        d_branch,
        line_near,
        name="branch_gradients",
    )
    d_pieces[0], grad_out = tie(d_pieces[0], grad_out)

    d_query, pairs_own, pairs_send = attention_backward(
        query, pairs, mask_bias, [d_pieces[0], *got_d_att], att_pieces, logs
    )
    pairs_own, in_total = tie(pairs_own, in_total)
    in_total = reduce_near(grid, in_total, grid.plane_bits[:-1])
    if parts == 2:
        pairs_got = swap(grid, pairs_send, part_bits[0])
    else:
        pairs_all = jnp.concatenate([pairs_own, pairs_send.astype(f32)])
        pairs_own = reduce_near(grid, pairs_all, part_bits)
        pairs_got = jnp.zeros(pairs_own.shape, bf16)
    last_columns = table_width - 2 * columns - width
    (last_grads,) = call(
        functools.partial(query_grads_kernel, small_each),
        [((width, last_columns), f32)],
        x_near,
        d_query,
        near_group,
        sums_one,
        sums_two,
        ffn_sums,
        to_near,
        near_unit,
        name="query_gradients",
    )
    last_grads, down_total = tie(last_grads, down_total)
    down_total = reduce_near(grid, down_total, grid.plane_bits[:-1])
    grad_keep, grad_send, back_keep, back_send = call(
        pair_grads_kernel,
        [
            ((width // 2, table_width), bf16),
            ((width // 2, table_width), bf16),
            ((line_len // 2, width), f32),
            ((line_len // 2, width), bf16),
        ],
        x_near,
        pairs_own,
        pairs_got,
        d_query,
        near_group,
        qkv_slice,
        grad_out,
        last_grads,
        name="pair_gradients",
    )
    grad_send, down_total, in_total = tie(grad_send, down_total, in_total)
    sum_down = line_sum(down_total)
    in_pairs = line_sum(in_total)
    back = back_keep + swap(grid, back_send, line_bits[1]).astype(f32)
    back = reduce_near(grid, back, line_bits[:1])
    total = grad_keep.astype(f32) + chip_swap(grad_send).astype(f32)
    total = reduce_near(grid, total, grid.plane_bits)
    total, in_pairs, d_one = tie(total, in_pairs, d_one)
    in_got = chip_swap(in_pairs[rows_each:])
    (sum_in,) = call(
        functools.partial(units_kernel, unit_ids),
        [((rows_each, ff), f32)],
        place,
        in_pairs[:rows_each],
        in_got,
        name="order_units",
    )

    got_total = line_swap(
        grid, [total[k * rows_each : (k + 1) * rows_each].astype(bf16) for k in range(1, groups)]
    )
    input_grad = d_one + back
    sum_qkv, sum_out, sum_vec, sum_ffn, sum_gain, sum_shift = call(
        functools.partial(finish_kernel, small_each),
        [
            ((rows_each, 3 * width), f32),
            ((rows_each, width), f32),
            ((4, rows_each), f32),
            ((1, ff_each), f32),
            ((2, rows_each), f32),
            ((2, rows_each), f32),
        ],
        place,
        total[:rows_each],
        *got_total,
        name="finish",
    )
    return (
        output[None],
        input_grad[None],
        sum_qkv,
        sum_out,
        sum_in,
        sum_down,
        sum_vec,
        sum_ffn.reshape(ff_each),
        sum_gain,
        sum_shift,
    )


def solution(mesh):
    return jax.shard_map(
        functools.partial(on_device, Grid(mesh)),
        mesh=mesh,
        in_specs=(
            P("dp", "seq", None),
            P("dp", None),
            P("dp", None, None),
            P("dp", None, None),
            P(("dp", "seq"), None),
            P(("dp", "seq"), None),
            P(("dp", "seq"), None),
            P(("dp", "seq"), None),
            P(None, ("dp", "seq")),
            P(("dp", "seq")),
            P(None, ("dp", "seq")),
            P(None, ("dp", "seq")),
            P("dp", "seq", None),
        ),
        out_specs=(
            P("dp", "seq", None),
            P("dp", "seq", None),
            P(("dp", "seq"), None),
            P(("dp", "seq"), None),
            P(("dp", "seq"), None),
            P(("dp", "seq"), None),
            P(None, ("dp", "seq")),
            P(("dp", "seq")),
            P(None, ("dp", "seq")),
            P(None, ("dp", "seq")),
        ),
        check_vma=False,
    )
```

```python
import functools

import jax
import jax.numpy as jnp
import numpy as np
from jax import lax
from jax.experimental import pallas as pl
from jax.experimental.pallas import tpu as pltpu
from jax.sharding import PartitionSpec as P

HD = 64
BLK = 64
HEAD_GROUPS = 4
SCORE_CELLS = 512 * 1024

norm_eps = 1e-05
masked_score = -1e30
BOTH = ("dp", "seq")
bf16 = jnp.bfloat16
f32 = jnp.float32


def normalize(field_in):
    mean_row = jnp.mean(field_in, axis=-1, keepdims=True)
    centred = field_in - mean_row
    inverse = lax.rsqrt(jnp.mean(centred * centred, axis=-1, keepdims=True) + norm_eps)
    return (centred * inverse, inverse)


def norm_back(grad_in, normed, inverse, gain_row):
    weighted = grad_in * gain_row
    inner = jnp.mean(weighted * normed, axis=-1, keepdims=True)
    return inverse * (weighted - jnp.mean(weighted, axis=-1, keepdims=True) - normed * inner)


def gelu_slope(field_in):
    return (
        0.5 * (1.0 + lax.erf(field_in * 0.7071067811865476))
        + field_in * jnp.exp(-0.5 * field_in * field_in) * 0.3989422804014327
    )


def dot(left, right, left_dim=1, right_dim=0):
    return lax.dot_general(
        left, right, (((left_dim,), (right_dim,)), ((), ())), preferred_element_type=f32
    )


def call(body, outs, *args, name, scratch=(), flops=1e8, in_place=()):
    space = lambda i, a: (
        pl.ANY if i in in_place else pltpu.SMEM if a.dtype == jnp.int32 else pltpu.VMEM
    )
    specs = [pl.BlockSpec(memory_space=space(i, a)) for i, a in enumerate(args)]
    moved = sum(int(np.prod(a.shape)) * a.dtype.itemsize for a in args)
    return pl.pallas_call(
        body,
        in_specs=specs,
        out_specs=[pl.BlockSpec(memory_space=pltpu.VMEM)] * len(outs),
        out_shape=[jax.ShapeDtypeStruct(shape, dtype) for shape, dtype in outs],
        scratch_shapes=list(scratch),
        compiler_params=pltpu.CompilerParams(vmem_limit_bytes=56 * 1024 * 1024),
        cost_estimate=pl.CostEstimate(flops=int(flops), bytes_accessed=moved, transcendentals=0),
        name=name,
    )(*args)


def copies(pairs, sems):
    started = []
    for i, (source, target) in enumerate(pairs):
        copy = pltpu.make_async_copy(source, target, sems.at[i])
        copy.start()
        started.append(copy)
    return started


def exact(left, right, left_dim=1, right_dim=0):
    return lax.dot_general(
        left,
        right,
        (((left_dim,), (right_dim,)), ((), ())),
        preferred_element_type=f32,
        precision=lax.Precision.HIGHEST,
    )


def iota(shape, dim):
    return lax.broadcasted_iota(jnp.int32, shape, dim)


def spread_rows(row, rows, each):
    lanes = row.shape[1]
    picked = jnp.where(iota((rows, lanes), 1) // each == iota((rows, lanes), 0), row, 0.0)
    select = (iota((lanes, each), 0) % each == iota((lanes, each), 1)).astype(f32)
    return exact(picked, select)


def pick(options, index):
    chosen = options[0]
    for i, option in enumerate(options[1:]):
        chosen = jnp.where(index == i + 1, option, chosen)
    return chosen


def crossed(number):
    return (number % 2) * 2 + number // 2


def pack_kernel(
    unit_ids,
    place_ref,
    qkv_ref,
    out_ref,
    in_ref,
    x_ref,
    cot_ref,
    vec_ref,
    ffn_ref,
    gain_ref,
    shift_ref,
    *outs,
):
    core, group = place_ref[0], place_ref[1]
    rows, width = out_ref.shape
    columns = width // HEAD_GROUPS
    rolled = lambda g: [
        qkv_ref[:, kind * width + g * columns : kind * width + (g + 1) * columns] for kind in (1, 2, 0)
    ]
    by_group = [jnp.concatenate(rolled(g), axis=1) for g in range(HEAD_GROUPS)]
    same_row = (iota((rows, rows), 0) == iota((rows, rows), 1)).astype(bf16)
    turned = [dot(same_row, ref[...], 1, 1) for ref in (vec_ref, gain_ref, shift_ref)]
    turned.append(spread_rows(ffn_ref[...].astype(f32), rows, ffn_ref.shape[1] // rows))
    small = jnp.concatenate(turned, axis=1).astype(bf16)
    for k in range(HEAD_GROUPS):
        chosen = pick(by_group, group ^ crossed(k))
        rest = outs[k].shape[1] - 3 * columns - width - small.shape[1]
        outs[k][:, : 2 * columns] = chosen[:, : 2 * columns]
        outs[k][:, 2 * columns : 2 * columns + width] = out_ref[...]
        outs[k][:, 2 * columns + width :] = jnp.concatenate(
            [chosen[:, 2 * columns :], small, jnp.zeros((rows, rest), bf16)], axis=1
        )
    each = ffn_ref.shape[1]
    units = [
        jnp.concatenate([in_ref[:, i * each : (i + 1) * each] for i in ids], axis=1) for ids in unit_ids
    ]
    outs[HEAD_GROUPS][...] = jnp.where(core == 0, units[0], units[1])
    far = jnp.where(core == 0, units[1], units[0])
    far_ref = outs[HEAD_GROUPS + 1]
    tokens = x_ref.shape[0]
    top = far_ref.shape[0] - 2 * tokens
    blank = jnp.zeros((top - 2 * rows, width), bf16)
    far_ref[:top] = jnp.concatenate([far[:, :width], far[:, width:], blank][: 3 if top > 2 * rows else 2])
    far_ref[top : top + tokens] = x_ref[...]
    far_ref[top + tokens :] = cot_ref[...]


def unfold_kernel(
    small_each, table_ref, far_ref, near_ref, line_ref, unit_ref, qkv_ref, out_ref, par_ref, ffn_ref
):
    columns = qkv_ref.shape[1] // 3
    width = out_ref.shape[1]
    start, at = 2 * columns, 2 * columns + width
    near = near_ref[...]
    both = lambda i, j: jnp.concatenate([table_ref[:, i:j], far_ref[:, i:j]], axis=0)
    rest = both(at, table_ref.shape[1])
    qkv_ref[:, :start] = dot(near, both(0, start)).astype(bf16)
    qkv_ref[:, start:] = dot(near, rest[:, :columns]).astype(bf16)
    out_ref[...] = dot(line_ref[...], both(start, at)).astype(bf16)
    small = rest[:, columns : columns + 8 + small_each]
    par_ref[...] = dot(small[:, :8], near, 0, 1)
    by_slot = dot(small[:, 8:], unit_ref[...], 0, 0)
    slot = iota(by_slot.shape, 1) % small_each == iota(by_slot.shape, 0)
    ffn_ref[...] = jnp.sum(jnp.where(slot, by_slot, 0.0), axis=0, keepdims=True)


def qkv_kernel(x_ref, table_ref, far_ref, sel_ref, q_ref, pair_ref):
    columns = q_ref.shape[1]
    width = x_ref.shape[1]
    half = width // 2
    start, at = 2 * columns, 2 * columns + width
    pairs = dot(x_ref[:, :half], table_ref[:, :start]) + dot(x_ref[:, half:], far_ref[:, :start])
    rest = jnp.concatenate([table_ref[:, at:], far_ref[:, at:]], axis=0)
    biases = dot(rest[:, columns : columns + 8], sel_ref[...], 0, 0)
    values = pairs[:, columns:] + biases[1:2]
    pair_ref[...] = jnp.concatenate([pairs[:, :columns], values], axis=1).astype(bf16)
    queries = dot(x_ref[...], rest[:, :columns]) + biases[0:1]
    q_ref[...] = (queries * HD ** (-0.5)).astype(bf16)


def head_mask(shape, head):
    lane = iota(shape, 1)
    return (lane >= head * HD) & (lane < (head + 1) * HD)


def split_pairs(pair_refs, k_ref, v_ref):
    width = k_ref.shape[1]
    start = 0
    for ref in pair_refs:
        end = start + ref.shape[0]
        k_ref[start:end] = ref[:, :width]
        v_ref[start:end] = ref[:, width:]
        start = end


def forward_kernel(q_ref, kv_ref, far_ref, b_ref, *refs):
    *o_refs, l_ref, k_ref, v_ref = refs
    step = pl.program_id(0)

    @pl.when(step == 0)
    def _():
        split_pairs((kv_ref, far_ref), k_ref, v_ref)

    query, keys, values, bias = q_ref[...], k_ref[...], v_ref[...], b_ref[...]
    rows, width = query.shape
    out = jnp.zeros(query.shape, f32)
    logs = jnp.zeros(l_ref.shape, f32)
    for head in range(width // HD):
        mine = head_mask(query.shape, head)
        scores = dot(jnp.where(mine, query, jnp.zeros_like(query)), keys, 1, 1) + bias
        top = jnp.max(scores, axis=1, keepdims=True)
        terms = jnp.exp(scores - top)
        total = jnp.sum(terms, axis=1, keepdims=True)
        probs = (terms * (1.0 / total)).astype(bf16)
        out = out + jnp.where(mine, dot(probs, values), 0.0)
        logs = jnp.where(iota(l_ref.shape, 1) == head, top + jnp.log(total), logs)
    l_ref[...] = logs
    low = out.astype(bf16)
    piece = o_refs[0].shape[0]
    each = rows // piece
    for k, o_ref in enumerate(o_refs):
        start = (k % each) * piece

        @pl.when(step == k // each)
        def _(o_ref=o_ref, start=start):
            o_ref[...] = low[start : start + piece]


def backward_kernel(q_ref, kv_ref, far_ref, b_ref, *refs):
    pieces, att_refs, refs = refs[:HEAD_GROUPS], refs[HEAD_GROUPS : 2 * HEAD_GROUPS], refs[2 * HEAD_GROUPS :]
    l_ref, dq_ref, own_ref, send_ref, k_ref, v_ref, d_ref, o_ref, dk_ref, dv_ref = refs
    step = pl.program_id(0)
    rows, width = q_ref.shape

    @pl.when(step == 0)
    def _():
        split_pairs((kv_ref, far_ref), k_ref, v_ref)
        dk_ref[...] = jnp.zeros(dk_ref.shape, f32)
        dv_ref[...] = jnp.zeros(dv_ref.shape, f32)
        piece = pieces[0].shape[0]
        for k, ref in enumerate(pieces):
            d_ref[k * piece : (k + 1) * piece] = ref[...]
            o_ref[k * piece : (k + 1) * piece] = att_refs[k][...]

    query, keys, values, bias = q_ref[...], k_ref[...], v_ref[...], b_ref[...]
    here = pl.ds(pl.multiple_of(step * rows, rows), rows)
    d_att = d_ref[here]
    products = d_att.astype(f32) * o_ref[here].astype(f32)
    logs = l_ref[...]
    d_query = jnp.zeros(query.shape, f32)
    for head in range(width // HD):
        mine = head_mask(query.shape, head)
        q_head = jnp.where(mine, query, jnp.zeros_like(query))
        d_head = jnp.where(mine, d_att, jnp.zeros_like(d_att))
        scores = dot(q_head, keys, 1, 1) + bias
        weights = jnp.exp(scores - logs[:, head : head + 1])
        d_probs = dot(d_head, values, 1, 1)
        delta = jnp.sum(jnp.where(mine, products, 0.0), axis=1, keepdims=True)
        d_scores = (weights * (d_probs - delta)).astype(bf16)
        d_query = d_query + jnp.where(mine, dot(d_scores, keys), 0.0)
        dk_ref[...] += dot(d_scores, q_head, 0, 0)
        dv_ref[...] += dot(weights.astype(bf16), d_head, 0, 0)
    dq_ref[...] = (d_query * HD ** (-0.5)).astype(bf16)

    @pl.when(step == pl.num_programs(0) - 1)
    def _():
        kept = own_ref.shape[0]
        own_ref[:, :width] = dk_ref[:kept]
        own_ref[:, width:] = dv_ref[:kept]
        send_ref[:, :width] = dk_ref[kept:].astype(bf16)
        send_ref[:, width:] = dv_ref[kept:].astype(bf16)


def attention_forward(query, pairs, bias):
    rows, width = query.shape
    key_rows = sum(a.shape[0] for a in pairs)
    tile = min(rows, SCORE_CELLS // key_rows)
    piece = rows // HEAD_GROUPS
    results = pl.pallas_call(
        forward_kernel,
        grid=(rows // tile,),
        in_specs=[
            pl.BlockSpec((tile, width), lambda i: (i, 0)),
            *[pl.BlockSpec(a.shape, lambda i: (0, 0)) for a in pairs],
            pl.BlockSpec((tile, key_rows), lambda i: (i, 0)),
        ],
        out_specs=[pl.BlockSpec((piece, width), lambda i: (0, 0))] * HEAD_GROUPS
        + [pl.BlockSpec((tile, 128), lambda i: (i, 0))],
        out_shape=[jax.ShapeDtypeStruct((piece, width), bf16)] * HEAD_GROUPS
        + [jax.ShapeDtypeStruct((rows, 128), f32)],
        scratch_shapes=[pltpu.VMEM((key_rows, width), bf16)] * 2,
        compiler_params=pltpu.CompilerParams(vmem_limit_bytes=56 * 1024 * 1024),
        cost_estimate=pl.CostEstimate(
            flops=16 * rows * key_rows * width, bytes_accessed=4 * rows * key_rows, transcendentals=0
        ),
        name="attention_forward",
    )(query, *pairs, bias)
    return results[:-1], results[-1]


def attention_backward(query, pairs, bias, d_pieces, att_pieces, logs):
    rows, width = query.shape
    key_rows = sum(a.shape[0] for a in pairs)
    tile = min(rows, SCORE_CELLS // key_rows)
    fixed = lambda n: pl.BlockSpec((n, 2 * width), lambda i: (0, 0))
    return pl.pallas_call(
        backward_kernel,
        grid=(rows // tile,),
        in_specs=[
            pl.BlockSpec((tile, width), lambda i: (i, 0)),
            *[pl.BlockSpec(a.shape, lambda i: (0, 0)) for a in pairs],
            pl.BlockSpec((tile, key_rows), lambda i: (i, 0)),
        ]
        + [pl.BlockSpec(d_pieces[0].shape, lambda i: (0, 0))] * (2 * HEAD_GROUPS)
        + [pl.BlockSpec((tile, 128), lambda i: (i, 0))],
        out_specs=[
            pl.BlockSpec((tile, width), lambda i: (i, 0)),
            fixed(rows),
            fixed(key_rows - rows),
        ],
        out_shape=[
            jax.ShapeDtypeStruct((rows, width), bf16),
            jax.ShapeDtypeStruct((rows, 2 * width), f32),
            jax.ShapeDtypeStruct((key_rows - rows, 2 * width), bf16),
        ],
        scratch_shapes=[pltpu.VMEM((key_rows, width), bf16)] * 2
        + [pltpu.VMEM((rows, width), bf16)] * 2
        + [pltpu.VMEM((key_rows, width), f32)] * 2,
        compiler_params=pltpu.CompilerParams(vmem_limit_bytes=56 * 1024 * 1024),
        cost_estimate=pl.CostEstimate(
            flops=30 * rows * key_rows * width, bytes_accessed=4 * rows * key_rows, transcendentals=0
        ),
        name="attention_backward",
    )(query, *pairs, bias, *d_pieces, *att_pieces, logs)


def swap_blocks(a, flags, block):
    for step, flag in enumerate(flags):
        size = block << step
        blocks = [a[:, i : i + size] for i in range(0, a.shape[1], size)]
        flipped = [blocks[i ^ 1] for i in range(len(blocks))]
        a = jnp.where(flag == 1, jnp.concatenate(flipped, axis=1), a)
    return a


def ffn_forward_kernel(
    flag_count,
    block,
    flag_ref,
    att_ref,
    att_far_ref,
    x_ref,
    far_ref,
    par_ref,
    ffn_ref,
    out_hbm,
    mix_hbm,
    in_near_hbm,
    in_far_hbm,
    down_near_hbm,
    down_far_hbm,
    first_ref,
    normed_ref,
    inverse_ref,
    mixed_ref,
    hidden_ref,
    active_ref,
    part_ref,
    send_ref,
    out_ref,
    mix_ref,
    in_near_ref,
    in_far_ref,
    down_near_ref,
    down_far_ref,
    sems,
):
    waits = copies(
        [
            (out_hbm, out_ref),
            (mix_hbm, mix_ref),
            (in_near_hbm, in_near_ref),
            (in_far_hbm, in_far_ref),
            (down_near_hbm, down_near_ref),
            (down_far_hbm, down_far_ref),
        ],
        sems,
    )
    flags = [flag_ref[i] for i in range(flag_count)]
    attended = jnp.concatenate([att_ref[...], att_far_ref[...]], axis=0)
    rows = x_ref.shape[0]
    top = far_ref.shape[0] - 2 * rows
    tokens = jnp.concatenate([x_ref[...], far_ref[top : top + rows]], axis=0).astype(f32)
    waits[0].wait()
    branch = dot(attended, out_ref[...]) + par_ref[2:3]
    normed, inverse = normalize(tokens + branch)
    first = normed * par_ref[4:5] + par_ref[6:7]
    first_ref[...] = first
    normed_ref[...] = normed
    inverse_ref[...] = jnp.broadcast_to(inverse, inverse_ref.shape)
    waits[1].wait()
    mixed = dot(first.astype(bf16), mix_ref[...]).astype(bf16)
    mixed_ref[...] = mixed
    half = mixed.shape[1] // 2
    waits[2].wait()
    hidden = dot(mixed[:, :half], in_near_ref[...])
    waits[3].wait()
    hidden = hidden + dot(mixed[:, half:], in_far_ref[...]) + ffn_ref[...]
    hidden = swap_blocks(hidden, flags, block)
    hidden_ref[...] = hidden
    active = (0.5 * hidden * (1.0 + lax.erf(hidden * 0.7071067811865476))).astype(bf16)
    active_ref[...] = active
    units = active.shape[1] // 2
    waits[4].wait()
    part = dot(active[:, :units], down_near_ref[...])
    waits[5].wait()
    part = part + dot(active[:, units:], down_far_ref[...])
    part_ref[...] = part
    send_ref[...] = part.astype(bf16)


def column_sum(a):
    return jnp.sum(a, axis=0, keepdims=True)


def ffn_backward_kernel(
    flag_count,
    block,
    flag_ref,
    part_ref,
    got_ref,
    first_ref,
    cot_ref,
    far_ref,
    hidden_ref,
    par_ref,
    mix_hbm,
    in_near_hbm,
    in_far_hbm,
    down_near_hbm,
    down_far_hbm,
    output_ref,
    keep_ref,
    send_ref,
    second_ref,
    d_hidden_ref,
    sums_ref,
    ffn_sum_ref,
    mix_ref,
    in_near_ref,
    in_far_ref,
    down_near_ref,
    down_far_ref,
    sems,
):
    waits = copies(
        [
            (down_near_hbm, down_near_ref),
            (down_far_hbm, down_far_ref),
            (in_near_hbm, in_near_ref),
            (in_far_hbm, in_far_ref),
            (mix_hbm, mix_ref),
        ],
        sems,
    )
    flags = [flag_ref[i] for i in range(flag_count)]
    rows = got_ref.shape[0] // 2
    other = jnp.concatenate([got_ref[rows:], got_ref[:rows]], axis=0).astype(f32)
    normed, inverse = normalize(first_ref[...] + part_ref[...] + other + par_ref[3:4])
    gain = par_ref[5:6]
    output_ref[...] = (normed[:rows] * gain + par_ref[7:8]).astype(bf16)
    out_grad = jnp.concatenate([cot_ref[...], far_ref[far_ref.shape[0] - rows :]], axis=0).astype(f32)
    d_two = norm_back(out_grad, normed, inverse, gain)
    d_second = d_two.astype(bf16)
    second_ref[...] = d_second
    sums_ref[...] = jnp.concatenate(
        [
            column_sum(out_grad[:rows] * normed[:rows]),
            column_sum(out_grad[:rows]),
            column_sum(d_second[:rows].astype(f32)),
            jnp.zeros((5, normed.shape[1]), f32),
        ],
        axis=0,
    )
    waits[0].wait()
    near = dot(d_second, down_near_ref[...], 1, 1)
    waits[1].wait()
    far = dot(d_second, down_far_ref[...], 1, 1)
    slope = gelu_slope(hidden_ref[...])
    d_hidden = jnp.concatenate([near, far], axis=1) * slope
    d_hidden = swap_blocks(d_hidden, flags, block).astype(bf16)
    d_hidden_ref[...] = d_hidden
    ffn_sum_ref[...] = column_sum(d_hidden.astype(f32))
    waits[2].wait()
    near = dot(d_hidden, in_near_ref[...], 1, 1).astype(bf16)
    waits[3].wait()
    far = dot(d_hidden, in_far_ref[...], 1, 1).astype(bf16)
    waits[4].wait()
    part = dot(jnp.concatenate([near, far], axis=1), mix_ref[...], 1, 1)
    keep_ref[...] = d_two[:rows] + part[:rows]
    send_ref[...] = part[rows:].astype(bf16)


def branch_backward_kernel(
    keep_ref, got_ref, normed_ref, inverse_ref, par_ref, out_ref, d_one_ref, branch_ref, sums_ref, *pieces
):
    d_first = keep_ref[...] + got_ref[...].astype(f32)
    normed, inverse = normed_ref[...], inverse_ref[:, :1]
    d_one = norm_back(d_first, normed, inverse, par_ref[4:5])
    d_one_ref[...] = d_one
    d_branch = d_one.astype(bf16)
    branch_ref[...] = d_branch
    sums_ref[...] = jnp.concatenate(
        [
            column_sum(d_first * normed),
            column_sum(d_first),
            column_sum(d_branch.astype(f32)),
            jnp.zeros((5, normed.shape[1]), f32),
        ],
        axis=0,
    )
    d_attended = dot(d_branch, out_ref[...], 1, 1).astype(bf16)
    columns = pieces[0].shape[1]
    for k, piece in enumerate(pieces):
        piece[...] = d_attended[:, k * columns : (k + 1) * columns]


def branch_grads_kernel(att_ref, branch_ref, line_ref, out_ref):
    attended = dot(att_ref[...], line_ref[...]).astype(bf16)
    out_ref[...] = dot(attended, branch_ref[...], 0, 0).astype(bf16)


def query_grads_kernel(
    small_each,
    x_ref,
    dq_ref,
    sel_ref,
    sums_ref,
    sums_two_ref,
    ffn_ref,
    near_ref,
    unit_ref,
    last_ref,
):
    columns = dq_ref.shape[1]
    d_query = dq_ref[...]
    queries = dot(x_ref[...], d_query, 0, 0)
    sums = jnp.concatenate([column_sum(d_query.astype(f32)), jnp.zeros((7, columns), f32)], axis=0)
    bias = dot(sel_ref[...], sums.astype(bf16), 1, 1)
    first, second = sums_ref[...], sums_two_ref[...]
    blank = jnp.zeros((2, first.shape[1]), f32)
    vectors = jnp.concatenate(
        [blank, first[2:3], second[2:3], first[0:1], second[0:1], first[1:2], second[1:2]], axis=0
    )
    vectors = dot(near_ref[...], vectors.astype(bf16), 0, 1) + bias
    units = ffn_ref.shape[1]
    slot = iota((8, units), 1) % small_each == iota((8, units), 0)
    by_slot = jnp.where(slot, ffn_ref[...], 0.0).astype(bf16)
    ffn = dot(unit_ref[...], by_slot, 1, 1)
    rest = last_ref.shape[1] - columns - 16
    last = [queries, vectors, ffn, jnp.zeros((queries.shape[0], rest), f32)]
    last_ref[...] = jnp.concatenate(last, axis=1)


def pair_grads_kernel(
    x_ref,
    own_ref,
    got_ref,
    dq_ref,
    sel_ref,
    qkv_ref,
    out_ref,
    last_ref,
    keep_ref,
    send_ref,
    back_ref,
    back_send_ref,
):
    pair_columns = own_ref.shape[1]
    columns = pair_columns // 2
    width = x_ref.shape[1]
    half = width // 2
    at = pair_columns + width
    d_pairs = (own_ref[...] + got_ref[...].astype(f32)).astype(bf16)
    pairs = dot(x_ref[...], d_pairs, 0, 0).astype(bf16)
    sums = [jnp.zeros((1, columns), f32), column_sum(d_pairs[:, columns:].astype(f32))]
    sums = jnp.concatenate([*sums, jnp.zeros((6, columns), f32)], axis=0)
    bias = dot(sel_ref[...], sums.astype(bf16), 1, 1)[:, 1:2]
    last = last_ref[...]
    last = (last + jnp.where(iota(last.shape, 1) == columns + 1, bias, 0.0)).astype(bf16)
    for ref, rows in ((send_ref, slice(half, width)), (keep_ref, slice(0, half))):
        ref[:, :pair_columns] = pairs[rows]
        ref[:, pair_columns:at] = out_ref[rows]
        ref[:, at:] = last[rows]
    grad_back = dot(dq_ref[...], qkv_ref[:, pair_columns:], 1, 1)
    grad_back = grad_back + dot(d_pairs, qkv_ref[:, :pair_columns], 1, 1)
    rows = back_ref.shape[0]
    back_ref[...] = grad_back[:rows]
    back_send_ref[...] = grad_back[rows:].astype(bf16)


def finish_kernel(small_each, place_ref, own_ref, *refs):
    pieces, outs = refs[: HEAD_GROUPS - 1], refs[HEAD_GROUPS - 1 :]
    qkv_ref, out_ref, vec_ref, ffn_ref, gain_ref, shift_ref = outs
    group = place_ref[1]
    rows, width = out_ref.shape
    columns = width // HEAD_GROUPS
    line = [own_ref[...]] + [piece[...].astype(f32) for piece in pieces]
    at = 2 * columns + width
    for g in range(HEAD_GROUPS):
        source = crossed(group ^ g)
        pairs = pick([a[:, : 2 * columns] for a in line], source)
        queries = pick([a[:, at : at + columns] for a in line], source)
        for kind, mine in enumerate((queries, pairs[:, :columns], pairs[:, columns:])):
            start = kind * width + g * columns
            qkv_ref[:, start : start + columns] = mine
    out_ref[...] = sum(a[:, 2 * columns : at] for a in line)
    rest = sum(a[:, at:] for a in line)
    small = rest[:, columns : columns + 8 + small_each]
    same_row = (iota((rows, rows), 0) == iota((rows, rows), 1)).astype(f32)
    turned = exact(small[:, :8], same_row, 0, 0)
    vec_ref[...] = turned[:4]
    gain_ref[...] = turned[4:6]
    shift_ref[...] = turned[6:8]
    each = small.shape[1] - 8
    lanes = rows * each
    select = (iota((each, lanes), 1) % each == iota((each, lanes), 0)).astype(f32)
    wide = exact(small[:, 8:], select)
    mine = iota((rows, lanes), 1) // each == iota((rows, lanes), 0)
    ffn_ref[...] = column_sum(jnp.where(mine, wide, 0.0))


def units_kernel(unit_ids, place_ref, keep_ref, got_ref, out_ref):
    count = 2 * len(unit_ids[0])
    each = out_ref.shape[1] // count
    for core in range(2):

        @pl.when(place_ref[0] == core)
        def _(core=core):
            keep, got = keep_ref[...], got_ref[...].astype(f32)
            blocks = {}
            for ids, source in ((unit_ids[core], keep), (unit_ids[1 - core], got)):
                for slot, device in enumerate(ids):
                    blocks[int(device)] = source[:, slot * each : (slot + 1) * each]
            out_ref[...] = jnp.concatenate([blocks[i] for i in range(count)], axis=1)


class Grid:
    def __init__(self, mesh):
        self.dp, self.seq = mesh.shape["dp"], mesh.shape["seq"]
        self.count = self.dp * self.seq
        self.xs, self.parts = self.dp // 2, self.seq // HEAD_GROUPS
        bits = lambda axis, size: [(axis, b) for b in range(size.bit_length() - 1)]
        x_bits, self.part_bits = bits("x", self.xs), bits("q", self.parts)
        self.group_bits = [("g", 1), ("g", 0)]
        alternate = len(x_bits) == len(self.part_bits)
        self.plane = (
            x_bits + self.part_bits,
            self.part_bits + x_bits if alternate else x_bits + self.part_bits,
        )
        self.core_bit = [(("c", 0), ("c", 0))]
        self.plane_bits = list(zip(*self.plane))

    def place(self, device):
        dp, seq = divmod(device, self.seq)
        return {"x": dp // 2, "c": dp % 2, "g": seq // self.parts, "q": seq % self.parts}

    def device(self, at):
        return (at["x"] * 2 + at["c"]) * self.seq + at["g"] * self.parts + at["q"]

    def flip(self, bits_of_core):
        pairs = []
        for device in range(self.count):
            at = self.place(device)
            axis, bit = bits_of_core[at["c"]]
            at[axis] ^= 1 << bit
            pairs.append((device, self.device(at)))
        return pairs

    def cross(self, by):
        pairs = []
        for device in range(self.count):
            at = self.place(device)
            at["g"] ^= by
            pairs.append((device, self.device(at)))
        return pairs

    def plane_masks(self, core):
        masks = {"x": [], "q": []}
        for index in range(self.xs * self.parts):
            for axis in masks:
                flips = [
                    1 << bit
                    for step, (a, bit) in enumerate(self.plane[core])
                    if a == axis and (index >> step) & 1
                ]
                masks[axis].append(sum(flips))
        return {axis: np.array(m, np.int32) for axis, m in masks.items()}


def same(bits):
    return [(bit, bit) for bit in bits]


def swap(grid, held, bits):
    return lax.ppermute(held, BOTH, grid.flip(bits))


def gather_near(grid, held, bit_pairs):
    for pair in bit_pairs:
        held = jnp.concatenate([held, swap(grid, held, pair)], axis=0)
    return held


def reduce_near(grid, total, bit_pairs):
    for pair in reversed(bit_pairs):
        half = total.shape[0] // 2
        got = swap(grid, total[half:].astype(bf16), pair)
        total = total[:half].astype(f32) + got.astype(f32)
    return total


def line_swap(grid, pieces):
    return [
        lax.ppermute(piece, BOTH, grid.cross(crossed(k + 1))) for k, piece in enumerate(pieces)
    ]


def tie(*values):
    return lax.optimization_barrier(values)


def on_device(
    grid,
    inputs,
    segments,
    rand_blocks,
    glob_blocks,
    w_qkv,
    w_out,
    w_in,
    w_down,
    vec_bias,
    ffn_bias,
    norm_gain,
    norm_shift,
    cotangent,
):
    local_len, width = inputs.shape[1:]
    rows_each, ff_each = w_in.shape[0], w_down.shape[0]
    ff = w_in.shape[1]
    ff_half = ff // 2
    groups, parts, xs = HEAD_GROUPS, grid.parts, grid.xs
    planes = xs * parts
    columns = width // groups
    line_len = groups * local_len
    small_each = ff_each // rows_each
    table_width = -(-(3 * columns + width + 8 + small_each) // 128) * 128
    dp_place, seq_place = lax.axis_index("dp"), lax.axis_index("seq")
    core, group, part = dp_place % 2, seq_place // parts, seq_place % parts
    coords = {"x": dp_place // 2, "c": core, "g": group, "q": part}
    place = jnp.stack([core, group]).astype(jnp.int32)
    chip_swap = lambda a: swap(grid, a, grid.core_bit[0])
    group_order = np.array([0, 2, 1, 3])
    group_slot = lambda g: (g % 2) * 2 + g // 2
    tokens = inputs.reshape(local_len, width)
    cot = cotangent.reshape(local_len, width)
    part_bits = same(grid.part_bits)

    masks = [grid.plane_masks(c) for c in range(2)]
    unit_ids = []
    for c in range(2):
        ids = [
            grid.device({"x": masks[c]["x"][index], "c": c, "g": g, "q": masks[c]["q"][index]})
            for index in range(planes)
            for g in group_order
        ]
        unit_ids.append(np.array(ids))

    far_top = -(-2 * rows_each // 16) * 16
    *packets, own_units, far_pack = call(
        functools.partial(pack_kernel, unit_ids),
        [((rows_each, table_width), bf16)] * groups
        + [((rows_each, ff_half), bf16), ((far_top + 2 * local_len, width), bf16)],
        place,
        w_qkv,
        w_out,
        w_in,
        tokens,
        cot,
        vec_bias,
        ffn_bias.reshape(1, ff_each),
        norm_gain,
        norm_shift,
        name="pack_weights",
        scratch=(),
    )
    got_packets = line_swap(grid, packets[1:])

    plane_x = [coords["x"] ^ jnp.asarray(masks[c]["x"]) for c in range(2)]
    plane_q = [part ^ jnp.asarray(masks[c]["q"]) for c in range(2)]
    line_groups = group ^ jnp.asarray(group_order, jnp.int32)
    row = jnp.arange(rows_each, dtype=jnp.int32)
    row_ids = jnp.arange(width, dtype=jnp.int32)
    by_core = lambda c, pair: jnp.where(c == 0, pair[0], pair[1])

    def device_of(x, c, g, q):
        return (x * 2 + c) * grid.seq + g * parts + q

    near_ids = jnp.stack(
        [
            device_of(by_core(c, plane_x)[:, None], c, line_groups[None, :], by_core(c, plane_q)[:, None])
            for c in (core, 1 - core)
        ]
    )
    def group_step(held, entry):
        axis, bit = grid.group_bits[entry]
        got = swap(grid, held, ((axis, bit), (axis, bit)))
        upper = (group >> bit) & 1 == 1
        return jnp.where(upper, jnp.concatenate([got, held]), jnp.concatenate([held, got]))

    def plane_gather(held):
        for pair in grid.plane_bits[:-1]:
            held = jnp.concatenate([held, swap(grid, held, pair)], axis=0)
        return held

    line_bits = same(grid.group_bits)
    got_pack = chip_swap(far_pack)
    got_units = jnp.concatenate([got_pack[:rows_each], got_pack[rows_each : 2 * rows_each]], axis=1)
    table = jnp.concatenate([packets[0], *got_packets], axis=0)
    units = jnp.concatenate([own_units, got_units], axis=0)[None]
    down = group_step(w_down[None], 0)
    table, units, down, sent_tokens, near_ids, line_groups, segments = tie(
        table, units, down, tokens, near_ids, line_groups, segments
    )
    near_rows = (near_ids[..., None] * rows_each + row).reshape(width)
    to_near = (row_ids[:, None] == near_rows[None, :]).astype(bf16)
    line_rows = jnp.repeat(line_groups, columns) * columns + row_ids % columns
    line_near = (line_rows[:, None] == near_rows[None, :]).astype(bf16)
    group_rows = group * columns + jnp.arange(columns, dtype=jnp.int32)
    near_group = (near_rows[:, None] == group_rows[None, :]).astype(bf16)
    own_x, own_q = by_core(core, plane_x), by_core(core, plane_q)
    slot_groups = jnp.asarray(group_order, jnp.int32)
    piece_ids = jnp.stack(
        [
            device_of(own_x[:, None], c, slot_groups[None, :], own_q[:, None])
            for c in (core, 1 - core)
        ],
        axis=2,
    )
    piece_rows = (piece_ids[..., None] * rows_each + row).reshape(width)
    to_piece = (row_ids[:, None] == piece_rows[None, :]).astype(bf16)
    own_ids = by_core(core, [jnp.asarray(ids, jnp.int32) for ids in unit_ids])
    unit = jnp.arange(ff_half, dtype=jnp.int32)
    unit_rows = jnp.repeat(own_ids, ff_each) * rows_each + (unit % ff_each) // small_each
    near_unit = (near_rows[:, None] == unit_rows[None, :]).astype(bf16)

    flags = [
        by_core(core, [(coords[axis] >> bit) & 1 for axis, bit in pair]) for pair in grid.plane_bits
    ]
    unit_block = ff_half // planes
    aligned = unit_block % 128 == 0
    kernel_flags = len(flags) if aligned else 0
    flag_row = jnp.stack(flags).astype(jnp.int32)
    outer_swap = (lambda a: a) if aligned else (lambda a: swap_blocks(a, flags, unit_block))

    own_blocks = local_len // BLK
    part_near = part ^ jnp.arange(parts, dtype=jnp.int32)
    chunk_ids = (line_groups[None, :] * parts + part_near[:, None]).reshape(-1)
    chunk_hot = chunk_ids[:, None] == jnp.arange(grid.seq, dtype=jnp.int32)[None, :]

    def take_chunks(chunks, hot):
        return jnp.sum(jnp.where(hot[:, :, None], chunks[None], 0), axis=1)

    offsets = jnp.arange(local_len, dtype=jnp.int32) // BLK
    block_near = (chunk_ids[:, None] * own_blocks + offsets[None, :]).reshape(-1)
    seg_near = take_chunks(segments.reshape(grid.seq, local_len), chunk_hot).reshape(-1)
    rand_line = take_chunks(rand_blocks.reshape(grid.seq, -1), chunk_hot[:groups])
    rand_line = rand_line.reshape(groups, own_blocks, 1, -1)
    rand_rows = jnp.broadcast_to(rand_line, (groups, own_blocks, BLK, rand_line.shape[-1]))
    rand_rows = rand_rows.reshape(line_len, -1)
    key_block, key_seg = block_near[None, :], seg_near[None, :]
    query_block, query_seg = block_near[:line_len, None], seg_near[:line_len, None]
    near = (key_block >= query_block - 1) & (key_block <= query_block + 1)
    for entry in range(rand_rows.shape[1]):
        near = near | (key_block == rand_rows[:, entry : entry + 1])
    glob_table = glob_blocks[0]
    doc = jnp.arange(glob_table.shape[0], dtype=jnp.int32)[None, :]
    for entry in range(glob_table.shape[1]):
        picked = jnp.sum(
            jnp.where(query_seg == doc, glob_table[None, :, entry], 0), axis=1, keepdims=True
        )
        near = near | (key_block == picked)
    mask_bias = jnp.where(near & (query_seg == key_seg), 0.0, masked_score).astype(f32)

    steps = len(grid.plane_bits)

    x_half = gather_near(grid, sent_tokens, line_bits[:1])
    table = gather_near(grid, table, grid.plane_bits[: steps // 2])
    down = group_step(down, 1)
    table, x_half, down, units = tie(table, x_half, down, units)
    x_far_half = swap(grid, x_half, line_bits[1])
    table = gather_near(grid, table, grid.plane_bits[steps // 2 :])
    units = group_step(units, 0)
    x_near = dot(jnp.concatenate([x_half, x_far_half]), to_near).astype(bf16)
    table, units, down, x_near, mask_bias, to_near, near_group, line_near, near_unit, to_piece = tie(
        table, units, down, x_near, mask_bias, to_near, near_group, line_near, near_unit, to_piece
    )
    table_far = swap(grid, table, grid.core_bit[0])
    down_near = plane_gather(down.reshape(-1, width))
    units = group_step(units, 1)

    query, own_pairs = call(
        qkv_kernel,
        [((line_len, columns), bf16), ((line_len, 2 * columns), bf16)],
        x_near,
        table,
        table_far,
        near_group,
        name="project",
    )
    own_pairs, table_far = tie(own_pairs, table_far)
    in_near = plane_gather(units.reshape(-1, ff_half))
    down_far = swap(grid, down_near, grid.plane_bits[-1])
    qkv_slice, out_line, params, ffn_row = call(
        functools.partial(unfold_kernel, small_each),
        [
            ((width, 3 * columns), bf16),
            ((width, width), bf16),
            ((8, width), f32),
            ((1, ff_half), f32),
        ],
        table,
        table_far,
        to_near,
        line_near,
        near_unit,
        name="unfold_weights",
    )
    ffn_row = outer_swap(ffn_row)
    kept_pairs, out_line, params, qkv_slice = tie(own_pairs, out_line, params, qkv_slice)
    far_pairs = swap(grid, own_pairs, part_bits[0])
    if parts > 2:
        far_pairs = gather_near(grid, jnp.concatenate([kept_pairs, far_pairs]), part_bits[1:])[line_len:]
    kept_pairs, far_pairs, in_near = tie(kept_pairs, far_pairs, in_near)
    pairs = (kept_pairs, far_pairs)
    in_far = swap(grid, in_near, grid.plane_bits[-1])
    in_near, in_far = outer_swap(in_near), outer_swap(in_far)

    att_pieces, logs = attention_forward(query, pairs, mask_bias)
    got_att = line_swap(grid, att_pieces[1:])
    attended = jnp.concatenate([att_pieces[0], *got_att], axis=1)
    attended_far = chip_swap(attended)

    half = width // 2
    chip_len = 2 * local_len
    weight_scratch = lambda *arrays: [pltpu.VMEM(a.shape, bf16) for a in arrays]
    first, normed, inverse, mixed, hidden, active, part_own, part_send = call(
        functools.partial(ffn_forward_kernel, kernel_flags, unit_block),
        [
            ((chip_len, width), f32),
            ((chip_len, width), f32),
            ((chip_len, 128), f32),
            ((chip_len, width), bf16),
            ((chip_len, ff_half), f32),
            ((chip_len, ff_half), bf16),
            ((chip_len, width), f32),
            ((chip_len, width), bf16),
        ],
        flag_row,
        attended,
        attended_far,
        tokens,
        got_pack,
        params,
        ffn_row,
        out_line,
        to_piece,
        in_near,
        in_far,
        down_near,
        down_far,
        name="ffn_forward",
        in_place=(7, 8, 9, 10, 11, 12),
        scratch=weight_scratch(out_line, to_piece, in_near, in_far, down_near, down_far)
        + [pltpu.SemaphoreType.DMA((6,))],
    )
    part_got = chip_swap(part_send)

    output, first_keep, first_send, d_second, d_hidden, sums_two, ffn_sums = call(
        functools.partial(ffn_backward_kernel, kernel_flags, unit_block),
        [
            ((local_len, width), bf16),
            ((local_len, width), f32),
            ((local_len, width), bf16),
            ((chip_len, width), bf16),
            ((chip_len, ff_half), bf16),
            ((8, width), f32),
            ((1, ff_half), f32),
        ],
        flag_row,
        part_own,
        part_got,
        first,
        cot,
        got_pack,
        hidden,
        params,
        to_piece,
        in_near,
        in_far,
        down_near,
        down_far,
        name="ffn_backward",
        in_place=(8, 9, 10, 11, 12),
        scratch=weight_scratch(to_piece, in_near, in_far, down_near, down_far)
        + [pltpu.SemaphoreType.DMA((5,))],
    )
    first_got = chip_swap(first_send)
    first_got, d_hidden = tie(first_got, d_hidden)
    d_hidden, ffn_sums = outer_swap(d_hidden), outer_swap(ffn_sums)
    in_send = dot(mixed[:, half:], d_hidden, 0, 0).astype(bf16)
    in_keep = dot(mixed[:, :half], d_hidden, 0, 0).astype(bf16)
    d_one, d_branch, sums_one, *d_pieces = call(
        branch_backward_kernel,
        [((local_len, width), f32), ((local_len, width), bf16), ((8, width), f32)]
        + [((local_len, columns), bf16)] * groups,
        first_keep,
        first_got,
        normed[:local_len],
        inverse[:local_len],
        params,
        out_line,
        name="branch_backward",
    )
    got_d_att = line_swap(grid, d_pieces[1:])
    d_branch, d_second = tie(d_branch, d_second)
    down_send = dot(active[:, width:], d_second, 0, 0).astype(bf16)
    down_keep = dot(active[:, :width], d_second, 0, 0).astype(bf16)

    def far_sum(keep, send):
        return keep.astype(f32) + swap(grid, send, grid.plane_bits[-1]).astype(f32)

    down_total = far_sum(down_keep, down_send)
    in_total = far_sum(in_keep, in_send)

    def line_sum(total):
        for axis, bit in reversed(grid.group_bits):
            size = total.shape[0] // 2
            upper = (group >> bit) & 1
            keep = lax.dynamic_slice_in_dim(total, upper * size, size, 0)
            send = lax.dynamic_slice_in_dim(total, (1 - upper) * size, size, 0)
            got = swap(grid, send.astype(bf16), ((axis, bit), (axis, bit)))
            total = keep + got.astype(f32)
        return total

    (grad_out,) = call(
        branch_grads_kernel,
        [((width, width), bf16)],
        attended,
        d_branch,
        line_near,
        name="branch_gradients",
    )
    d_pieces[0], grad_out = tie(d_pieces[0], grad_out)

    d_query, pairs_own, pairs_send = attention_backward(
        query, pairs, mask_bias, [d_pieces[0], *got_d_att], att_pieces, logs
    )
    pairs_own, in_total = tie(pairs_own, in_total)
    in_total = reduce_near(grid, in_total, grid.plane_bits[:-1])
    if parts == 2:
        pairs_got = swap(grid, pairs_send, part_bits[0])
    else:
        pairs_all = jnp.concatenate([pairs_own, pairs_send.astype(f32)])
        pairs_own = reduce_near(grid, pairs_all, part_bits)
        pairs_got = jnp.zeros(pairs_own.shape, bf16)
    last_columns = table_width - 2 * columns - width
    (last_grads,) = call(
        functools.partial(query_grads_kernel, small_each),
        [((width, last_columns), f32)],
        x_near,
        d_query,
        near_group,
        sums_one,
        sums_two,
        ffn_sums,
        to_near,
        near_unit,
        name="query_gradients",
    )
    last_grads, down_total = tie(last_grads, down_total)
    down_total = reduce_near(grid, down_total, grid.plane_bits[:-1])
    grad_keep, grad_send, back_keep, back_send = call(
        pair_grads_kernel,
        [
            ((width // 2, table_width), bf16),
            ((width // 2, table_width), bf16),
            ((line_len // 2, width), f32),
            ((line_len // 2, width), bf16),
        ],
        x_near,
        pairs_own,
        pairs_got,
        d_query,
        near_group,
        qkv_slice,
        grad_out,
        last_grads,
        name="pair_gradients",
    )
    grad_send, down_total, in_total = tie(grad_send, down_total, in_total)
    sum_down = line_sum(down_total)
    in_pairs = line_sum(in_total)
    back = back_keep + swap(grid, back_send, line_bits[1]).astype(f32)
    back = reduce_near(grid, back, line_bits[:1])
    total = grad_keep.astype(f32) + chip_swap(grad_send).astype(f32)
    total = reduce_near(grid, total, grid.plane_bits)
    total, in_pairs, d_one = tie(total, in_pairs, d_one)
    in_got = chip_swap(in_pairs[rows_each:])
    (sum_in,) = call(
        functools.partial(units_kernel, unit_ids),
        [((rows_each, ff), f32)],
        place,
        in_pairs[:rows_each],
        in_got,
        name="order_units",
    )

    got_total = line_swap(
        grid, [total[k * rows_each : (k + 1) * rows_each].astype(bf16) for k in range(1, groups)]
    )
    input_grad = d_one + back
    own_total, sum_in = tie(total[:rows_each], sum_in)
    sum_qkv, sum_out, sum_vec, sum_ffn, sum_gain, sum_shift = call(
        functools.partial(finish_kernel, small_each),
        [
            ((rows_each, 3 * width), f32),
            ((rows_each, width), f32),
            ((4, rows_each), f32),
            ((1, ff_each), f32),
            ((2, rows_each), f32),
            ((2, rows_each), f32),
        ],
        place,
        own_total,
        *got_total,
        name="finish",
    )
    return (
        output[None],
        input_grad[None],
        sum_qkv,
        sum_out,
        sum_in,
        sum_down,
        sum_vec,
        sum_ffn.reshape(ff_each),
        sum_gain,
        sum_shift,
    )


def solution(mesh):
    return jax.shard_map(
        functools.partial(on_device, Grid(mesh)),
        mesh=mesh,
        in_specs=(
            P("dp", "seq", None),
            P("dp", None),
            P("dp", None, None),
            P("dp", None, None),
            P(("dp", "seq"), None),
            P(("dp", "seq"), None),
            P(("dp", "seq"), None),
            P(("dp", "seq"), None),
            P(None, ("dp", "seq")),
            P(("dp", "seq")),
            P(None, ("dp", "seq")),
            P(None, ("dp", "seq")),
            P("dp", "seq", None),
        ),
        out_specs=(
            P("dp", "seq", None),
            P("dp", "seq", None),
            P(("dp", "seq"), None),
            P(("dp", "seq"), None),
            P(("dp", "seq"), None),
            P(("dp", "seq"), None),
            P(None, ("dp", "seq")),
            P(("dp", "seq")),
            P(None, ("dp", "seq")),
            P(None, ("dp", "seq")),
        ),
        check_vma=False,
    )
```
